32 devices in a mesh: fsdp: 4 (over y, core), ctx: 8 (over z, x).
Axes of the slice: x: 2, y: 2, z: 4, core: 2. Of those that a mesh axis runs over, the one named last changes fastest.
Arguments:
- tokens: bfloat16 [4, 4096, 576], P('fsdp', 'ctx'), may hold values from -6 to 6
- segment_ids: int32 [4, 4096], P('fsdp'), may hold values from 0 to 20, as said below
- positions: int32 [4, 4096], P('fsdp'), may hold values from 0 to 1999, as said below
- cotangent: bfloat16 [4, 4096, 576], P('fsdp', 'ctx'), may hold values from -6 to 6
- norm_first: bfloat16 [576], P('fsdp'), may hold values from 0.099609375 to 1.8984375
- query_weight: bfloat16 [576, 576], P('fsdp'), may hold values from -0.25 to 0.25
- key_weight: bfloat16 [576, 192], P('fsdp'), may hold values from -0.25 to 0.25
- value_weight: bfloat16 [576, 192], P('fsdp'), may hold values from -0.25 to 0.25
- output_weight: bfloat16 [576, 576], P('fsdp'), may hold values from -1 to 1
- norm_second: bfloat16 [576], P('fsdp'), may hold values from 0.099609375 to 1.8984375
- gate_weight: bfloat16 [576, 1536], P('fsdp'), may hold values from -0.25 to 0.25
- up_weight: bfloat16 [576, 1536], P('fsdp'), may hold values from -0.25 to 0.25
- down_weight: bfloat16 [1536, 576], P('fsdp'), may hold values from -0.15625 to 0.15625
Outputs:
- result: bfloat16 [4, 4096, 576], P('fsdp', 'ctx')
- tokens_grad: bfloat16 [4, 4096, 576], P('fsdp', 'ctx')
- first_grad: float32 [576], P('fsdp')
- query_grad: float32 [576, 576], P('fsdp')
- key_grad: float32 [576, 192], P('fsdp')
- value_grad: float32 [576, 192], P('fsdp')
- output_grad: float32 [576, 576], P('fsdp')
- second_grad: float32 [576], P('fsdp')
- gate_grad: float32 [576, 1536], P('fsdp')
- up_grad: float32 [576, 1536], P('fsdp')
- down_grad: float32 [1536, 576], P('fsdp')
The draws below stay inside these ranges and needn't reach their ends.
Inputs may be any that keep to these rules, and one draw needn't show every extreme that they name: `segment_ids`: within a sequence, listed in order of place, documents follow one another and each is 200 to 2000 tokens long (the last one may be cut by the sequence's end); ids count documents from 0 in order of place; in every draw some sequence holds only documents of 200 tokens. Row r of a sequence holds place b * 256 + r % 256 with c = r // 512 and b = c if r % (512) < 256, else 2 * 8 - 1 - c. `positions`: A token's position is its place minus the place where its document begins; some document in every draw has exactly 2000 tokens.
All inputs are finite; a program needn't handle non-finite values.
Results may differ from the reference program's by a relative error of at most 0.02.
Values may be sent and summed in bfloat16 or wider, within the bound.
No kernel may reach another device: no remote copies, remote signals or barrier semaphores. Data moves between devices by JAX's collectives and lax.ppermute only.
A program may use at most 192 MiB of HBM per device.

```python
import math
import jax
import jax.numpy as jnp
from jax import lax

D = 576
HEADS = 9
KV_HEADS = 3
HEAD_DIM = 64
FF = 1536
SEQ_LEN = 4096
DOC_LEAST = 200
DOC_MOST = 2000
SEQS = 4
BLOCK = 256


def document_layout(key):
    drawn = jax.random.fold_in(key, 11)
    length_key, pick_key = jax.random.split(drawn)
    doc_count = SEQ_LEN // DOC_LEAST + 1
    doc_lengths = jax.random.randint(length_key, (SEQS, doc_count), DOC_LEAST, DOC_MOST + 1)
    chosen = jax.random.randint(pick_key, (), 0, SEQS)
    shortest = (chosen + 1) % SEQS
    seq_index = jnp.arange(SEQS)[:, None]
    doc_index = jnp.arange(doc_count)[None, :]
    doc_lengths = jnp.where(seq_index == shortest, DOC_LEAST, doc_lengths)
    doc_lengths = jnp.where((seq_index == chosen) & (doc_index == 0), DOC_MOST, doc_lengths)
    doc_ends = jnp.cumsum(doc_lengths, axis=1)
    pair_count = SEQ_LEN // (2 * BLOCK)
    slots = jnp.arange(SEQ_LEN)
    holder = slots // (2 * BLOCK)
    within = slots % (2 * BLOCK)
    block_index = jnp.where(within < BLOCK, holder, 2 * pair_count - 1 - holder)
    place = block_index * BLOCK + within % BLOCK
    passed = doc_ends[:, :, None] <= place[None, None, :]
    segment = jnp.sum(passed.astype(jnp.int32), axis=1)
    begin = jnp.sum(jnp.where(passed, doc_lengths[:, :, None], 0), axis=1)
    return (segment.astype(jnp.int32), (place[None, :] - begin).astype(jnp.int32))


def draw_segment_ids(key, part):
    return document_layout(key)[0]


def draw_positions(key, part):
    return document_layout(key)[1]


def shard_levels(rng, shape, shards, smallest, top_value):
    level, own = 1.0, jax.random.fold_in(rng, 6)
    for dim, shards_of in shards:
        steps = jnp.exp(jax.random.uniform(jax.random.fold_in(own, dim), (shards_of,), jnp.float32, smallest / len(shards), top_value / len(shards)))
        level = level * jnp.repeat(steps, shape[dim] // shards_of).reshape([-1 if axis == dim else 1 for axis in range(len(shape))])
    return level


def centred(own_key, dims, deviation, bound, cuts=(), kind=jnp.bfloat16):
    values = deviation * jax.random.normal(own_key, dims, jnp.float32)
    if cuts:
        values = values * shard_levels(own_key, dims, cuts, -0.22, 0.18)
    return jnp.clip(values, -bound, bound).astype(kind)


def setup_inputs(seed: int = 0) -> dict:
    key_of = jax.random.split(jax.random.key(seed), 14)
    tokens = centred(key_of[0], (SEQS, SEQ_LEN, D), 1.0, 6.0, ((0, 4), (1, 8)))
    segment_ids = draw_segment_ids(jax.random.fold_in(key_of[13], 71), 0)
    positions = draw_positions(jax.random.fold_in(key_of[13], 71), 0)
    cotangent = centred(key_of[3], (SEQS, SEQ_LEN, D), 1.0, 6.0, ((0, 4), (1, 8)))
    norm_first = jnp.clip(1.0 + 0.18 * jax.random.normal(key_of[4], (D,), jnp.float32), 0.099609375, 1.8984375).astype(jnp.bfloat16)
    query_weight = centred(key_of[5], (D, HEADS * HEAD_DIM), D ** -0.5, 0.25, ((0, 4),))
    key_weight = centred(key_of[6], (D, KV_HEADS * HEAD_DIM), D ** -0.5, 0.25, ((0, 4),))
    value_weight = centred(key_of[7], (D, KV_HEADS * HEAD_DIM), D ** -0.5, 0.25, ((0, 4),))
    output_weight = centred(key_of[8], (HEADS * HEAD_DIM, D), (D // 16) ** -0.5, 1.0, ((0, 4),))
    norm_second = jnp.clip(1.0 + 0.18 * jax.random.normal(key_of[9], (D,), jnp.float32), 0.099609375, 1.8984375).astype(jnp.bfloat16)
    gate_weight = centred(key_of[10], (D, FF), D ** -0.5, 0.25, ((0, 4),))
    up_weight = centred(key_of[11], (D, FF), D ** -0.5, 0.25, ((0, 4),))
    down_weight = centred(key_of[12], (FF, D), FF ** -0.5, 0.15625, ((0, 4),))
    return dict(tokens=tokens, segment_ids=segment_ids, positions=positions, cotangent=cotangent, norm_first=norm_first, query_weight=query_weight, key_weight=key_weight, value_weight=value_weight, output_weight=output_weight, norm_second=norm_second, gate_weight=gate_weight, up_weight=up_weight, down_weight=down_weight)


EPSILON = 1e-05
MASKED = -1e+30

@jax.custom_vjp
def low(v):
    return lax.optimization_barrier(v.astype(jnp.bfloat16)).astype(jnp.float32)

@jax.custom_vjp
def low_back(v):
    return v

def low_keep(v):
    return (low(v), None)

def low_pass(kept, grad):
    return (grad,)

def back_keep(v):
    return (v, None)

def back_low(kept, grad):
    return (low(grad),)
low.defvjp(low_keep, low_pass)
low_back.defvjp(back_keep, back_low)

def rms_gain(values, gain):
    return values * lax.rsqrt(lax.optimization_barrier(jnp.mean(values * values, axis=-1, keepdims=True)) + EPSILON) * gain

def angles(positions, head_width):
    frequency = jnp.exp(jnp.arange(head_width // 2, dtype=jnp.float32) * (-math.log(10000.0) * 2.0 / head_width))
    phase_angle = positions.astype(jnp.float32)[:, None] * frequency[None, :]
    phase_angle = jnp.concatenate([phase_angle, phase_angle], axis=-1)
    return (jnp.cos(phase_angle)[:, None, :], jnp.sin(phase_angle)[:, None, :])

def rotate(values, cos_table, sin_table):
    half_width = values.shape[-1] // 2
    turned = jnp.concatenate([-values[..., half_width:], values[..., :half_width]], axis=-1)
    return values * cos_table + turned * sin_table

def matmul(left, right):
    return jnp.dot(left, right, precision=lax.Precision.HIGHEST)

def layer_forward(tokens, segments, places, first_gain, query_weight, key_weight, value_weight, output_weight, second_gain, gate_weight, up_weight, down_weight):
    length = tokens.shape[1]
    group = HEADS // KV_HEADS
    scale = HEAD_DIM ** (-0.5)
    block_rows = min(512, length)
    blocks = length // block_rows

    def one_sequence(carried, pieces):
        seq_tokens, seq_segments, seq_positions = pieces
        normed = low(rms_gain(seq_tokens, first_gain))
        cos_table, sin_table = angles(seq_positions, HEAD_DIM)
        queries = low(rotate(low_back(matmul(normed, query_weight)).reshape(length, KV_HEADS, group, HEAD_DIM), cos_table[:, None], sin_table[:, None]))
        keys = low(rotate(low_back(matmul(normed, key_weight)).reshape(length, KV_HEADS, HEAD_DIM), cos_table, sin_table))
        values = low(low_back(matmul(normed, value_weight))).reshape(length, KV_HEADS, HEAD_DIM)

        def query_block(part):
            block_queries, block_segments, block_positions = part
            scores = low_back(jnp.einsum('qcgd,kcd->qcgk', block_queries, keys, precision=lax.Precision.HIGHEST))
            visible = (block_segments[:, None] == seq_segments[None, :]) & (seq_positions[None, :] <= block_positions[:, None])
            scores = jnp.where(visible[:, None, None, :], scores * scale, MASKED)
            soft_weights = low(jax.nn.softmax(scores, axis=-1))
            return jnp.einsum('qcgk,kcd->qcgd', soft_weights, values, precision=lax.Precision.HIGHEST)
        attended = lax.map(jax.checkpoint(query_block), (queries.reshape(blocks, block_rows, KV_HEADS, group, HEAD_DIM), seq_segments.reshape(blocks, block_rows), seq_positions.reshape(blocks, block_rows)))
        attended = low(low_back(attended.reshape(length, HEADS * HEAD_DIM)))
        middle = seq_tokens + low_back(matmul(attended, output_weight))
        normed_mid = low(rms_gain(middle, second_gain))
        gate_pre = low_back(matmul(normed_mid, gate_weight))
        up_pre = low_back(matmul(normed_mid, up_weight))
        hidden = low(jax.nn.silu(gate_pre) * up_pre)
        return (carried, middle + low_back(matmul(hidden, down_weight)))
    _, result = lax.scan(jax.checkpoint(one_sequence), None, (tokens, segments, places))
    return result

def reference(tokens, segment_ids, positions, cotangent, norm_first, query_weight, key_weight, value_weight, output_weight, norm_second, gate_weight, up_weight, down_weight):
    floats = tuple((argument.astype(jnp.float32) for argument in (tokens, norm_first, query_weight, key_weight, value_weight, output_weight, norm_second, gate_weight, up_weight, down_weight)))

    def closed(*arrays):
        return layer_forward(arrays[0], segment_ids, positions, *arrays[1:])
    result, pullback = jax.vjp(closed, *floats)
    grads = pullback(cotangent.astype(jnp.float32))
    return (result.astype(jnp.bfloat16), grads[0].astype(jnp.bfloat16), grads[1], grads[2], grads[3], grads[4], grads[5], grads[6], grads[7], grads[8], grads[9])
```

```python
import functools
import math

import jax
import jax.numpy as jnp
from jax import lax
from jax.experimental import pallas as pl
from jax.experimental.pallas import tpu as pltpu
from jax.sharding import PartitionSpec as P

HEADS = 9
KV_HEADS = 3
GROUP = HEADS // KV_HEADS
HEAD_DIM = 64
EPSILON = 1e-05
MASKED = -1e30
AXES = ("fsdp", "ctx")
F32 = jnp.float32
BF16 = jnp.bfloat16


def rms_gain(values, gain):
    return values * lax.rsqrt(jnp.mean(values * values, axis=-1, keepdims=True) + EPSILON) * gain


def swiglu(gate_pre, up_pre):
    return jax.nn.silu(gate_pre) * up_pre


def outer_product(left, right):
    return lax.dot_general(left, right, (((0,), (0,)), ((), ())), preferred_element_type=F32)


def inner_product(left, right):
    return lax.dot_general(left, right, (((1,), (1,)), ((), ())), preferred_element_type=F32)


def moves(fsdp, ctx, step):
    pairs = []
    for f in range(fsdp):
        for c in range(ctx):
            to = step(f // 2, f % 2, c // 2, c % 2)
            if to is not None:
                y, core, h, x = to
                pairs.append((f * ctx + c, (2 * y + core) * ctx + 2 * h + x))
    return pairs


def make_send(fsdp, ctx):
    ys, hs = fsdp // 2, ctx // 2

    def along(step):
        pairs = moves(fsdp, ctx, step)
        return lambda a: lax.ppermute(a, AXES, pairs)

    return dict(
        turn=along(lambda y, k, h, x: (y, x, h, k)),
        core=along(lambda y, k, h, x: (y, 1 - k, h, x)),
        up=along(lambda y, k, h, x: (y, k, h + 1, x) if h + 1 < hs else None),
        down=along(lambda y, k, h, x: (y, k, h - 1, x) if h > 0 else None),
        shift=[along(lambda y, k, h, x, s=s: ((y + s) % ys, k, h, x)) for s in range(ys)],
    )


def bias_of(begin, place, block_id, keys, rows):
    key_place = block_id * keys + lax.broadcasted_iota(jnp.int32, (keys, rows), 0)
    seen = (key_place >= begin) & (key_place <= place)
    return jnp.where(seen, 0.0, MASKED)


def dot(left, right, left_dim, right_dim):
    return lax.dot_general(
        left, right, (((left_dim,), (right_dim,)), ((), ())), preferred_element_type=F32
    )


def load_blocks(pieces, held):
    at = 0
    for piece in pieces:
        if len(piece.shape) == 3:
            held[at] = piece[...]
            at += 1
        else:
            for part in range(piece.shape[0]):
                held[at] = piece[part]
                at += 1


def each_pair(sc, blocks, work):
    def step(i, _):
        q = lax.div(i, blocks)
        k = lax.rem(i, blocks)
        block_id = sc[4 + k]

        @pl.when((block_id >= sc[2 + q]) & (block_id <= sc[q]))
        def _():
            work(q, k, block_id)

        return 0

    lax.fori_loop(0, 2 * blocks, step, 0)


def forward_kernel(pieces, blocks, first, last, *refs):
    refs = list(refs)
    sc, pos, qz = refs[:3]
    kv = refs[3 : 3 + pieces]
    refs = refs[3 + pieces :]
    if not first:
        peak_in, total_in, mix_in = refs[:3]
        refs = refs[3:]
    if last:
        out, lse = refs[:2]
        held, bias, peak, total, mix = refs[2:]
    else:
        peak, total, mix = refs[:3]
        held, bias = refs[3:]
    rows = qz.shape[-1]
    if first:
        peak[...] = jnp.full(peak.shape, MASKED, F32)
        total[...] = jnp.zeros(total.shape, F32)
        mix[...] = jnp.zeros(mix.shape, F32)
    else:
        peak[...] = peak_in[...]
        total[...] = total_in[...]
        mix[...] = mix_in[...]
    load_blocks(kv, held)

    def work(q, k, block_id):
        place = sc[q] * rows + lax.broadcasted_iota(jnp.int32, (1, rows), 1)
        bias[...] = bias_of(place - pos[q], place, block_id, rows, rows)
        for c in range(KV_HEADS):
            block = held[k, c]
            values = block.T[HEAD_DIM:]
            for g in range(GROUP):
                h = c * GROUP + g
                scores = dot(block, qz[q, h], 1, 0) + bias[...]
                old = peak[q, h : h + 1]
                new = jnp.maximum(old, jnp.max(scores, axis=0, keepdims=True))
                expo = jnp.exp(scores - new)
                fade = jnp.exp(old - new)
                peak[q, h : h + 1] = new
                total[q, h : h + 1] = total[q, h : h + 1] * fade + jnp.sum(
                    expo, axis=0, keepdims=True
                )
                mix[q, h] = mix[q, h] * fade + dot(values, expo.astype(BF16), 1, 0)

    each_pair(sc, blocks, work)
    if last:
        for q in range(2):
            lse[q] = peak[q] + jnp.log(total[q])
            for h in range(HEADS):
                out[q, h] = (mix[q, h] / total[q, h : h + 1]).astype(BF16)


def backward_kernel(pieces, blocks, first, own_type, *refs):
    refs = list(refs)
    sc, pos, qz, gz, lse, delta = refs[:6]
    kv = refs[6 : 6 + pieces]
    refs = refs[6 + pieces :]
    if not first:
        dq_in = refs[0]
        refs = refs[1:]
    dq, own, other, held, bias, dkv = refs
    rows = qz.shape[-1]
    if first:
        dq[...] = jnp.zeros(dq.shape, F32)
    else:
        dq[...] = dq_in[...]
    load_blocks(kv, held)
    dkv[...] = jnp.zeros(dkv.shape, F32)

    def work(q, k, block_id):
        place = sc[q] * rows + lax.broadcasted_iota(jnp.int32, (1, rows), 1)
        bias[...] = bias_of(place - pos[q], place, block_id, rows, rows)
        for c in range(KV_HEADS):
            block = held[k, c]
            keys = block.T[:HEAD_DIM]
            for g in range(GROUP):
                h = c * GROUP + g
                scores = dot(block, qz[q, h], 1, 0) + bias[...]
                probs = jnp.exp(scores - lse[q, h : h + 1])
                d_probs = dot(block, gz[q, h], 1, 0)
                d_scores = (probs * (d_probs - delta[q, h : h + 1])).astype(BF16)
                dkv[k, c] += dot(d_scores, qz[q, h], 1, 1) + dot(
                    probs.astype(BF16), gz[q, h], 1, 1
                )
                dq[q, h] += dot(keys, d_scores, 1, 0)

    each_pair(sc, blocks, work)
    half = blocks // 2
    own[...] = dkv[:half].astype(own_type)
    other[...] = dkv[half:].astype(BF16)


VM = pl.BlockSpec(memory_space=pltpu.VMEM)
SM = pl.BlockSpec(memory_space=pltpu.SMEM)
LIMIT = pltpu.CompilerParams(vmem_limit_bytes=48 * 1024 * 1024)


def count_blocks(pieces):
    return sum(1 if p.ndim == 3 else p.shape[0] for p in pieces)


def attend_forward(sc, pos, qz, pieces, carried, last):
    rows = qz.shape[-1]
    blocks = count_blocks(pieces)
    first = carried is None
    stat = jax.ShapeDtypeStruct((2, HEADS, rows), F32)
    mix = jax.ShapeDtypeStruct((2, HEADS, HEAD_DIM, rows), F32)
    scratch = [
        pltpu.VMEM((blocks, KV_HEADS, rows, 2 * HEAD_DIM), BF16),
        pltpu.VMEM((rows, rows), F32),
    ]
    if last:
        out_shape = (jax.ShapeDtypeStruct(mix.shape, BF16), stat)
        scratch += [pltpu.VMEM(s.shape, F32) for s in (stat, stat, mix)]
        aliases = {}
    else:
        out_shape = (stat, stat, mix)
        aliases = {} if first else {3 + len(pieces) + i: i for i in range(3)}
    given = (sc, pos, qz, *pieces) + (() if first else tuple(carried))
    pairs = blocks * HEADS * rows * rows
    return pl.pallas_call(
        functools.partial(forward_kernel, len(pieces), blocks, first, last),
        out_shape=out_shape,
        in_specs=[SM] + [VM] * (len(given) - 1),
        out_specs=[VM] * len(out_shape),
        scratch_shapes=scratch,
        input_output_aliases=aliases,
        compiler_params=LIMIT,
        cost_estimate=pl.CostEstimate(
            flops=pairs * 512, bytes_accessed=6 << 20, transcendentals=pairs
        ),
    )(*given)


def attend_backward(sc, pos, qz, gz, lse, delta, pieces, dq, own_type):
    rows = qz.shape[-1]
    blocks = count_blocks(pieces)
    first = dq is None
    wide = (KV_HEADS, rows, 2 * HEAD_DIM)
    given = (sc, pos, qz, gz, lse, delta, *pieces) + (() if first else (dq,))
    pairs = blocks * HEADS * rows * rows
    return pl.pallas_call(
        functools.partial(backward_kernel, len(pieces), blocks, first, own_type),
        out_shape=(
            jax.ShapeDtypeStruct((2, HEADS, HEAD_DIM, rows), F32),
            jax.ShapeDtypeStruct((blocks // 2,) + wide, own_type),
            jax.ShapeDtypeStruct((blocks // 2,) + wide, BF16),
        ),
        in_specs=[SM] + [VM] * (len(given) - 1),
        out_specs=[VM] * 3,
        scratch_shapes=[
            pltpu.VMEM((blocks,) + wide, BF16),
            pltpu.VMEM((rows, rows), F32),
            pltpu.VMEM((blocks,) + wide, F32),
        ],
        input_output_aliases={} if first else {len(given) - 1: 0},
        compiler_params=LIMIT,
        cost_estimate=pl.CostEstimate(
            flops=pairs * 1280, bytes_accessed=10 << 20, transcendentals=pairs
        ),
    )(*given)


def slabs(grad, shards):
    rows = grad.shape[0] // shards
    wide = -(-grad.shape[1] // 128)
    grad = jnp.pad(grad, ((0, 0), (0, wide * 128 - grad.shape[1])))
    return (
        grad.reshape(shards, rows, wide, 128).transpose(0, 2, 1, 3).reshape(shards, wide * rows, 128)
    )


def unslab(flat, at, rows, columns):
    wide = -(-columns // 128)
    part = flat[at : at + wide * rows].reshape(wide, rows, 128)
    part = part.transpose(1, 0, 2).reshape(rows, wide * 128)[:, :columns]
    return part.astype(F32), at + wide * rows


def reduce_grads(grads, send, fsdp, ctx, core, y):
    ys = fsdp // 2
    packed = jnp.concatenate([slabs(g.astype(BF16), fsdp) for g in grads], axis=1)
    rows = packed.shape[1]
    full = -(-rows // (16 * ctx)) * 16 * ctx
    packed = jnp.pad(packed, ((0, 0), (0, full - rows), (0, 0))).reshape(ys, 2, full, 128)
    mine = lax.dynamic_index_in_dim(packed, core, 1, False)
    give = lax.dynamic_index_in_dim(packed, 1 - core, 1, False)
    chip = (mine.astype(F32) + send["core"](give).astype(F32)).astype(BF16)
    total = lax.dynamic_index_in_dim(chip, y, 0, False).astype(F32)
    for s in range(1, ys):
        part = lax.dynamic_index_in_dim(chip, lax.rem(y + s, ys), 0, False)
        total = total + send["shift"][s](part).astype(F32)
    parts = total.astype(BF16).reshape(ctx, full // ctx, 128)
    got = lax.all_to_all(parts, "ctx", 0, 0, tiled=True)
    summed = jnp.sum(got.astype(F32), axis=0, keepdims=True).astype(BF16)
    spread = jnp.broadcast_to(summed, parts.shape)
    return lax.all_to_all(spread, "ctx", 0, 0, tiled=True).reshape(full, 128)


def gather_rows(own, send, fsdp, core, y):
    ys = fsdp // 2
    buffer = jnp.zeros((ys, 2) + own.shape, own.dtype)
    for s in range(ys):
        got = own if s == 0 else send["shift"][s](own)
        twin = send["core"](got)
        source = lax.rem(y - s + ys, ys)
        buffer = lax.dynamic_update_slice(buffer, got[None, None], (source, core, 0, 0))
        buffer = lax.dynamic_update_slice(buffer, twin[None, None], (source, 1 - core, 0, 0))
    return buffer.reshape((fsdp * own.shape[0],) + own.shape[1:])


def body(
    fsdp,
    ctx,
    tokens,
    segment_ids,
    positions,
    cotangent,
    norm_first,
    query_weight,
    key_weight,
    value_weight,
    output_weight,
    norm_second,
    gate_weight,
    up_weight,
    down_weight,
):
    send = make_send(fsdp, ctx)
    hs = ctx // 2
    _, count, width = tokens.shape
    rows = count // 2
    kv_width = KV_HEADS * HEAD_DIM
    fi, ci = lax.axis_index("fsdp"), lax.axis_index("ctx")
    y, core = lax.div(fi, 2), lax.rem(fi, 2)
    h = lax.div(ci, 2)
    packed = jnp.concatenate(
        [query_weight, key_weight, value_weight, norm_first[:, None], norm_second[:, None]], axis=1
    )
    first_full = gather_rows(packed, send, fsdp, core, y)
    output_full = lax.all_gather(output_weight, "fsdp", axis=0, tiled=True)
    gate_full = lax.all_gather(gate_weight, "fsdp", axis=0, tiled=True)
    up_full = lax.all_gather(up_weight, "fsdp", axis=0, tiled=True)
    down_full = lax.all_gather(down_weight, "fsdp", axis=0, tiled=True)
    query_full = first_full[:, :width]
    key_full = first_full[:, width : width + kv_width]
    value_full = first_full[:, width + kv_width : width + 2 * kv_width]
    first_gain = first_full[:, width + 2 * kv_width].astype(F32)
    second_gain = first_full[:, width + 2 * kv_width + 1].astype(F32)
    own_pos = lax.dynamic_slice_in_dim(positions, ci * count, count, 1).reshape(count)
    own_pos = send["turn"](own_pos)
    x_low = send["turn"](tokens.reshape(count, width))
    grad_low = send["turn"](cotangent.reshape(count, width))
    place_c = 2 * h + core
    blocks_total = 2 * ctx
    low_id, high_id = place_c, blocks_total - 1 - place_c
    pos2 = own_pos.reshape(2, 1, rows)
    begins = jnp.stack([low_id, high_id]) * rows - pos2[:, 0, 0]
    query_ids = [low_id, high_id, lax.div(begins[0], rows), lax.div(begins[1], rows)]

    def scalars(ids):
        return jnp.stack(query_ids + ids).astype(jnp.int32)

    frequency = jnp.exp(
        jnp.arange(HEAD_DIM // 2, dtype=F32) * (-math.log(10000.0) * 2.0 / HEAD_DIM)
    )
    angle = frequency[:, None] * own_pos.astype(F32)[None, :]
    cos, sin = jnp.cos(angle), jnp.sin(angle)
    cos_t, sin_t = cos.T[:, None, :], sin.T[:, None, :]

    flat = x_low.astype(F32)
    first_normed = rms_gain(flat, first_gain).astype(BF16)
    query_pre = lax.dot_general(
        query_full, first_normed, (((0,), (1,)), ((), ())), preferred_element_type=F32
    ).reshape(HEADS, 2, HEAD_DIM // 2, count)
    qa, qb = query_pre[:, 0], query_pre[:, 1]
    queries = jnp.concatenate([qa * cos - qb * sin, qb * cos + qa * sin], axis=1).astype(BF16)
    queries = queries * jnp.asarray(HEAD_DIM**-0.5, BF16)
    queries = queries.reshape(HEADS, HEAD_DIM, 2, rows).transpose(2, 0, 1, 3)
    qz = jnp.concatenate([queries, jnp.zeros_like(queries)], axis=2)
    key_pre = jnp.dot(first_normed, key_full, preferred_element_type=F32)
    key_pre = key_pre.reshape(count, KV_HEADS, 2, HEAD_DIM // 2)
    ka, kb = key_pre[:, :, 0], key_pre[:, :, 1]
    keys = jnp.concatenate([ka * cos_t - kb * sin_t, kb * cos_t + ka * sin_t], axis=2)
    values = jnp.dot(first_normed, value_full, preferred_element_type=F32)
    kv = jnp.concatenate(
        [keys.astype(BF16), values.astype(BF16).reshape(count, KV_HEADS, HEAD_DIM)], axis=2
    )
    kv = kv.reshape(2, rows, KV_HEADS, 2 * HEAD_DIM).transpose(0, 2, 1, 3)

    stages = []
    twin_c = 2 * h + 1 - core
    stages.append(
        ((kv, send["core"](kv)), [low_id, high_id, twin_c, blocks_total - 1 - twin_c])
    )
    go_up, go_down = kv[0], kv
    for s in range(1, hs):
        go_up, go_down = send["up"](go_up), send["down"](go_down)
        ids = []
        for k in (core, 1 - core):
            from_up, from_down = 2 * (h - s) + k, 2 * (h + s) + k
            ids += [
                jnp.where(h >= s, from_up, -1),
                jnp.where(h + s < hs, from_down, -1),
                jnp.where(h + s < hs, blocks_total - 1 - from_down, -1),
            ]
        stages.append(((go_up, go_down, send["core"](go_up), send["core"](go_down)), ids))
    carried = None
    for s, (pieces, ids) in enumerate(stages):
        carried = attend_forward(scalars(ids), pos2, qz, pieces, carried, s == hs - 1)
    mixed, lse = carried
    attended = mixed.transpose(0, 3, 1, 2).reshape(count, width)

    middle = flat + jnp.dot(attended, output_full, preferred_element_type=F32)
    second_normed = rms_gain(middle, second_gain).astype(BF16)
    gate_pre = jnp.dot(second_normed, gate_full, preferred_element_type=F32)
    up_pre = jnp.dot(second_normed, up_full, preferred_element_type=F32)
    hidden = swiglu(gate_pre, up_pre).astype(BF16)
    result = (middle + jnp.dot(hidden, down_full, preferred_element_type=F32)).astype(BF16)
    result = send["turn"](result)
    down_local = outer_product(hidden, grad_low)
    d_hidden = inner_product(grad_low, down_full)
    _, swiglu_back = jax.vjp(swiglu, gate_pre, up_pre)
    d_gate, d_up = swiglu_back(d_hidden)
    d_gate, d_up = d_gate.astype(BF16), d_up.astype(BF16)
    gate_local = outer_product(second_normed, d_gate)
    up_local = outer_product(second_normed, d_up)
    d_second = inner_product(d_gate, gate_full) + inner_product(d_up, up_full)
    _, second_back = jax.vjp(rms_gain, middle, second_gain)
    d_middle, second_local = second_back(d_second)
    d_middle = d_middle + grad_low.astype(F32)
    d_branch = d_middle.astype(BF16)
    output_local = outer_product(attended, d_branch)
    d_mixed = lax.dot_general(
        output_full, d_branch, (((1,), (1,)), ((), ())), preferred_element_type=F32
    ).astype(BF16)
    d_mixed = d_mixed.reshape(HEADS, HEAD_DIM, 2, rows).transpose(2, 0, 1, 3)
    gz = jnp.concatenate([jnp.zeros_like(d_mixed), d_mixed], axis=2)
    delta = jnp.sum(d_mixed.astype(F32) * mixed.astype(F32), axis=2)
    late = reduce_grads(
        [gate_local, up_local, output_local, down_local], send, fsdp, ctx, core, y
    )

    dq = None
    came_up = came_down = None
    for s in range(hs - 1, 0, -1):
        pieces, ids = stages[s]
        dq, own, other = attend_backward(
            scalars(ids), pos2, qz, gz, lse, delta, pieces, dq, BF16
        )
        total = own.astype(F32) + send["core"](other).astype(F32)
        to_down, to_up = total[0], total[1:]
        if came_up is not None:
            to_down = to_down + came_down.astype(F32)
            to_up = to_up + came_up.astype(F32)
        came_down = send["down"](to_down.astype(BF16))
        came_up = send["up"](to_up.astype(BF16))
    pieces, ids = stages[0]
    dq, own, other = attend_backward(scalars(ids), pos2, qz, gz, lse, delta, pieces, dq, F32)
    dkv = own + send["core"](other).astype(F32)
    if came_up is not None:
        dkv = dkv + came_up.astype(F32)
        dkv = dkv + jnp.stack([came_down, jnp.zeros_like(came_down)]).astype(F32)

    dq = (dq * HEAD_DIM**-0.5).transpose(1, 2, 0, 3).reshape(HEADS, 2, HEAD_DIM // 2, count)
    da, db = dq[:, 0], dq[:, 1]
    d_query_pre = jnp.concatenate([da * cos + db * sin, db * cos - da * sin], axis=1)
    d_query_pre = d_query_pre.astype(BF16).reshape(width, count)
    dkv = dkv.transpose(0, 2, 1, 3).reshape(count, KV_HEADS, 2 * HEAD_DIM)
    da, db = dkv[..., : HEAD_DIM // 2], dkv[..., HEAD_DIM // 2 : HEAD_DIM]
    d_key_pre = jnp.concatenate([da * cos_t + db * sin_t, db * cos_t - da * sin_t], axis=2)
    d_key_pre = d_key_pre.astype(BF16).reshape(count, kv_width)
    d_value_pre = dkv[..., HEAD_DIM:].astype(BF16).reshape(count, kv_width)
    query_local = lax.dot_general(
        first_normed, d_query_pre, (((0,), (1,)), ((), ())), preferred_element_type=F32
    )
    key_local = outer_product(first_normed, d_key_pre)
    value_local = outer_product(first_normed, d_value_pre)
    d_first = (
        lax.dot_general(
            d_query_pre, query_full, (((0,), (1,)), ((), ())), preferred_element_type=F32
        )
        + inner_product(d_key_pre, key_full)
        + inner_product(d_value_pre, value_full)
    )
    _, first_back = jax.vjp(rms_gain, flat, first_gain)
    d_tokens, first_local = first_back(d_first)
    tokens_grad = send["turn"]((d_tokens + d_middle).astype(BF16))
    front = jnp.concatenate(
        [query_local, key_local, value_local, first_local[:, None], second_local[:, None]], axis=1
    )
    front = reduce_grads([front], send, fsdp, ctx, core, y)

    shard = gate_weight.shape[0]
    columns = gate_weight.shape[1]
    gate_grad, at = unslab(late, 0, shard, columns)
    up_grad, at = unslab(late, at, shard, columns)
    output_grad, at = unslab(late, at, shard, width)
    down_grad, at = unslab(late, at, down_weight.shape[0], width)
    front, _ = unslab(front, 0, shard, front_width(width, kv_width))
    return (
        result[None],
        tokens_grad[None],
        front[:, width + 2 * kv_width],
        front[:, :width],
        front[:, width : width + kv_width],
        front[:, width + kv_width : width + 2 * kv_width],
        output_grad,
        front[:, width + 2 * kv_width + 1],
        gate_grad,
        up_grad,
        down_grad,
    )


def front_width(width, kv_width):
    return width + 2 * kv_width + 2


def solution(mesh):
    flat, split = P("fsdp"), P("fsdp", None)
    whole = P("fsdp", "ctx", None)
    return jax.shard_map(
        functools.partial(body, mesh.shape["fsdp"], mesh.shape["ctx"]),
        mesh=mesh,
        in_specs=(whole, split, split, whole, flat, split, split, split, split, flat, split, split, split),
        out_specs=(whole, whole, flat, split, split, split, split, flat, split, split, split),
        check_vma=False,
    )
```

```python
import functools
import math

import jax
import jax.numpy as jnp
from jax import lax
from jax.experimental import pallas as pl
from jax.experimental.pallas import tpu as pltpu
from jax.sharding import Mesh
from jax.sharding import PartitionSpec as P

HEADS = 9
KV_HEADS = 3
GROUP = HEADS // KV_HEADS
HEAD_DIM = 64
EPSILON = 1e-05
MASKED = -1e30
DOC_MOST = 2000
AXES = ("y", "core", "h", "x")
CTX = ("h", "x")
F32 = jnp.float32
BF16 = jnp.bfloat16


def moves(fsdp, ctx, step):
    pairs = []
    for f in range(fsdp):
        for c in range(ctx):
            to = step(f // 2, f % 2, c // 2, c % 2)
            if to is not None:
                y, core, h, x = to
                pairs.append((f * ctx + c, (2 * y + core) * ctx + 2 * h + x))
    return pairs


def make_send(fsdp, ctx):
    ys, hs, blocks = fsdp // 2, ctx // 2, 2 * ctx

    def along(pairs):
        return lambda a: lax.ppermute(a, AXES, pairs)

    def by(step):
        return along(moves(fsdp, ctx, step))

    def home(slot):
        def step(y, core, h, x):
            low = 2 * h + x
            block = low if h % 2 == slot else blocks - 1 - low
            return (y, int(block % 4 in (1, 2)), block // 4, core)

        return moves(fsdp, ctx, step)

    def back(pairs):
        return along([(b, a) for a, b in pairs])

    return dict(
        home=[along(home(0)), along(home(1))],
        back=[back(home(0)), back(home(1))],
        core=by(lambda y, k, h, x: (y, 1 - k, h, x)),
        across=by(lambda y, k, h, x: (y, k, h, 1 - x)),
        up=by(lambda y, k, h, x: (y, k, h + 1, x) if h + 1 < hs else None),
        down=by(lambda y, k, h, x: (y, k, h - 1, x) if h > 0 else None),
        shift=[by(lambda y, k, h, x, s=s: ((y + s) % ys, k, h, x)) for s in range(ys)],
    )


def pick_home(a, h):
    r = a.shape[1] // 2
    low, high = a[:, :r], a[:, r:]
    even = lax.rem(h, 2) == 0
    return jnp.where(even, low, high), jnp.where(even, high, low)


def send_home(send, pair):
    return send["home"][0](pair[0]), send["home"][1](pair[1])


def send_back(send, a, b):
    return send["back"][0](a), send["back"][1](b)


def low_high(a, b, h):
    even = lax.rem(h, 2) == 0
    return jnp.concatenate([jnp.where(even, a, b), jnp.where(even, b, a)], axis=1)


def tie(*values):
    return lax.optimization_barrier(values)


def bias_of(begin, place, block_id, keys, rows):
    key_place = block_id * keys + lax.broadcasted_iota(jnp.int32, (keys, rows), 0)
    seen = (key_place >= begin) & (key_place <= place)
    return jnp.where(seen, 0.0, MASKED)


def dot(left, right, left_dim, right_dim):
    return lax.dot_general(
        left, right, (((left_dim,), (right_dim,)), ((), ())), preferred_element_type=F32
    )


def load_blocks(pieces, held):
    held[:2] = pieces[0][...]
    held[2:] = pieces[1][...]


def each_pair(sc, stage, work):
    base, core = sc[4] - 4 * stage, sc[5]

    def step(i, _):
        q = lax.div(i, 4)
        k = lax.rem(i, 4)
        within = jnp.where(k < 2, core, 1 - core)
        block_id = base + jnp.where(lax.rem(k, 2) == 0, within, 3 - within)

        @pl.when((block_id >= sc[2 + q]) & (block_id <= sc[q]))
        def _():
            work(q, k, block_id)

        return 0

    lax.fori_loop(0, 8, step, 0)


def forward_kernel(stage, last, *refs):
    first = stage == 0
    refs = list(refs)
    sc, pos, qz = refs[:3]
    kv = refs[3:5]
    refs = refs[5:]
    if not first:
        peak_in, total_in, mix_in = refs[:3]
        refs = refs[3:]
    if last:
        out, lse = refs[:2]
        held, bias, peak, total, mix = refs[2:]
    else:
        peak, total, mix = refs[:3]
        held, bias = refs[3:]
    rows = pos.shape[-1]
    if first:
        peak[...] = jnp.full(peak.shape, MASKED, F32)
        total[...] = jnp.zeros(total.shape, F32)
        mix[...] = jnp.zeros(mix.shape, F32)
    else:
        peak[...] = peak_in[...]
        total[...] = total_in[...]
        mix[...] = mix_in[...]
    load_blocks(kv, held)

    def work(q, k, block_id):
        place = sc[q] * rows + lax.broadcasted_iota(jnp.int32, (1, rows), 1)
        bias[...] = bias_of(place - pos[q], place, block_id, rows, rows)
        for c in range(KV_HEADS):
            seen = dot(held[k, c], qz[q, c], 1, 0) + jnp.concatenate([bias[...]] * GROUP, axis=1)
            old = peak[q, c]
            new = jnp.maximum(old, jnp.max(seen, axis=0, keepdims=True))
            expo = jnp.exp(seen - new)
            fade = jnp.exp(old - new)
            peak[q, c] = new
            total[q, c] = total[q, c] * fade + jnp.sum(expo, axis=0, keepdims=True)
            values = held[k, c].T[HEAD_DIM:]
            mix[q, c] = mix[q, c] * fade + dot(values, expo.astype(BF16), 1, 0)

    each_pair(sc, stage, work)
    if last:
        lse[...] = peak[...] + jnp.log(total[...])
        for q in range(2):
            for c in range(KV_HEADS):
                out[q, c] = (mix[q, c] / total[q, c]).astype(BF16)


def backward_kernel(stage, first, own_type, *refs):
    refs = list(refs)
    sc, pos, qz, gz, lse, delta = refs[:6]
    kv = refs[6:8]
    refs = refs[8:]
    if not first:
        dq_in = refs[0]
        refs = refs[1:]
    dq, own, other_a, other_b, held, bias, dkv = refs
    rows = pos.shape[-1]
    if first:
        dq[...] = jnp.zeros(dq.shape, F32)
    else:
        dq[...] = dq_in[...]
    load_blocks(kv, held)
    dkv[...] = jnp.zeros(dkv.shape, F32)

    def work(q, k, block_id):
        place = sc[q] * rows + lax.broadcasted_iota(jnp.int32, (1, rows), 1)
        bias[...] = bias_of(place - pos[q], place, block_id, rows, rows)
        scores = [dot(held[k, c], qz[q, c], 1, 0) for c in range(KV_HEADS)]
        for c in range(KV_HEADS):
            seen = scores[c] + jnp.concatenate([bias[...]] * GROUP, axis=1)
            probs = jnp.exp(seen - lse[q, c])
            d_scores = (probs * (dot(held[k, c], gz[q, c], 1, 0) - delta[q, c])).astype(BF16)
            dkv[k, c] += dot(d_scores, qz[q, c], 1, 1) + dot(probs.astype(BF16), gz[q, c], 1, 1)
            dq[q, c] += dot(held[k, c].T[:HEAD_DIM], d_scores, 1, 0)

    each_pair(sc, stage, work)
    own[...] = dkv[:2].astype(own_type)
    other_a[...] = dkv[2].astype(BF16)
    other_b[...] = dkv[3].astype(BF16)


SM = pl.BlockSpec(memory_space=pltpu.SMEM)
HB = pl.BlockSpec(memory_space=pl.ANY)


def whole(a):
    return pl.BlockSpec(
        a.shape, lambda i: (0,) * len(a.shape), pipeline_mode=pl.Buffered(buffer_count=1)
    )


def wholes(*arrays):
    return [whole(a) for a in arrays]


FREE = pl.CostEstimate(flops=0, bytes_accessed=0, transcendentals=0)
LIMIT = pltpu.CompilerParams(vmem_limit_bytes=60 << 20)


def attend_forward(stage, sc, pos, qz, pieces, carried, last):
    rows = pos.shape[-1]
    blocks = 4
    first = carried is None
    stat = jax.ShapeDtypeStruct((2, KV_HEADS, 1, GROUP * rows), F32)
    mix = jax.ShapeDtypeStruct((2, KV_HEADS, HEAD_DIM, GROUP * rows), F32)
    scratch = [
        pltpu.VMEM((blocks, KV_HEADS, rows, 2 * HEAD_DIM), BF16),
        pltpu.VMEM((rows, rows), F32),
    ]
    if last:
        out_shape = (jax.ShapeDtypeStruct(mix.shape, BF16), stat)
        scratch += [pltpu.VMEM(s.shape, F32) for s in (stat, stat, mix)]
        aliases = {}
    else:
        out_shape = (stat, stat, mix)
        aliases = {} if first else {3 + len(pieces) + i: i for i in range(3)}
    given = (sc, pos, qz, *pieces) + (() if first else tuple(carried))
    pairs = blocks * HEADS * rows * rows
    return pl.pallas_call(
        functools.partial(forward_kernel, stage, last),
        out_shape=out_shape,
        grid=(1,),
        in_specs=[SM] + wholes(*given[1:]),
        out_specs=wholes(*out_shape),
        scratch_shapes=scratch,
        input_output_aliases=aliases,
        compiler_params=LIMIT,
        cost_estimate=FREE,
    )(*given)


def attend_backward(stage, sc, pos, qz, gz, lse, delta, pieces, dq, own_type):
    rows = pos.shape[-1]
    blocks = 4
    first = dq is None
    wide = (KV_HEADS, rows, 2 * HEAD_DIM)
    given = (sc, pos, qz, gz, lse, delta, *pieces) + (() if first else (dq,))
    pairs = blocks * HEADS * rows * rows
    out_shape = (
        jax.ShapeDtypeStruct((2, KV_HEADS, HEAD_DIM, GROUP * rows), F32),
        jax.ShapeDtypeStruct((blocks // 2,) + wide, own_type),
        jax.ShapeDtypeStruct(wide, BF16),
        jax.ShapeDtypeStruct(wide, BF16),
    )
    return pl.pallas_call(
        functools.partial(backward_kernel, stage, first, own_type),
        out_shape=out_shape,
        grid=(1,),
        in_specs=[SM] + wholes(*given[1:]),
        out_specs=wholes(*out_shape),
        scratch_shapes=[
            pltpu.VMEM((blocks,) + wide, BF16),
            pltpu.VMEM((rows, rows), F32),
            pltpu.VMEM((blocks,) + wide, F32),
        ],
        input_output_aliases={} if first else {len(given) - 1: 0},
        compiler_params=LIMIT,
        cost_estimate=FREE,
    )(*given)


def load_parts(sc, at, pieces, full, sems, dim):
    size = pieces[0].shape[dim]
    copies = []
    for i, piece in enumerate(pieces):
        if len(pieces) == 1:
            to = full
        elif dim == 0:
            to = full.at[pl.ds(pl.multiple_of(sc[at + i] * size, 16), size)]
        else:
            to = full.at[:, pl.ds(pl.multiple_of(sc[at + i] * size, 128), size)]
        copies.append(pltpu.make_async_copy(piece, to, sems.at[i]))
    for copy in copies:
        copy.start()
    return copies


def norm_scale(v):
    return lax.rsqrt(jnp.mean(v * v, axis=0, keepdims=True) + EPSILON)


def project_kernel(pieces, *refs):
    sc, xa, xb, cos, sin = refs[:5]
    parts = refs[5 : 5 + pieces]
    qz, kv, normed_t, gains, pos, ids, full, sems = refs[5 + pieces :]
    copies = load_parts(sc, 3, parts, full, sems, 0)
    rows = xa.shape[-1]
    width = full.shape[0]
    for q, x in enumerate((xa, xb)):
        p = x[width : width + 16].astype(F32)
        p = p[0:1] * 64.0 + p[1:2]
        pos[q] = p.astype(jnp.int32)
        block = sc[2] + (sc[0] if q == 0 else 3 - sc[0])
        lane = lax.broadcasted_iota(jnp.int32, (1, rows), 1).astype(F32)
        begin = block * rows + jnp.min(lane - p).astype(jnp.int32)
        ids[q] = block
        ids[2 + q] = lax.div(begin, rows)
    ids[4] = sc[2]
    ids[5] = sc[0]
    flat = [x[:width].astype(F32) for x in (xa, xb)]
    scaled = [v * norm_scale(v) for v in flat]
    for copy in copies:
        copy.wait()
    gains[...] = full[:, width + 320 : width + 448]
    gain = full[:, width + 384 : width + 385].astype(F32)
    half = HEAD_DIM // 2
    for q in range(2):
        normed = (scaled[q] * gain).astype(BF16)
        at = slice(q * rows, (q + 1) * rows)
        normed_t[:, at] = normed
        made = jnp.dot(normed.T, full[:, : width + 384], preferred_element_type=F32).T
        c, s = cos[:, at], sin[:, at]
        for h in range(HEADS):
            a = made[64 * h : 64 * h + half]
            b = made[64 * h + half : 64 * h + 64]
            ra = (a * c - b * s).astype(BF16) * jnp.asarray(HEAD_DIM**-0.5, BF16)
            rb = (b * c + a * s).astype(BF16) * jnp.asarray(HEAD_DIM**-0.5, BF16)
            group, lanes = h // GROUP, slice(h % GROUP * rows, (h % GROUP + 1) * rows)
            qz[q, group, :half, lanes] = ra
            qz[q, group, half : 2 * half, lanes] = rb
            qz[q, group, 2 * half :, lanes] = jnp.zeros((2 * half, rows), BF16)
        for k in range(KV_HEADS):
            row = width + 64 * k
            a = made[row : row + half]
            b = made[row + half : row + 64]
            ra = (a * c - b * s).astype(BF16)
            rb = (b * c + a * s).astype(BF16)
            v = made[row + 192 : row + 256].astype(BF16)
            kv[q, k] = jnp.concatenate([ra, rb, v], axis=0).T


def project(sc, xs, cos, sin, parts):
    rows = xs[0].shape[1]
    count = 2 * rows
    width = HEADS * HEAD_DIM
    out_shape = (
        jax.ShapeDtypeStruct((2, KV_HEADS, 2 * HEAD_DIM, GROUP * rows), BF16),
        jax.ShapeDtypeStruct((2, KV_HEADS, rows, 2 * HEAD_DIM), BF16),
        jax.ShapeDtypeStruct((width, count), BF16),
        jax.ShapeDtypeStruct((width, 128), BF16),
        jax.ShapeDtypeStruct((2, 1, rows), jnp.int32),
        jax.ShapeDtypeStruct((8,), jnp.int32),
    )
    return pl.pallas_call(
        functools.partial(project_kernel, len(parts)),
        out_shape=out_shape,
        grid=(1,),
        in_specs=[SM] + wholes(*xs, cos, sin) + [HB] * len(parts),
        out_specs=wholes(*out_shape[:-1]) + [SM],
        scratch_shapes=[
            pltpu.VMEM((width, parts[0].shape[1]), BF16),
            pltpu.SemaphoreType.DMA((len(parts),)),
        ],
        compiler_params=LIMIT,
        cost_estimate=FREE,
    )(sc, *xs, cos, sin, *parts)


def wide(value):
    over = -value.shape[1] % 128
    if not over:
        return value
    return jnp.concatenate([value, jnp.zeros((value.shape[0], over), value.dtype)], axis=1)


def slot_of(sc, fsdp, f):
    ys = fsdp // 2
    return lax.rem(f + sc[0], 2), lax.rem(lax.div(f, 2) - sc[1] + ys, ys)


def put_slabs(packed, sc, fsdp, at, value):
    value = wide(value).astype(BF16)
    r = value.shape[0] // fsdp
    for f in range(fsdp):
        k, y = slot_of(sc, fsdp, f)
        for s in range(value.shape[1] // 128):
            packed[k, y, pl.ds(at + s * r, r)] = value[
                f * r : (f + 1) * r, s * 128 : (s + 1) * 128
            ]


def norm_back(v, gain, grad):
    r = norm_scale(v)
    scaled = grad * gain
    d_v = r * scaled - v * (r * r * r * jnp.mean(scaled * v, axis=0, keepdims=True))
    return d_v, jnp.sum(grad * (v * r), axis=1, keepdims=True)


def feed_kernel(fsdp, pieces, chunk, *refs):
    sc, xa, xb, ca, cb, mix, gains = refs[:7]
    parts = refs[7 : 7 + pieces]
    downs = refs[7 + pieces : 7 + 2 * pieces]
    refs = refs[7 + 2 * pieces :]
    res_a, res_b, d_middle, gz, delta, mine, give, second = refs[:8]
    full, out_w, down, packed, att_t, mid, n2, n2_t, res, d_second, cot_t, cot = refs[8:20]
    sems, out_sems, down_sems, grad_sems = refs[20:]
    ff = down.shape[1]
    out_copies = load_parts(sc, 3, [p.at[:, 2 * ff :] for p in parts], out_w, out_sems, 0)
    copies = load_parts(sc, 3, [p.at[:, : 2 * ff] for p in parts], full, sems, 0)
    down_copies = load_parts(sc, 3, downs, down, down_sems, 1)
    rows = xa.shape[-1]
    width, ff = down.shape
    shard = width // fsdp
    down_shard = ff // fsdp
    for q, c in enumerate((ca, cb)):
        cot_t[:, q * rows : (q + 1) * rows] = c[...]
        for h in range(HEADS):
            att_t[64 * h : 64 * h + 64, q * rows : (q + 1) * rows] = mix[
                q, h // GROUP, :, h % GROUP * rows : (h % GROUP + 1) * rows
            ]
    cot[...] = cot_t[...].T
    gain = gains[:, 65:66].astype(F32)
    for copy in out_copies:
        copy.wait()
    branch_t = jnp.dot(out_w[...].T, att_t[...], preferred_element_type=F32)
    for q, x in enumerate((xa, xb)):
        at = slice(q * rows, (q + 1) * rows)
        mid[:, at] = x[:width].astype(F32) + branch_t[:, at]
    n2_t[...] = (mid[...] * norm_scale(mid[...]) * gain).astype(BF16)
    n2[...] = n2_t[...].T
    res[...] = mid[...]
    d_second[...] = jnp.zeros(d_second.shape, F32)
    for copy in copies + down_copies:
        copy.wait()
    up_at = ff // 128 * shard
    out_at = 2 * up_at
    down_at = out_at + -(-width // 128) * shard
    used = down_at + -(-down_shard // 128) * width
    rows_all = packed.shape[2]
    if rows_all > used:
        packed[:, :, used:] = jnp.zeros((2, fsdp // 2, rows_all - used, 128), BF16)

    def step(j, _):
        cols = pl.ds(pl.multiple_of(j * chunk, 128), chunk)
        up_cols = pl.ds(pl.multiple_of(ff + j * chunk, 128), chunk)
        gate_w, up_w, down_w = full[:, cols], full[:, up_cols], down[:, cols]
        gate = jnp.dot(n2[...], gate_w, preferred_element_type=F32)
        up = jnp.dot(n2[...], up_w, preferred_element_type=F32)
        sig = 1.0 / (1.0 + jnp.exp(-gate))
        silu = gate * sig
        hidden = (silu * up).astype(BF16)
        res[...] += dot(down_w, hidden, 1, 1)
        d_hidden = jnp.dot(cot[...], down_w, preferred_element_type=F32)
        d_gate = (d_hidden * up * (sig * (1.0 + gate * (1.0 - sig)))).astype(BF16)
        d_up = (d_hidden * silu).astype(BF16)
        d_second[...] += dot(gate_w, d_gate, 1, 1) + dot(up_w, d_up, 1, 1)
        slab = pl.multiple_of(j * (chunk // 128) * shard, 8)
        put_slabs(packed, sc, fsdp, slab, jnp.dot(n2_t[...], d_gate, preferred_element_type=F32))
        put_slabs(
            packed, sc, fsdp, up_at + slab, jnp.dot(n2_t[...], d_up, preferred_element_type=F32)
        )
        down_g = jnp.dot(cot_t[...], hidden, preferred_element_type=F32).astype(BF16)
        if down_shard % 128:
            for n in range(chunk // down_shard):
                slot_k, slot_y = slot_of(sc, fsdp, j * (chunk // down_shard) + n)
                part = wide(down_g[:, n * down_shard : (n + 1) * down_shard])
                for s in range(part.shape[1] // 128):
                    packed[slot_k, slot_y, down_at + s * width : down_at + (s + 1) * width] = part[
                        :, s * 128 : (s + 1) * 128
                    ]
        else:
            for n in range(chunk // 128):
                slab = j * (chunk // 128) + n
                slot_k, slot_y = slot_of(sc, fsdp, lax.div(slab, down_shard // 128))
                at = pl.multiple_of(down_at + lax.rem(slab, down_shard // 128) * width, 16)
                packed[slot_k, slot_y, pl.ds(at, width)] = down_g[:, n * 128 : (n + 1) * 128]
        return 0

    lax.fori_loop(0, ff // chunk, step, 0)
    spans = [(0, out_at), (down_at, rows_all - down_at), (out_at, down_at - out_at)]
    sends = [
        [
            pltpu.make_async_copy(
                packed.at[k, :, pl.ds(at, n)], to.at[:, pl.ds(at, n)], grad_sems.at[k, i]
            )
            for k, to in enumerate((mine, give))
        ]
        for i, (at, n) in enumerate(spans)
    ]
    for copy in sends[0] + sends[1]:
        copy.start()
    res_a[...] = res[:, :rows].astype(BF16)
    res_b[...] = res[:, rows:].astype(BF16)
    d_v, gain_grad = norm_back(mid[...], gain, d_second[...])
    second[...] = jnp.broadcast_to(gain_grad, second.shape)
    d_mid = cot_t[...].astype(F32) + d_v
    d_middle[...] = d_mid
    branch = d_mid.astype(BF16)
    put_slabs(packed, sc, fsdp, out_at, dot(att_t[...], branch, 1, 1))
    for copy in sends[2]:
        copy.start()
    d_mix = jnp.dot(out_w[...], branch, preferred_element_type=F32).astype(BF16)
    for q in range(2):
        for h in range(HEADS):
            at = slice(q * rows, (q + 1) * rows)
            part = d_mix[64 * h : 64 * h + 64, at]
            group, lanes = h // GROUP, slice(h % GROUP * rows, (h % GROUP + 1) * rows)
            gz[q, group, :64, lanes] = jnp.zeros((64, rows), BF16)
            gz[q, group, 64:, lanes] = part
            delta[q, group, :, lanes] = jnp.sum(
                part.astype(F32) * att_t[64 * h : 64 * h + 64, at].astype(F32),
                axis=0,
                keepdims=True,
            )
    for copy in sends[0] + sends[1] + sends[2]:
        copy.wait()


def feed_rows(fsdp, ctx, width, ff):
    used = (2 * (ff // 128) + -(-width // 128)) * (width // fsdp) + -(-(ff // fsdp) // 128) * width
    return -(-used // (16 * ctx)) * 16 * ctx


def feed(fsdp, ctx, sc, xs, cots, mix, gains, parts, downs):
    rows = cots[0].shape[1]
    width = cots[0].shape[0]
    count = 2 * rows
    ff = downs[0].shape[1] * len(downs)
    packed = (fsdp // 2, feed_rows(fsdp, ctx, width, ff), 128)
    out_shape = (
        jax.ShapeDtypeStruct((width, rows), BF16),
        jax.ShapeDtypeStruct((width, rows), BF16),
        jax.ShapeDtypeStruct((width, count), F32),
        jax.ShapeDtypeStruct((2, KV_HEADS, 2 * HEAD_DIM, GROUP * rows), BF16),
        jax.ShapeDtypeStruct((2, KV_HEADS, 1, GROUP * rows), F32),
        jax.ShapeDtypeStruct(packed, BF16),
        jax.ShapeDtypeStruct(packed, BF16),
        jax.ShapeDtypeStruct((width, 128), F32),
    )
    return pl.pallas_call(
        functools.partial(feed_kernel, fsdp, len(parts), ff // 4 if ff // fsdp % 128 else ff // 3),
        out_shape=out_shape,
        grid=(1,),
        in_specs=[SM] + wholes(*xs, *cots, mix, gains) + [HB] * (2 * len(parts)),
        out_specs=wholes(*out_shape[:5]) + [HB, HB] + wholes(out_shape[7]),
        scratch_shapes=[
            pltpu.VMEM((width, 2 * ff), BF16),
            pltpu.VMEM((width, width), BF16),
            pltpu.VMEM((width, ff), BF16),
            pltpu.VMEM((2,) + packed, BF16),
            pltpu.VMEM((width, count), BF16),
            pltpu.VMEM((width, count), F32),
            pltpu.VMEM((count, width), BF16),
            pltpu.VMEM((width, count), BF16),
            pltpu.VMEM((width, count), F32),
            pltpu.VMEM((width, count), F32),
            pltpu.VMEM((width, count), BF16),
            pltpu.VMEM((count, width), BF16),
            pltpu.SemaphoreType.DMA((len(parts),)),
            pltpu.SemaphoreType.DMA((len(parts),)),
            pltpu.SemaphoreType.DMA((len(parts),)),
            pltpu.SemaphoreType.DMA((2, 3)),
        ],
        compiler_params=LIMIT,
        cost_estimate=FREE,
    )(sc, *xs, *cots, mix, gains, *parts, *downs)


def last_kernel(fsdp, pieces, chain, *refs):
    sc, xa, xb, cos, sin, normed_t, gains, second, d_middle, dq, own, *twin = refs[:13]
    refs = refs[13:]
    if chain:
        came = refs[0]
        refs = refs[1:]
    parts = refs[:pieces]
    grad_a, grad_b, mine, give, full, packed, made, sems = refs[pieces:]
    copies = load_parts(sc, 3, parts, full, sems, 0)
    rows = xa.shape[-1]
    width = full.shape[0]
    half = HEAD_DIM // 2
    for q in range(2):
        at = slice(q * rows, (q + 1) * rows)
        c, s = cos[:, at], sin[:, at]
        for h in range(HEADS):
            group, lanes = h // GROUP, slice(h % GROUP * rows, (h % GROUP + 1) * rows)
            a = dq[q, group, :half, lanes] * HEAD_DIM**-0.5
            b = dq[q, group, half:, lanes] * HEAD_DIM**-0.5
            made[64 * h : 64 * h + half, at] = (a * c + b * s).astype(BF16)
            made[64 * h + half : 64 * h + 64, at] = (b * c - a * s).astype(BF16)
        for k in range(KV_HEADS):
            both = own[q, k] + twin[q][k].astype(F32)
            if chain:
                both = both + came[q, k].astype(F32)
            both = both.T
            a, b = both[:half], both[half : 2 * half]
            row = width + 64 * k
            made[row : row + half, at] = (a * c + b * s).astype(BF16)
            made[row + half : row + 64, at] = (b * c - a * s).astype(BF16)
            made[row + 192 : row + 256, at] = both[2 * half :].astype(BF16)
    for copy in copies:
        copy.wait()
    gain = gains[:, 64:65].astype(F32)
    d_first = jnp.dot(full[:, : width + 384], made[...], preferred_element_type=F32)
    v = jnp.concatenate([xa[:width], xb[:width]], axis=1).astype(F32)
    d_v, first = norm_back(v, gain, d_first)
    d_x = (d_middle[...] + d_v).astype(BF16)
    grad_a[...] = d_x[:, :rows]
    grad_b[...] = d_x[:, rows:]
    front = dot(normed_t[...], made[...], 1, 1)
    lane = lax.broadcasted_iota(jnp.int32, (width, 64), 1)
    ends = jnp.where(lane == 0, first, second[:, :64])
    put_slabs(packed, sc, fsdp, 0, jnp.concatenate([front, ends], axis=1))
    used = (width + 448) // 128 * (width // fsdp)
    total = packed.shape[2]
    if total > used:
        packed[:, :, used:] = jnp.zeros((2, fsdp // 2, total - used, 128), BF16)
    mine[...] = packed[0]
    give[...] = packed[1]


def last(fsdp, ctx, sc, xs, cos, sin, normed_t, gains, second, d_middle, dq, dkv, parts):
    width, count = normed_t.shape
    rows = count // 2
    used = (width + 448) // 128 * (width // fsdp)
    packed = (fsdp // 2, -(-used // (16 * ctx)) * 16 * ctx, 128)
    given = (*xs, cos, sin, normed_t, gains, second, d_middle, dq, *dkv)
    out_shape = (
        jax.ShapeDtypeStruct((width, rows), BF16),
        jax.ShapeDtypeStruct((width, rows), BF16),
        jax.ShapeDtypeStruct(packed, BF16),
        jax.ShapeDtypeStruct(packed, BF16),
    )
    return pl.pallas_call(
        functools.partial(last_kernel, fsdp, len(parts), len(dkv) == 4),
        out_shape=out_shape,
        grid=(1,),
        in_specs=[SM] + wholes(*given) + [HB] * len(parts),
        out_specs=wholes(*out_shape),
        scratch_shapes=[
            pltpu.VMEM((width, parts[0].shape[1]), BF16),
            pltpu.VMEM((2,) + packed, BF16),
            pltpu.VMEM((width + 384, count), BF16),
            pltpu.SemaphoreType.DMA((len(parts),)),
        ],
        compiler_params=LIMIT,
        cost_estimate=FREE,
    )(sc, *given, *parts)


def unpack_kernel(places, flat, *outs):
    for out, (at, rows, skip) in zip(outs, places, strict=True):
        columns = out.shape[1]
        done = 0
        while done < columns:
            slab, lane = divmod(skip + done, 128)
            n = min(128 - lane, columns - done)
            out[:, done : done + n] = flat[
                at + slab * rows : at + (slab + 1) * rows, lane : lane + n
            ].astype(F32)
            done += n


def join_unpack_kernel(places, sc, near, far, *refs):
    *outs, flat = refs
    part = near.shape[0] // 2
    for half in range(2):
        for x in range(2):
            piece = near if x == 0 else far
            at = pl.multiple_of(part * (2 * half + lax.rem(sc[0] + x, 2)), 16)
            flat[pl.ds(at, part)] = piece[half * part : (half + 1) * part]
    unpack_kernel(places, flat, *outs)


def unpack(flat, places):
    out_shape = tuple(jax.ShapeDtypeStruct((p[1], p[3]), F32) for p in places)
    return pl.pallas_call(
        functools.partial(unpack_kernel, [p[:3] for p in places]),
        out_shape=out_shape,
        grid=(1,),
        in_specs=wholes(flat),
        out_specs=wholes(*out_shape),
        compiler_params=LIMIT,
        cost_estimate=FREE,
    )(flat)


def join_unpack(x, near, far, places):
    out_shape = tuple(jax.ShapeDtypeStruct((p[1], p[3]), F32) for p in places)
    return pl.pallas_call(
        functools.partial(join_unpack_kernel, [p[:3] for p in places]),
        out_shape=out_shape,
        grid=(1,),
        in_specs=[SM] + wholes(near, far),
        out_specs=wholes(*out_shape),
        scratch_shapes=[pltpu.VMEM((2 * near.shape[0], 128), BF16)],
        compiler_params=LIMIT,
        cost_estimate=FREE,
    )(x, near, far)


def chip_sum(mine, got, i):
    return mine[i].astype(F32) + got[i].astype(F32)


def sum_y(mine, got, send):
    total = chip_sum(mine, got, 0)
    for s in range(1, mine.shape[0]):
        total = total + send["shift"][s](chip_sum(mine, got, s).astype(BF16)).astype(F32)
    return total.astype(BF16)


def spread_kernel(got, out):
    total = got[0].astype(F32)
    for i in range(1, got.shape[0]):
        total = total + got[i].astype(F32)
    total = total.astype(BF16)
    for i in range(got.shape[0]):
        out[i] = total


def simple_call(kernel, out_shape, *given):
    return pl.pallas_call(
        kernel,
        out_shape=out_shape,
        grid=(1,),
        in_specs=wholes(*given),
        out_specs=whole(out_shape),
        compiler_params=LIMIT,
        cost_estimate=FREE,
    )(*given)


def sum_over(total, axes, size):
    parts = total.reshape(size, total.shape[0] // size, 128)
    got = lax.all_to_all(parts, axes, 0, 0, tiled=True)
    spread = simple_call(spread_kernel, jax.ShapeDtypeStruct(got.shape, BF16), got)
    return lax.all_to_all(spread, axes, 0, 0, tiled=True).reshape(-1, 128)


def came_kernel(own, twin_a, twin_b, *refs):
    *came, out = refs
    for i, twin in enumerate((twin_a, twin_b)):
        total = own[i].astype(F32) + twin[...].astype(F32)
        for c in came:
            total = total + c[i].astype(F32)
        out[i] = total.astype(BF16)


def halves_kernel(one, one_came, two, two_came, out):
    n = one.shape[0]
    out[:n] = (one[...].astype(F32) + one_came[...].astype(F32)).astype(BF16)
    out[n:] = (two[...].astype(F32) + two_came[...].astype(F32)).astype(BF16)


def first_kernel(x, mine, got, to_y, to_x):
    i = pl.program_id(0)
    total = (mine[...].astype(F32) + got[...].astype(F32)).astype(BF16)

    @pl.when(i < 2)
    def _():
        to_y[...] = total

    @pl.when(i >= 2)
    def _():
        to_x[...] = total


def first_sums(x, mine, got):
    n = mine.shape[1] // 4
    block = (1, n, 128)

    def at(i, x):
        return jnp.where(i == 2, 0, 1), jnp.where(i < 2, i, 3 - x[0]), 0

    shapes = (jax.ShapeDtypeStruct((2, n, 128), BF16),) * 2
    return pl.pallas_call(
        first_kernel,
        out_shape=shapes,
        grid_spec=pltpu.PrefetchScalarGridSpec(
            num_scalar_prefetch=1,
            grid=(4,),
            in_specs=[pl.BlockSpec(block, at)] * 2,
            out_specs=[
                pl.BlockSpec(block, lambda i, x: (jnp.minimum(i, 1), 0, 0)),
                pl.BlockSpec(block, lambda i, x: (jnp.maximum(i - 2, 0), 0, 0)),
            ],
        ),
        compiler_params=LIMIT,
        cost_estimate=FREE,
    )(x, mine, got)


def second_kernel(x, mine, got, came_y, came_x, *outs):
    i = pl.program_id(0)
    total = mine[...].astype(F32) + got[...].astype(F32)
    came = jnp.where(i < 2, came_y[...].astype(F32), came_x[...].astype(F32))
    total = (total + came).astype(BF16)[0]
    for n, out in enumerate(outs):

        @pl.when(i == n)
        def _(out=out):
            out[...] = total


def second_sums(x, mine, got, came_y, came_x):
    n = mine.shape[1] // 4
    block = (1, n, 128)

    def own(i, x):
        return (i == 2) * 1, jnp.where(i == 0, 1 - x[0], jnp.where(i == 1, x[0], 2 + x[0])), 0

    def from_y(i, x):
        return jnp.where(i == 0, 1 - x[0], x[0]), 0, 0

    def from_x(i, x):
        return jnp.where(i == 3, 0, 1), 0, 0

    return pl.pallas_call(
        second_kernel,
        out_shape=(jax.ShapeDtypeStruct((n, 128), BF16),) * 4,
        grid_spec=pltpu.PrefetchScalarGridSpec(
            num_scalar_prefetch=1,
            grid=(4,),
            in_specs=[
                pl.BlockSpec(block, own),
                pl.BlockSpec(block, own),
                pl.BlockSpec(block, from_y),
                pl.BlockSpec(block, from_x),
            ],
            out_specs=[pl.BlockSpec((n, 128), lambda i, x: (0, 0))] * 4,
        ),
        compiler_params=LIMIT,
        cost_estimate=FREE,
    )(x, mine, got, came_y, came_x)


def gather_y(own, send, fsdp):
    return [own] + [send["shift"][s](own) for s in range(1, fsdp // 2)]


def gather_pieces(got, send, fsdp, core, y, join, dim):
    pieces = got + [send["core"](g) for g in got]
    own = got[0]
    if not join:
        return pieces
    buffer = jnp.zeros((fsdp,) + own.shape, own.dtype)
    for piece, f in zip(pieces, piece_order(fsdp, core, y), strict=True):
        buffer = lax.dynamic_update_index_in_dim(buffer, piece, f, 0)
    if dim:
        buffer = buffer.swapaxes(0, 1)
        return [buffer.reshape(own.shape[0], fsdp * own.shape[1])]
    return [buffer.reshape(fsdp * own.shape[0], own.shape[1])]


def piece_order(fsdp, core, y):
    ys = fsdp // 2
    source = [lax.rem(y - s + ys, ys) * 2 for s in range(ys)]
    return [f + core for f in source] + [f + 1 - core for f in source]


def body(
    fsdp,
    ctx,
    tokens,
    segment_ids,
    positions,
    cotangent,
    norm_first,
    query_weight,
    key_weight,
    value_weight,
    output_weight,
    norm_second,
    gate_weight,
    up_weight,
    down_weight,
):
    send = make_send(fsdp, ctx)
    ys, hs = fsdp // 2, ctx // 2
    _, count, width = tokens.shape
    rows = count // 2
    kv_width = KV_HEADS * HEAD_DIM
    y, core = lax.axis_index("y"), lax.axis_index("core")
    h, x = lax.axis_index("h"), lax.axis_index("x")
    ci = 2 * h + x
    reach = min(hs - 1, -(-(-(-(DOC_MOST - 1) // rows)) // 4))
    order = jnp.stack([core, y, 4 * h] + piece_order(fsdp, core, y)).astype(jnp.int32)
    shard = gate_weight.shape[0]
    join = shard % 16 != 0
    own_pos = lax.dynamic_slice_in_dim(positions, ci * count, count, 1)
    pos_rows = jnp.concatenate(
        [lax.div(own_pos, 64), lax.rem(own_pos, 64), jnp.zeros((14, count), jnp.int32)], axis=0
    )
    carried = jnp.concatenate([tokens.reshape(count, width).T, pos_rows.astype(BF16)], axis=0)
    *pair, query_weight = tie(*pick_home(carried, h), query_weight)
    xs = send_home(send, pair)
    packed = jnp.concatenate(
        [
            query_weight,
            key_weight,
            value_weight,
            norm_first[:, None],
            norm_second[:, None],
            jnp.zeros((shard, 62), BF16),
        ],
        axis=1,
    )
    first_parts = gather_y(packed, send, fsdp)
    first_parts = gather_pieces(first_parts, send, fsdp, core, y, join, 0)
    pos_f = jnp.concatenate([a[width : width + 2] for a in xs], axis=1).astype(F32)
    pos_f = pos_f[0:1] * 64.0 + pos_f[1:2]
    frequency = jnp.exp(
        jnp.arange(HEAD_DIM // 2, dtype=F32) * (-math.log(10000.0) * 2.0 / HEAD_DIM)
    )
    angle = frequency[:, None] * pos_f
    cos, sin = jnp.cos(angle), jnp.sin(angle)
    qz, kv, normed_t, gains, pos, ids = project(order, xs, cos, sin, first_parts)

    feed_own = jnp.concatenate([gate_weight, up_weight, output_weight], axis=1)
    feed_own, down_own, _ = tie(feed_own, down_weight.T, first_parts[-1])
    feed_got = gather_y(feed_own, send, fsdp)
    down_got = gather_y(down_own, send, fsdp)
    cot_t, _ = tie(cotangent.reshape(count, width).T, kv)
    stages = []
    carried = None
    for s in range(reach + 1):
        stages.append((kv, send["core"](kv)))
        if s < reach:
            kv = send["up"](kv)
        carried = attend_forward(s, ids, pos, qz, stages[s], carried, s == reach)
        if s < reach:
            kv, *carried = tie(kv, *carried)
    mixed, lse = carried
    cots = send_home(send, pick_home(cot_t, h))
    feed_parts = gather_pieces(feed_got, send, fsdp, core, y, join, 0)
    down_parts = gather_pieces(down_got, send, fsdp, core, y, join, 1)
    res_a, res_b, d_middle, gz, delta, mine, give, second = feed(
        fsdp, ctx, order, xs, cots, mixed, gains, feed_parts, down_parts
    )

    got = send["core"](give)
    crossed = ys == 2
    x_ref = x.astype(jnp.int32).reshape(1)
    if crossed:
        first_y, first_x = first_sums(x_ref, mine, got)
    dq = None
    came = None
    for s in range(reach, -1, -1):
        sc = ids
        if s == reach - 1 and crossed:
            sc, first_y, first_x = tie(sc, first_y, first_x)
            came_y, came_x = send["shift"][1](first_y), send["across"](first_x)
        if s == 0 and crossed:
            give_one, keep_one, give_two, keep_two = second_sums(x_ref, mine, got, came_y, came_x)
            sc, give_one, give_two = tie(sc, give_one, give_two)
            came_one, came_two = send["across"](give_one), send["shift"][1](give_two)
        if came is not None:
            sc, came = tie(sc, came)
            came = send["down"](came)
        dq, own, *other = attend_backward(
            s, sc, pos, qz, gz, lse, delta, stages[s], dq, F32 if s == 0 else BF16
        )
        twin = tuple(send["core"](o) for o in other)
        if s > 0:
            if s < reach:
                *twin, came, dq = tie(*twin, came, dq)
            given = (own, *twin) if came is None else (own, *twin, came)
            came = simple_call(came_kernel, jax.ShapeDtypeStruct(own.shape, BF16), *given)
    dkv = (own, *twin) if came is None else (own, *twin, came)
    result = send_back(send, res_a, res_b)
    if crossed:
        *result, came_one, came_two, dq = tie(*result, came_one, came_two, dq)
    else:
        *result, dq = tie(*result, dq)
    tok_a, tok_b, mine_front, give_front = last(
        fsdp, ctx, order, xs, cos, sin, normed_t, gains, second, d_middle, dq, dkv, first_parts
    )
    got_front = send["core"](give_front)
    front = sum_y(mine_front, got_front, send)
    if crossed:
        late = simple_call(
            halves_kernel,
            jax.ShapeDtypeStruct((mine.shape[1] // 2, 128), BF16),
            keep_one,
            came_one,
            keep_two,
            came_two,
        )
        late = sum_over(late, ("h",), hs)
        late_far = send["across"](late)
    else:
        late = sum_over(sum_y(mine, got, send), CTX, ctx)
    front = sum_over(front, CTX, ctx)
    tokens_grad = send_back(send, tok_a, tok_b)

    ff = gate_weight.shape[1]
    down_shard = down_weight.shape[0]
    gate_rows, out_rows = ff // 128 * shard, -(-width // 128) * shard
    places = [
        (0, shard, 0, ff),
        (gate_rows, shard, 0, ff),
        (2 * gate_rows, shard, 0, width),
        (2 * gate_rows + out_rows, width, 0, down_shard),
    ]
    if crossed:
        late_grads = join_unpack(x_ref, late, late_far, places)
    else:
        late_grads = unpack(late, places)
    gate_grad, up_grad, output_grad, down_grad = late_grads
    query_grad, key_grad, value_grad, ends = unpack(
        front,
        [
            (0, shard, 0, width),
            (0, shard, width, kv_width),
            (0, shard, width + kv_width, kv_width),
            (0, shard, width + 2 * kv_width, 64),
        ],
    )
    return (
        low_high(*result, h).T[None],
        low_high(*tokens_grad, h).T[None],
        ends[:, 0],
        query_grad,
        key_grad,
        value_grad,
        output_grad,
        ends[:, 1],
        gate_grad,
        up_grad,
        down_grad.T,
    )


def solution(mesh):
    fsdp, ctx = mesh.shape["fsdp"], mesh.shape["ctx"]
    places = Mesh(mesh.devices.reshape(fsdp // 2, 2, ctx // 2, 2), AXES)
    owner = ("y", "core")
    flat, split = P(owner), P(owner, None)
    whole = P(owner, CTX, None)
    return jax.shard_map(
        functools.partial(body, fsdp, ctx),
        mesh=places,
        in_specs=(whole, split, split, whole, flat, split, split, split, split, flat, split, split, split),
        out_specs=(whole, whole, flat, split, split, split, split, flat, split, split, split),
        check_vma=False,
    )
```

```python
import functools
import math

import jax
import jax.numpy as jnp
from jax import lax
from jax.experimental import pallas as pl
from jax.experimental.pallas import tpu as pltpu
from jax.sharding import Mesh
from jax.sharding import PartitionSpec as P

HEADS = 9
KV_HEADS = 3
GROUP = HEADS // KV_HEADS
HEAD_DIM = 64
EPSILON = 1e-05
MASKED = -1e30
DOC_MOST = 2000
AXES = ("y", "core", "h", "x")
CTX = ("h", "x")
F32 = jnp.float32
BF16 = jnp.bfloat16


def moves(fsdp, ctx, step):
    pairs = []
    for f in range(fsdp):
        for c in range(ctx):
            to = step(f // 2, f % 2, c // 2, c % 2)
            if to is not None:
                y, core, h, x = to
                pairs.append((f * ctx + c, (2 * y + core) * ctx + 2 * h + x))
    return pairs


def make_send(fsdp, ctx):
    ys, hs, blocks = fsdp // 2, ctx // 2, 2 * ctx

    def along(pairs):
        return lambda a: lax.ppermute(a, AXES, pairs)

    def by(step):
        return along(moves(fsdp, ctx, step))

    def home(slot):
        def step(y, core, h, x):
            low = 2 * h + x
            block = low if h % 2 == slot else blocks - 1 - low
            return (y, int(block % 4 in (1, 2)), block // 4, core)

        return moves(fsdp, ctx, step)

    def back(pairs):
        return along([(b, a) for a, b in pairs])

    return dict(
        home=[along(home(0)), along(home(1))],
        back=[back(home(0)), back(home(1))],
        core=by(lambda y, k, h, x: (y, 1 - k, h, x)),
        across=by(lambda y, k, h, x: (y, k, h, 1 - x)),
        up=by(lambda y, k, h, x: (y, k, h + 1, x) if h + 1 < hs else None),
        down=by(lambda y, k, h, x: (y, k, h - 1, x) if h > 0 else None),
        shift=[by(lambda y, k, h, x, s=s: ((y + s) % ys, k, h, x)) for s in range(ys)],
    )


def pick_home(a, h):
    r = a.shape[1] // 2
    low, high = a[:, :r], a[:, r:]
    even = lax.rem(h, 2) == 0
    return jnp.where(even, low, high), jnp.where(even, high, low)


def send_home(send, pair):
    return send["home"][0](pair[0]), send["home"][1](pair[1])


def send_back(send, a, b):
    return send["back"][0](a), send["back"][1](b)


def low_high(a, b, h):
    even = lax.rem(h, 2) == 0
    return jnp.concatenate([jnp.where(even, a, b), jnp.where(even, b, a)], axis=1)


def tie(*values):
    return lax.optimization_barrier(values)


def bias_of(begin, place, block_id, keys, rows):
    key_place = block_id * keys + lax.broadcasted_iota(jnp.int32, (keys, rows), 0)
    seen = (key_place >= begin) & (key_place <= place)
    return jnp.where(seen, 0.0, MASKED)


def dot(left, right, left_dim, right_dim):
    return lax.dot_general(
        left, right, (((left_dim,), (right_dim,)), ((), ())), preferred_element_type=F32
    )


def load_blocks(pieces, held):
    held[:2] = pieces[0][...]
    held[2:] = pieces[1][...]


def each_pair(sc, stage, work):
    base, core = sc[4] - 4 * stage, sc[5]

    def step(i, _):
        q = lax.div(i, 4)
        k = lax.rem(i, 4)
        within = jnp.where(k < 2, core, 1 - core)
        block_id = base + jnp.where(lax.rem(k, 2) == 0, within, 3 - within)

        @pl.when((block_id >= sc[2 + q]) & (block_id <= sc[q]))
        def _():
            work(q, k, block_id)

        return 0

    lax.fori_loop(0, 8, step, 0)


def forward_kernel(stage, last, *refs):
    first = stage == 0
    refs = list(refs)
    sc, pos, qz = refs[:3]
    kv = refs[3:5]
    refs = refs[5:]
    if not first:
        peak_in, total_in, mix_in = refs[:3]
        refs = refs[3:]
    if last:
        out, lse = refs[:2]
        held, bias, peak, total, mix = refs[2:]
    else:
        peak, total, mix = refs[:3]
        held, bias = refs[3:]
    rows = pos.shape[-1]
    if first:
        peak[...] = jnp.full(peak.shape, MASKED, F32)
        total[...] = jnp.zeros(total.shape, F32)
        mix[...] = jnp.zeros(mix.shape, F32)
    else:
        peak[...] = peak_in[...]
        total[...] = total_in[...]
        mix[...] = mix_in[...]
    load_blocks(kv, held)

    def work(q, k, block_id):
        place = sc[q] * rows + lax.broadcasted_iota(jnp.int32, (1, rows), 1)
        bias[...] = bias_of(place - pos[q], place, block_id, rows, rows)
        for c in range(KV_HEADS):
            seen = dot(held[k, c], qz[q, c], 1, 0) + jnp.concatenate([bias[...]] * GROUP, axis=1)
            old = peak[q, c]
            new = jnp.maximum(old, jnp.max(seen, axis=0, keepdims=True))
            expo = jnp.exp(seen - new)
            fade = jnp.exp(old - new)
            peak[q, c] = new
            total[q, c] = total[q, c] * fade + jnp.sum(expo, axis=0, keepdims=True)
            values = held[k, c].T[HEAD_DIM:]
            mix[q, c] = mix[q, c] * fade + dot(values, expo.astype(BF16), 1, 0)

    each_pair(sc, stage, work)
    if last:
        lse[...] = peak[...] + jnp.log(total[...])
        for q in range(2):
            for c in range(KV_HEADS):
                out[q, c] = (mix[q, c] / total[q, c]).astype(BF16)


def backward_kernel(stage, first, own_type, *refs):
    refs = list(refs)
    sc, pos, qz, gz, lse, delta = refs[:6]
    kv = refs[6:8]
    refs = refs[8:]
    if not first:
        dq_in = refs[0]
        refs = refs[1:]
    dq, own, other_a, other_b, held, bias, dkv = refs
    rows = pos.shape[-1]
    if first:
        dq[...] = jnp.zeros(dq.shape, F32)
    else:
        dq[...] = dq_in[...]
    load_blocks(kv, held)
    dkv[...] = jnp.zeros(dkv.shape, F32)

    def work(q, k, block_id):
        place = sc[q] * rows + lax.broadcasted_iota(jnp.int32, (1, rows), 1)
        bias[...] = bias_of(place - pos[q], place, block_id, rows, rows)
        scores = [dot(held[k, c], qz[q, c], 1, 0) for c in range(KV_HEADS)]
        for c in range(KV_HEADS):
            seen = scores[c] + jnp.concatenate([bias[...]] * GROUP, axis=1)
            probs = jnp.exp(seen - lse[q, c])
            d_scores = (probs * (dot(held[k, c], gz[q, c], 1, 0) - delta[q, c])).astype(BF16)
            dkv[k, c] += dot(d_scores, qz[q, c], 1, 1) + dot(probs.astype(BF16), gz[q, c], 1, 1)
            dq[q, c] += dot(held[k, c].T[:HEAD_DIM], d_scores, 1, 0)

    each_pair(sc, stage, work)
    own[...] = dkv[:2].astype(own_type)
    other_a[...] = dkv[2].astype(BF16)
    other_b[...] = dkv[3].astype(BF16)


SM = pl.BlockSpec(memory_space=pltpu.SMEM)
HB = pl.BlockSpec(memory_space=pl.ANY)


def whole(a):
    return pl.BlockSpec(
        a.shape, lambda i: (0,) * len(a.shape), pipeline_mode=pl.Buffered(buffer_count=1)
    )


def wholes(*arrays):
    return [whole(a) for a in arrays]


def takes(us):
    return pl.CostEstimate(flops=int(us * 1.15e9), bytes_accessed=0, transcendentals=0)


LIMIT = pltpu.CompilerParams(vmem_limit_bytes=(64 << 20) - (256 << 10))


def attend_forward(stage, sc, pos, qz, pieces, carried, last):
    rows = pos.shape[-1]
    blocks = 4
    first = carried is None
    stat = jax.ShapeDtypeStruct((2, KV_HEADS, 1, GROUP * rows), F32)
    mix = jax.ShapeDtypeStruct((2, KV_HEADS, HEAD_DIM, GROUP * rows), F32)
    scratch = [
        pltpu.VMEM((blocks, KV_HEADS, rows, 2 * HEAD_DIM), BF16),
        pltpu.VMEM((rows, rows), F32),
    ]
    if last:
        out_shape = (jax.ShapeDtypeStruct(mix.shape, BF16), stat)
        scratch += [pltpu.VMEM(s.shape, F32) for s in (stat, stat, mix)]
        aliases = {}
    else:
        out_shape = (stat, stat, mix)
        aliases = {} if first else {3 + len(pieces) + i: i for i in range(3)}
    given = (sc, pos, qz, *pieces) + (() if first else tuple(carried))
    pairs = blocks * HEADS * rows * rows
    return pl.pallas_call(
        functools.partial(forward_kernel, stage, last),
        out_shape=out_shape,
        grid=(1,),
        in_specs=[SM] + wholes(*given[1:]),
        out_specs=wholes(*out_shape),
        scratch_shapes=scratch,
        input_output_aliases=aliases,
        compiler_params=LIMIT,
        cost_estimate=takes((10, 12)[stage] if stage < 2 else 3),
    )(*given)


def attend_backward(stage, sc, pos, qz, gz, lse, delta, pieces, dq, own_type):
    rows = pos.shape[-1]
    blocks = 4
    first = dq is None
    wide = (KV_HEADS, rows, 2 * HEAD_DIM)
    given = (sc, pos, qz, gz, lse, delta, *pieces) + (() if first else (dq,))
    pairs = blocks * HEADS * rows * rows
    out_shape = (
        jax.ShapeDtypeStruct((2, KV_HEADS, HEAD_DIM, GROUP * rows), F32),
        jax.ShapeDtypeStruct((blocks // 2,) + wide, own_type),
        jax.ShapeDtypeStruct(wide, BF16),
        jax.ShapeDtypeStruct(wide, BF16),
    )
    return pl.pallas_call(
        functools.partial(backward_kernel, stage, first, own_type),
        out_shape=out_shape,
        grid=(1,),
        in_specs=[SM] + wholes(*given[1:]),
        out_specs=wholes(*out_shape),
        scratch_shapes=[
            pltpu.VMEM((blocks,) + wide, BF16),
            pltpu.VMEM((rows, rows), F32),
            pltpu.VMEM((blocks,) + wide, F32),
        ],
        input_output_aliases={} if first else {len(given) - 1: 0},
        compiler_params=LIMIT,
        cost_estimate=takes((12, 14)[stage] if stage < 2 else 4),
    )(*given)


def load_parts(sc, at, pieces, full, sems, dim):
    size = pieces[0].shape[dim]
    copies = []
    for i, piece in enumerate(pieces):
        if len(pieces) == 1:
            to = full
        elif dim == 0:
            to = full.at[pl.ds(pl.multiple_of(sc[at + i] * size, 16), size)]
        else:
            to = full.at[:, pl.ds(pl.multiple_of(sc[at + i] * size, 128), size)]
        copies.append(pltpu.make_async_copy(piece, to, sems.at[i]))
    for copy in copies:
        copy.start()
    return copies


def norm_scale(v):
    return lax.rsqrt(jnp.mean(v * v, axis=0, keepdims=True) + EPSILON)


def prepare_kernel(sc, tokens, positions, first, second):
    width, count = tokens.shape
    rows = count // 2
    p = positions[:, pl.ds(pl.multiple_of(sc[0], 128), count)]
    row = lax.broadcasted_iota(jnp.int32, (16, count), 0)
    p = jnp.where(row == 0, p >> 6, jnp.where(row == 1, p & 63, 0)).astype(F32).astype(BF16)
    for parity in range(2):

        @pl.when(sc[1] == parity)
        def _(parity=parity):
            for half, out in enumerate((first, second)):
                half = half ^ parity
                out[:width] = tokens[:, half * rows : (half + 1) * rows]
                out[width:] = p[:, half * rows : (half + 1) * rows]


def prepare(at, h, tokens, positions):
    width, count = tokens.shape
    out = jax.ShapeDtypeStruct((width + 16, count // 2), BF16)
    sc = jnp.stack([at, lax.rem(h, 2)]).astype(jnp.int32)
    return pl.pallas_call(
        prepare_kernel,
        out_shape=(out, out),
        grid=(1,),
        in_specs=[SM] + wholes(tokens, positions),
        out_specs=wholes(out, out),
        compiler_params=LIMIT,
        cost_estimate=takes(2),
    )(sc, tokens, positions)


def project_kernel(pieces, *refs):
    sc, xa, xb, cos, sin = refs[:5]
    parts = refs[5 : 5 + pieces]
    qz, kv, normed_t, gains, pos, ids, full, sems = refs[5 + pieces :]
    copies = load_parts(sc, 3, parts, full, sems, 0)
    rows = xa.shape[-1]
    width = full.shape[0]
    for q, x in enumerate((xa, xb)):
        p = x[width : width + 16].astype(F32)
        p = p[0:1] * 64.0 + p[1:2]
        pos[q] = p.astype(jnp.int32)
        block = sc[2] + (sc[0] if q == 0 else 3 - sc[0])
        lane = lax.broadcasted_iota(jnp.int32, (1, rows), 1).astype(F32)
        begin = block * rows + jnp.min(lane - p).astype(jnp.int32)
        ids[q] = block
        ids[2 + q] = lax.div(begin, rows)
    ids[4] = sc[2]
    ids[5] = sc[0]
    flat = [x[:width].astype(F32) for x in (xa, xb)]
    scaled = [v * norm_scale(v) for v in flat]
    for copy in copies:
        copy.wait()
    gains[...] = full[:, width + 320 : width + 448]
    gain = full[:, width + 384 : width + 385].astype(F32)
    half = HEAD_DIM // 2
    for q in range(2):
        normed = (scaled[q] * gain).astype(BF16)
        at = slice(q * rows, (q + 1) * rows)
        normed_t[:, at] = normed
        made = jnp.dot(normed.T, full[:, : width + 384], preferred_element_type=F32).T
        c, s = cos[:, at], sin[:, at]
        for h in range(HEADS):
            a = made[64 * h : 64 * h + half]
            b = made[64 * h + half : 64 * h + 64]
            ra = (a * c - b * s).astype(BF16) * jnp.asarray(HEAD_DIM**-0.5, BF16)
            rb = (b * c + a * s).astype(BF16) * jnp.asarray(HEAD_DIM**-0.5, BF16)
            group, lanes = h // GROUP, slice(h % GROUP * rows, (h % GROUP + 1) * rows)
            qz[q, group, :half, lanes] = ra
            qz[q, group, half : 2 * half, lanes] = rb
            qz[q, group, 2 * half :, lanes] = jnp.zeros((2 * half, rows), BF16)
        for k in range(KV_HEADS):
            row = width + 64 * k
            a = made[row : row + half]
            b = made[row + half : row + 64]
            ra = (a * c - b * s).astype(BF16)
            rb = (b * c + a * s).astype(BF16)
            v = made[row + 192 : row + 256].astype(BF16)
            kv[q, k] = jnp.concatenate([ra, rb, v], axis=0).T


def project(sc, xs, cos, sin, parts):
    rows = xs[0].shape[1]
    count = 2 * rows
    width = HEADS * HEAD_DIM
    out_shape = (
        jax.ShapeDtypeStruct((2, KV_HEADS, 2 * HEAD_DIM, GROUP * rows), BF16),
        jax.ShapeDtypeStruct((2, KV_HEADS, rows, 2 * HEAD_DIM), BF16),
        jax.ShapeDtypeStruct((width, count), BF16),
        jax.ShapeDtypeStruct((width, 128), BF16),
        jax.ShapeDtypeStruct((2, 1, rows), jnp.int32),
        jax.ShapeDtypeStruct((8,), jnp.int32),
    )
    return pl.pallas_call(
        functools.partial(project_kernel, len(parts)),
        out_shape=out_shape,
        grid=(1,),
        in_specs=[SM] + wholes(*xs, cos, sin) + [HB] * len(parts),
        out_specs=wholes(*out_shape[:-1]) + [SM],
        scratch_shapes=[
            pltpu.VMEM((width, parts[0].shape[1]), BF16),
            pltpu.SemaphoreType.DMA((len(parts),)),
        ],
        compiler_params=LIMIT,
        cost_estimate=takes(5),
    )(sc, *xs, cos, sin, *parts)


def wide(value):
    over = -value.shape[1] % 128
    if not over:
        return value
    return jnp.concatenate([value, jnp.zeros((value.shape[0], over), value.dtype)], axis=1)


def slot_of(sc, fsdp, f):
    ys = fsdp // 2
    return lax.rem(f + sc[0], 2), lax.rem(lax.div(f, 2) - sc[1] + ys, ys)


def put_slabs(packed, sc, fsdp, at, value):
    value = wide(value).astype(BF16)
    r = value.shape[0] // fsdp
    for f in range(fsdp):
        k, y = slot_of(sc, fsdp, f)
        for s in range(value.shape[1] // 128):
            packed[k, y, pl.ds(at + s * r, r)] = value[
                f * r : (f + 1) * r, s * 128 : (s + 1) * 128
            ]


def norm_back(v, gain, grad):
    r = norm_scale(v)
    scaled = grad * gain
    d_v = r * scaled - v * (r * r * r * jnp.mean(scaled * v, axis=0, keepdims=True))
    return d_v, jnp.sum(grad * (v * r), axis=1, keepdims=True)


def feed_kernel(fsdp, pieces, chunk, *refs):
    sc, xa, xb, ca, cb, mix, gains = refs[:7]
    parts = refs[7 : 7 + pieces]
    downs = refs[7 + pieces : 7 + 2 * pieces]
    refs = refs[7 + 2 * pieces :]
    res_a, res_b, d_middle, gz, delta, mine, give, second = refs[:8]
    full, out_w, down, packed, att_t, mid, n2, n2_t, res, d_second, cot_t, cot = refs[8:20]
    sems, out_sems, down_sems, grad_sems = refs[20:]
    ff = down.shape[1]
    out_copies = load_parts(sc, 3, [p.at[:, 2 * ff :] for p in parts], out_w, out_sems, 0)
    copies = load_parts(sc, 3, [p.at[:, : 2 * ff] for p in parts], full, sems, 0)
    down_copies = load_parts(sc, 3, downs, down, down_sems, 1)
    rows = xa.shape[-1]
    width, ff = down.shape
    shard = width // fsdp
    down_shard = ff // fsdp
    for q, c in enumerate((ca, cb)):
        cot_t[:, q * rows : (q + 1) * rows] = c[...]
        for h in range(HEADS):
            att_t[64 * h : 64 * h + 64, q * rows : (q + 1) * rows] = mix[
                q, h // GROUP, :, h % GROUP * rows : (h % GROUP + 1) * rows
            ]
    cot[...] = cot_t[...].T
    gain = gains[:, 65:66].astype(F32)
    for copy in out_copies:
        copy.wait()
    branch_t = jnp.dot(out_w[...].T, att_t[...], preferred_element_type=F32)
    for q, x in enumerate((xa, xb)):
        at = slice(q * rows, (q + 1) * rows)
        mid[:, at] = x[:width].astype(F32) + branch_t[:, at]
    n2_t[...] = (mid[...] * norm_scale(mid[...]) * gain).astype(BF16)
    n2[...] = n2_t[...].T
    res[...] = mid[...]
    d_second[...] = jnp.zeros(d_second.shape, F32)
    for copy in copies + down_copies:
        copy.wait()
    up_at = ff // 128 * shard
    out_at = 2 * up_at
    down_at = out_at + -(-width // 128) * shard
    used = down_at + -(-down_shard // 128) * width
    rows_all = packed.shape[2]
    if rows_all > used:
        packed[:, :, used:] = jnp.zeros((2, fsdp // 2, rows_all - used, 128), BF16)

    sends = []

    def send(at, n):
        for k, to in enumerate((mine, give)):
            span = pl.ds(at, n)
            copy = pltpu.make_async_copy(
                packed.at[k, :, span], to.at[:, span], grad_sems.at[len(sends)]
            )
            copy.start()
            sends.append(copy)

    for j in range(ff // chunk):
        cols = slice(j * chunk, (j + 1) * chunk)
        up_cols = slice(ff + j * chunk, ff + (j + 1) * chunk)
        gate_w, up_w, down_w = full[:, cols], full[:, up_cols], down[:, cols]
        gate = jnp.dot(n2[...], gate_w, preferred_element_type=F32)
        up = jnp.dot(n2[...], up_w, preferred_element_type=F32)
        sig = 1.0 / (1.0 + jnp.exp(-gate))
        silu = gate * sig
        hidden = (silu * up).astype(BF16)
        res[...] += dot(down_w, hidden, 1, 1)
        d_hidden = jnp.dot(cot[...], down_w, preferred_element_type=F32)
        d_gate = (d_hidden * up * (sig * (1.0 + gate * (1.0 - sig)))).astype(BF16)
        d_up = (d_hidden * silu).astype(BF16)
        d_second[...] += dot(gate_w, d_gate, 1, 1) + dot(up_w, d_up, 1, 1)
        slab = j * (chunk // 128) * shard
        put_slabs(packed, sc, fsdp, slab, jnp.dot(n2_t[...], d_gate, preferred_element_type=F32))
        put_slabs(
            packed, sc, fsdp, up_at + slab, jnp.dot(n2_t[...], d_up, preferred_element_type=F32)
        )
        down_g = jnp.dot(cot_t[...], hidden, preferred_element_type=F32).astype(BF16)
        if down_shard % 128:
            for n in range(chunk // down_shard):
                slot_k, slot_y = slot_of(sc, fsdp, j * (chunk // down_shard) + n)
                part = wide(down_g[:, n * down_shard : (n + 1) * down_shard])
                for s in range(part.shape[1] // 128):
                    packed[slot_k, slot_y, down_at + s * width : down_at + (s + 1) * width] = part[
                        :, s * 128 : (s + 1) * 128
                    ]
        else:
            for n in range(chunk // 128):
                slab = j * (chunk // 128) + n
                slot_k, slot_y = slot_of(sc, fsdp, slab // (down_shard // 128))
                at = down_at + slab % (down_shard // 128) * width
                packed[slot_k, slot_y, at : at + width] = down_g[:, n * 128 : (n + 1) * 128]
        send(j * (chunk // 128) * shard, chunk // 128 * shard)
        send(up_at + j * (chunk // 128) * shard, chunk // 128 * shard)

    send(down_at, rows_all - down_at)
    res_a[...] = res[:, :rows].astype(BF16)
    res_b[...] = res[:, rows:].astype(BF16)
    d_v, gain_grad = norm_back(mid[...], gain, d_second[...])
    second[...] = jnp.broadcast_to(gain_grad, second.shape)
    d_mid = cot_t[...].astype(F32) + d_v
    d_middle[...] = d_mid
    branch = d_mid.astype(BF16)
    put_slabs(packed, sc, fsdp, out_at, dot(att_t[...], branch, 1, 1))
    send(out_at, down_at - out_at)
    d_mix = jnp.dot(out_w[...], branch, preferred_element_type=F32).astype(BF16)
    for q in range(2):
        for h in range(HEADS):
            at = slice(q * rows, (q + 1) * rows)
            part = d_mix[64 * h : 64 * h + 64, at]
            group, lanes = h // GROUP, slice(h % GROUP * rows, (h % GROUP + 1) * rows)
            gz[q, group, :64, lanes] = jnp.zeros((64, rows), BF16)
            gz[q, group, 64:, lanes] = part
            delta[q, group, :, lanes] = jnp.sum(
                part.astype(F32) * att_t[64 * h : 64 * h + 64, at].astype(F32),
                axis=0,
                keepdims=True,
            )
    for copy in sends:
        copy.wait()


def feed_rows(fsdp, ctx, width, ff):
    used = (2 * (ff // 128) + -(-width // 128)) * (width // fsdp) + -(-(ff // fsdp) // 128) * width
    return -(-used // (16 * ctx)) * 16 * ctx


def feed(fsdp, ctx, sc, xs, cots, mix, gains, parts, downs):
    rows = cots[0].shape[1]
    width = cots[0].shape[0]
    count = 2 * rows
    ff = downs[0].shape[1] * len(downs)
    packed = (fsdp // 2, feed_rows(fsdp, ctx, width, ff), 128)
    out_shape = (
        jax.ShapeDtypeStruct((width, rows), BF16),
        jax.ShapeDtypeStruct((width, rows), BF16),
        jax.ShapeDtypeStruct((width, count), F32),
        jax.ShapeDtypeStruct((2, KV_HEADS, 2 * HEAD_DIM, GROUP * rows), BF16),
        jax.ShapeDtypeStruct((2, KV_HEADS, 1, GROUP * rows), F32),
        jax.ShapeDtypeStruct(packed, BF16),
        jax.ShapeDtypeStruct(packed, BF16),
        jax.ShapeDtypeStruct((width, 128), F32),
    )
    return pl.pallas_call(
        functools.partial(feed_kernel, fsdp, len(parts), ff // 4 if ff // fsdp % 128 else ff // 3),
        out_shape=out_shape,
        grid=(1,),
        in_specs=[SM] + wholes(*xs, *cots, mix, gains) + [HB] * (2 * len(parts)),
        out_specs=wholes(*out_shape[:5]) + [HB, HB] + wholes(out_shape[7]),
        scratch_shapes=[
            pltpu.VMEM((width, 2 * ff), BF16),
            pltpu.VMEM((width, width), BF16),
            pltpu.VMEM((width, ff), BF16),
            pltpu.VMEM((2,) + packed, BF16),
            pltpu.VMEM((width, count), BF16),
            pltpu.VMEM((width, count), F32),
            pltpu.VMEM((count, width), BF16),
            pltpu.VMEM((width, count), BF16),
            pltpu.VMEM((width, count), F32),
            pltpu.VMEM((width, count), F32),
            pltpu.VMEM((width, count), BF16),
            pltpu.VMEM((count, width), BF16),
            pltpu.SemaphoreType.DMA((len(parts),)),
            pltpu.SemaphoreType.DMA((len(parts),)),
            pltpu.SemaphoreType.DMA((len(parts),)),
            pltpu.SemaphoreType.DMA((24,)),
        ],
        compiler_params=LIMIT,
        cost_estimate=takes(19),
    )(sc, *xs, *cots, mix, gains, *parts, *downs)


def last_kernel(fsdp, pieces, chain, *refs):
    sc, xa, xb, cos, sin, normed_t, gains, second, d_middle, dq, own, *twin = refs[:13]
    refs = refs[13:]
    if chain:
        came = refs[0]
        refs = refs[1:]
    parts = refs[:pieces]
    grad_a, grad_b, mine, give, full, packed, made, sems = refs[pieces:]
    copies = load_parts(sc, 3, parts, full, sems, 0)
    rows = xa.shape[-1]
    width = full.shape[0]
    half = HEAD_DIM // 2
    for q in range(2):
        at = slice(q * rows, (q + 1) * rows)
        c, s = cos[:, at], sin[:, at]
        for h in range(HEADS):
            group, lanes = h // GROUP, slice(h % GROUP * rows, (h % GROUP + 1) * rows)
            a = dq[q, group, :half, lanes] * HEAD_DIM**-0.5
            b = dq[q, group, half:, lanes] * HEAD_DIM**-0.5
            made[64 * h : 64 * h + half, at] = (a * c + b * s).astype(BF16)
            made[64 * h + half : 64 * h + 64, at] = (b * c - a * s).astype(BF16)
        for k in range(KV_HEADS):
            both = own[q, k] + twin[q][k].astype(F32)
            if chain:
                both = both + came[q, k].astype(F32)
            both = both.T
            a, b = both[:half], both[half : 2 * half]
            row = width + 64 * k
            made[row : row + half, at] = (a * c + b * s).astype(BF16)
            made[row + half : row + 64, at] = (b * c - a * s).astype(BF16)
            made[row + 192 : row + 256, at] = both[2 * half :].astype(BF16)
    for copy in copies:
        copy.wait()
    gain = gains[:, 64:65].astype(F32)
    d_first = jnp.dot(full[:, : width + 384], made[...], preferred_element_type=F32)
    v = jnp.concatenate([xa[:width], xb[:width]], axis=1).astype(F32)
    d_v, first = norm_back(v, gain, d_first)
    d_x = (d_middle[...] + d_v).astype(BF16)
    grad_a[...] = d_x[:, :rows]
    grad_b[...] = d_x[:, rows:]
    front = dot(normed_t[...], made[...], 1, 1)
    lane = lax.broadcasted_iota(jnp.int32, (width, 64), 1)
    ends = jnp.where(lane == 0, first, second[:, :64])
    put_slabs(packed, sc, fsdp, 0, jnp.concatenate([front, ends], axis=1))
    used = (width + 448) // 128 * (width // fsdp)
    total = packed.shape[2]
    if total > used:
        packed[:, :, used:] = jnp.zeros((2, fsdp // 2, total - used, 128), BF16)
    mine[...] = packed[0]
    give[...] = packed[1]


def last(fsdp, ctx, sc, xs, cos, sin, normed_t, gains, second, d_middle, dq, dkv, parts):
    width, count = normed_t.shape
    rows = count // 2
    used = (width + 448) // 128 * (width // fsdp)
    packed = (fsdp // 2, -(-used // (16 * ctx)) * 16 * ctx, 128)
    given = (*xs, cos, sin, normed_t, gains, second, d_middle, dq, *dkv)
    out_shape = (
        jax.ShapeDtypeStruct((width, rows), BF16),
        jax.ShapeDtypeStruct((width, rows), BF16),
        jax.ShapeDtypeStruct(packed, BF16),
        jax.ShapeDtypeStruct(packed, BF16),
    )
    return pl.pallas_call(
        functools.partial(last_kernel, fsdp, len(parts), len(dkv) == 4),
        out_shape=out_shape,
        grid=(1,),
        in_specs=[SM] + wholes(*given) + [HB] * len(parts),
        out_specs=wholes(*out_shape),
        scratch_shapes=[
            pltpu.VMEM((width, parts[0].shape[1]), BF16),
            pltpu.VMEM((2,) + packed, BF16),
            pltpu.VMEM((width + 384, count), BF16),
            pltpu.SemaphoreType.DMA((len(parts),)),
        ],
        compiler_params=LIMIT,
        cost_estimate=takes(0),
    )(sc, *given, *parts)


def unpack_kernel(places, flat, *outs):
    for out, (at, rows, skip) in zip(outs, places, strict=True):
        columns = out.shape[1]
        done = 0
        while done < columns:
            slab, lane = divmod(skip + done, 128)
            n = min(128 - lane, columns - done)
            out[:, done : done + n] = flat[
                at + slab * rows : at + (slab + 1) * rows, lane : lane + n
            ].astype(F32)
            done += n


def join_unpack_kernel(places, sc, near, far, *refs):
    *outs, flat = refs
    part = near.shape[0] // 2
    for half in range(2):
        for x in range(2):
            piece = near if x == 0 else far
            at = pl.multiple_of(part * (2 * half + lax.rem(sc[0] + x, 2)), 16)
            flat[pl.ds(at, part)] = piece[half * part : (half + 1) * part]
    unpack_kernel(places, flat, *outs)


def unpack(flat, places):
    out_shape = tuple(jax.ShapeDtypeStruct((p[1], p[3]), F32) for p in places)
    return pl.pallas_call(
        functools.partial(unpack_kernel, [p[:3] for p in places]),
        out_shape=out_shape,
        grid=(1,),
        in_specs=wholes(flat),
        out_specs=wholes(*out_shape),
        compiler_params=LIMIT,
        cost_estimate=takes(2),
    )(flat)


def join_unpack(x, near, far, places):
    out_shape = tuple(jax.ShapeDtypeStruct((p[1], p[3]), F32) for p in places)
    return pl.pallas_call(
        functools.partial(join_unpack_kernel, [p[:3] for p in places]),
        out_shape=out_shape,
        grid=(1,),
        in_specs=[SM] + wholes(near, far),
        out_specs=wholes(*out_shape),
        scratch_shapes=[pltpu.VMEM((2 * near.shape[0], 128), BF16)],
        compiler_params=LIMIT,
        cost_estimate=takes(3),
    )(x, near, far)


def chip_sum(mine, got, i):
    return mine[i].astype(F32) + got[i].astype(F32)


def sum_y(mine, got, send):
    total = chip_sum(mine, got, 0)
    for s in range(1, mine.shape[0]):
        total = total + send["shift"][s](chip_sum(mine, got, s).astype(BF16)).astype(F32)
    return total.astype(BF16)


def spread_kernel(got, out):
    total = got[0].astype(F32)
    for i in range(1, got.shape[0]):
        total = total + got[i].astype(F32)
    total = total.astype(BF16)
    for i in range(got.shape[0]):
        out[i] = total


def simple_call(kernel, out_shape, *given):
    return pl.pallas_call(
        kernel,
        out_shape=out_shape,
        grid=(1,),
        in_specs=wholes(*given),
        out_specs=whole(out_shape),
        compiler_params=LIMIT,
        cost_estimate=takes(0),
    )(*given)


def exchange(total, axes, size):
    parts = total.reshape(size, total.shape[0] // size, 128)
    return lax.all_to_all(parts, axes, 0, 0, tiled=True)


def spread(got):
    return simple_call(spread_kernel, jax.ShapeDtypeStruct(got.shape, BF16), got)


def gather_over(spread, axes):
    return lax.all_to_all(spread, axes, 0, 0, tiled=True).reshape(-1, 128)


def came_kernel(own, twin_a, twin_b, *refs):
    *came, out = refs
    for i, twin in enumerate((twin_a, twin_b)):
        total = own[i].astype(F32) + twin[...].astype(F32)
        for c in came:
            total = total + c[i].astype(F32)
        out[i] = total.astype(BF16)


def halves_kernel(one, one_came, two, two_came, out):
    n = one.shape[0]
    out[:n] = (one[...].astype(F32) + one_came[...].astype(F32)).astype(BF16)
    out[n:] = (two[...].astype(F32) + two_came[...].astype(F32)).astype(BF16)


def first_kernel(x, *refs):
    mine, got, (to_y, to_x) = refs[:4], refs[4:8], refs[8:]
    for i in range(4):
        out = to_y if i < 2 else to_x
        out[i % 2] = (mine[i][0].astype(F32) + got[i][0].astype(F32)).astype(BF16)


def first_sums(x, mine, got):
    n = mine.shape[1] // 4
    block = (1, n, 128)
    places = [
        lambda i, x: (1, 0, 0),
        lambda i, x: (1, 1, 0),
        lambda i, x: (0, 3 - x[0], 0),
        lambda i, x: (1, 3 - x[0], 0),
    ]
    out = pl.BlockSpec((2, n, 128), lambda i, x: (0, 0, 0))
    return pl.pallas_call(
        first_kernel,
        out_shape=(jax.ShapeDtypeStruct((2, n, 128), BF16),) * 2,
        grid_spec=pltpu.PrefetchScalarGridSpec(
            num_scalar_prefetch=1,
            grid=(1,),
            in_specs=[pl.BlockSpec(block, at) for at in places] * 2,
            out_specs=[out, out],
        ),
        compiler_params=LIMIT,
        cost_estimate=takes(0),
    )(x, *[mine] * 4, *[got] * 4)


def second_kernel(x, *refs):
    mine, got, came, outs = refs[:4], refs[4:8], refs[8:12], refs[12:]
    for i in range(4):
        total = mine[i][0].astype(F32) + got[i][0].astype(F32) + came[i][0].astype(F32)
        outs[i][...] = total.astype(BF16)


def second_sums(x, mine, got, came_y, came_x):
    n = mine.shape[1] // 4
    block = (1, n, 128)
    own = [
        lambda i, x: (0, 1 - x[0], 0),
        lambda i, x: (0, x[0], 0),
        lambda i, x: (1, 2 + x[0], 0),
        lambda i, x: (0, 2 + x[0], 0),
    ]
    came = [
        lambda i, x: (1 - x[0], 0, 0),
        lambda i, x: (x[0], 0, 0),
        lambda i, x: (1, 0, 0),
        lambda i, x: (0, 0, 0),
    ]
    return pl.pallas_call(
        second_kernel,
        out_shape=(jax.ShapeDtypeStruct((n, 128), BF16),) * 4,
        grid_spec=pltpu.PrefetchScalarGridSpec(
            num_scalar_prefetch=1,
            grid=(1,),
            in_specs=[pl.BlockSpec(block, at) for at in own + own + came],
            out_specs=[pl.BlockSpec((n, 128), lambda i, x: (0, 0))] * 4,
        ),
        compiler_params=LIMIT,
        cost_estimate=takes(0),
    )(x, *[mine] * 4, *[got] * 4, came_y, came_y, came_x, came_x)


def gather_y(own, send, fsdp):
    return [own] + [send["shift"][s](own) for s in range(1, fsdp // 2)]


def gather_pieces(got, send, fsdp, core, y, join, dim):
    pieces = got + [send["core"](g) for g in got]
    own = got[0]
    if not join:
        return pieces
    buffer = jnp.zeros((fsdp,) + own.shape, own.dtype)
    for piece, f in zip(pieces, piece_order(fsdp, core, y), strict=True):
        buffer = lax.dynamic_update_index_in_dim(buffer, piece, f, 0)
    if dim:
        buffer = buffer.swapaxes(0, 1)
        return [buffer.reshape(own.shape[0], fsdp * own.shape[1])]
    return [buffer.reshape(fsdp * own.shape[0], own.shape[1])]


def piece_order(fsdp, core, y):
    ys = fsdp // 2
    source = [lax.rem(y - s + ys, ys) * 2 for s in range(ys)]
    return [f + core for f in source] + [f + 1 - core for f in source]


def body(
    fsdp,
    ctx,
    tokens,
    segment_ids,
    positions,
    cotangent,
    norm_first,
    query_weight,
    key_weight,
    value_weight,
    output_weight,
    norm_second,
    gate_weight,
    up_weight,
    down_weight,
):
    send = make_send(fsdp, ctx)
    ys, hs = fsdp // 2, ctx // 2
    _, count, width = tokens.shape
    rows = count // 2
    kv_width = KV_HEADS * HEAD_DIM
    y, core = lax.axis_index("y"), lax.axis_index("core")
    h, x = lax.axis_index("h"), lax.axis_index("x")
    ci = 2 * h + x
    reach = min(hs - 1, -(-(-(-(DOC_MOST - 1) // rows)) // 4))
    order = jnp.stack([core, y, 4 * h] + piece_order(fsdp, core, y)).astype(jnp.int32)
    shard = gate_weight.shape[0]
    join = shard % 16 != 0
    x_pair = prepare(2 * count * h + count * x, h, tokens.reshape(count, width).T, positions)
    *pair, query_weight, norm_first, norm_second = tie(
        *x_pair, query_weight, norm_first, norm_second
    )
    xs = send_home(send, pair)
    packed = jnp.concatenate(
        [
            query_weight,
            key_weight,
            value_weight,
            norm_first[:, None],
            norm_second[:, None],
            jnp.zeros((shard, 62), BF16),
        ],
        axis=1,
    )
    first_parts = gather_y(packed, send, fsdp)
    first_parts = gather_pieces(first_parts, send, fsdp, core, y, join, 0)
    cot_t, _ = tie(cotangent.reshape(count, width).T, first_parts[-1])
    cots = send_home(send, pick_home(cot_t, h))
    pos_f = jnp.concatenate([a[width : width + 2] for a in xs], axis=1).astype(F32)
    pos_f = pos_f[0:1] * 64.0 + pos_f[1:2]
    frequency = jnp.exp(
        jnp.arange(HEAD_DIM // 2, dtype=F32) * (-math.log(10000.0) * 2.0 / HEAD_DIM)
    )
    angle = frequency[:, None] * pos_f
    cos, sin = jnp.cos(angle), jnp.sin(angle)
    qz, kv, normed_t, gains, pos, ids = project(order, xs, cos, sin, first_parts)

    feed_own = jnp.concatenate([gate_weight, up_weight, output_weight], axis=1)
    feed_own, down_own, _ = tie(feed_own, down_weight.T, first_parts[-1])
    feed_got = gather_y(feed_own, send, fsdp)
    down_got = gather_y(down_own, send, fsdp)
    stages = []
    carried = None
    for s in range(reach + 1):
        stages.append((kv, send["core"](kv)))
        if s < reach:
            kv = send["up"](kv)
        carried = attend_forward(s, ids, pos, qz, stages[s], carried, s == reach)
        if s < reach:
            kv, *carried = tie(kv, *carried)
    mixed, lse = carried
    feed_parts = gather_pieces(feed_got, send, fsdp, core, y, join, 0)
    down_parts = gather_pieces(down_got, send, fsdp, core, y, join, 1)
    res_a, res_b, d_middle, gz, delta, mine, give, second = feed(
        fsdp, ctx, order, xs, cots, mixed, gains, feed_parts, down_parts
    )

    crossed = ys == 2
    x_ref = x.astype(jnp.int32).reshape(1)
    dq = None
    came = None
    for s in range(reach, -1, -1):
        sc = ids
        if s == reach - 1:
            give, dq = tie(give, dq)
            got = send["core"](give)
        if s == reach - 1 and crossed:
            first_y, first_x = first_sums(x_ref, mine, got)
            sc, first_y, first_x = tie(sc, first_y, first_x)
            came_y, came_x = send["shift"][1](first_y), send["across"](first_x)
        if s == 0 and crossed:
            came_y, came_x, dq = tie(came_y, came_x, dq)
            give_one, keep_one, give_two, keep_two = second_sums(x_ref, mine, got, came_y, came_x)
            sc, give_one, give_two = tie(sc, give_one, give_two)
            came_one, came_two = send["across"](give_one), send["shift"][1](give_two)
        if came is not None:
            sc, came = tie(sc, came)
            came = send["down"](came)
        dq, own, *other = attend_backward(
            s, sc, pos, qz, gz, lse, delta, stages[s], dq, F32 if s == 0 else BF16
        )
        twin = tuple(send["core"](o) for o in other)
        if s > 0:
            if s == reach - 1:
                *twin, came, dq, res_a, res_b = tie(*twin, came, dq, *result)
            elif s < reach:
                *twin, came, dq = tie(*twin, came, dq)
            given = (own, *twin) if came is None else (own, *twin, came)
            came = simple_call(came_kernel, jax.ShapeDtypeStruct(own.shape, BF16), *given)
            if s == reach:
                came, res_a, res_b = tie(came, res_a, res_b)
                result = send_back(send, res_a, res_b)
    dkv = (own, *twin) if came is None else (own, *twin, came)
    if crossed:
        late = simple_call(
            halves_kernel,
            jax.ShapeDtypeStruct((mine.shape[1] // 2, 128), BF16),
            keep_one,
            came_one,
            keep_two,
            came_two,
        )
        late = exchange(late, ("h",), hs)
    else:
        late = exchange(sum_y(mine, got, send), CTX, ctx)
    late, dq = tie(spread(late), dq)
    late = gather_over(late, ("h",) if crossed else CTX)
    tok_a, tok_b, mine_front, give_front = last(
        fsdp, ctx, order, xs, cos, sin, normed_t, gains, second, d_middle, dq, dkv, first_parts
    )
    got_front = send["core"](give_front)
    front = sum_y(mine_front, got_front, send)
    front, late, tok_a, tok_b = tie(front, late, tok_a, tok_b)
    front = spread(exchange(front, CTX, ctx))
    if crossed:
        late_far = send["across"](late)
    front = gather_over(front, CTX)
    tokens_grad = send_back(send, tok_a, tok_b)

    ff = gate_weight.shape[1]
    down_shard = down_weight.shape[0]
    gate_rows, out_rows = ff // 128 * shard, -(-width // 128) * shard
    places = [
        (0, shard, 0, ff),
        (gate_rows, shard, 0, ff),
        (2 * gate_rows, shard, 0, width),
        (2 * gate_rows + out_rows, width, 0, down_shard),
    ]
    if crossed:
        late_grads = join_unpack(x_ref, late, late_far, places)
    else:
        late_grads = unpack(late, places)
    gate_grad, up_grad, output_grad, down_grad = late_grads
    query_grad, key_grad, value_grad, ends = unpack(
        front,
        [
            (0, shard, 0, width),
            (0, shard, width, kv_width),
            (0, shard, width + kv_width, kv_width),
            (0, shard, width + 2 * kv_width, 64),
        ],
    )
    return (
        low_high(res_a, res_b, h).T[None],
        low_high(*tokens_grad, h).T[None],
        ends[:, 0],
        query_grad,
        key_grad,
        value_grad,
        output_grad,
        ends[:, 1],
        gate_grad,
        up_grad,
        down_grad.T,
    )


def solution(mesh):
    fsdp, ctx = mesh.shape["fsdp"], mesh.shape["ctx"]
    places = Mesh(mesh.devices.reshape(fsdp // 2, 2, ctx // 2, 2), AXES)
    owner = ("y", "core")
    flat, split = P(owner), P(owner, None)
    whole = P(owner, CTX, None)
    return jax.shard_map(
        functools.partial(body, fsdp, ctx),
        mesh=places,
        in_specs=(whole, split, split, whole, flat, split, split, split, split, flat, split, split, split),
        out_specs=(whole, whole, flat, split, split, split, split, flat, split, split, split),
        check_vma=False,
    )
```

```python
import functools
import math

import jax
import jax.numpy as jnp
from jax import lax
from jax.experimental import pallas as pl
from jax.experimental.pallas import tpu as pltpu
from jax.sharding import Mesh
from jax.sharding import PartitionSpec as P

HEADS = 9
KV_HEADS = 3
GROUP = HEADS // KV_HEADS
HEAD_DIM = 64
EPSILON = 1e-05
MASKED = -1e30
DOC_MOST = 2000
AXES = ("y", "core", "h", "x")
CTX = ("h", "x")
F32 = jnp.float32
BF16 = jnp.bfloat16


def moves(fsdp, ctx, step):
    pairs = []
    for f in range(fsdp):
        for c in range(ctx):
            to = step(f // 2, f % 2, c // 2, c % 2)
            if to is not None:
                y, core, h, x = to
                pairs.append((f * ctx + c, (2 * y + core) * ctx + 2 * h + x))
    return pairs


def make_send(fsdp, ctx):
    ys, hs, blocks = fsdp // 2, ctx // 2, 2 * ctx

    def along(pairs):
        return lambda a: lax.ppermute(a, AXES, pairs)

    def by(step):
        return along(moves(fsdp, ctx, step))

    def home(slot):
        def step(y, core, h, x):
            low = 2 * h + x
            block = low if h % 2 == slot else blocks - 1 - low
            return (y, int(block % 4 in (1, 2)), block // 4, core)

        return moves(fsdp, ctx, step)

    def back(pairs):
        return along([(b, a) for a, b in pairs])

    return dict(
        home=[along(home(0)), along(home(1))],
        back=[back(home(0)), back(home(1))],
        core=by(lambda y, k, h, x: (y, 1 - k, h, x)),
        across=by(lambda y, k, h, x: (y, k, h, 1 - x)),
        up=by(lambda y, k, h, x: (y, k, h + 1, x) if h + 1 < hs else None),
        down=by(lambda y, k, h, x: (y, k, h - 1, x) if h > 0 else None),
        around=[by(lambda y, k, h, x, s=s: (y, k, (h + s) % hs, x)) for s in range(hs)],
        shift=[by(lambda y, k, h, x, s=s: ((y + s) % ys, k, h, x)) for s in range(ys)],
    )


def pick_home(a, h):
    r = a.shape[1] // 2
    low, high = a[:, :r], a[:, r:]
    even = lax.rem(h, 2) == 0
    return jnp.where(even, low, high), jnp.where(even, high, low)


def send_home(send, pair):
    return send["home"][0](pair[0]), send["home"][1](pair[1])


def send_back(send, a, b):
    return send["back"][0](a), send["back"][1](b)


def low_high(a, b, h):
    even = lax.rem(h, 2) == 0
    return jnp.concatenate([jnp.where(even, a, b), jnp.where(even, b, a)], axis=1)


def tie(*values):
    return lax.optimization_barrier(values)


def bias_of(begin, place, block_id, keys, rows):
    key_place = block_id * keys + lax.broadcasted_iota(jnp.int32, (keys, rows), 0)
    seen = (key_place >= begin) & (key_place <= place)
    return jnp.where(seen, 0.0, MASKED)


def dot(left, right, left_dim, right_dim):
    return lax.dot_general(
        left, right, (((left_dim,), (right_dim,)), ((), ())), preferred_element_type=F32
    )


def load_blocks(pieces, held):
    held[:2] = pieces[0][...]
    held[2:] = pieces[1][...]


def each_pair(sc, stage, work):
    base, core = sc[4] - 4 * stage, sc[5]

    def step(i, _):
        q = lax.div(i, 4)
        k = lax.rem(i, 4)
        within = jnp.where(k < 2, core, 1 - core)
        block_id = base + jnp.where(lax.rem(k, 2) == 0, within, 3 - within)

        @pl.when((block_id >= sc[2 + q]) & (block_id <= sc[q]))
        def _():
            work(q, k, block_id)

        return 0

    lax.fori_loop(0, 8, step, 0)


def forward_kernel(stage, last, *refs):
    first = stage == 0
    refs = list(refs)
    sc, pos, qz = refs[:3]
    kv = refs[3:5]
    refs = refs[5:]
    if not first:
        peak_in, total_in, mix_in = refs[:3]
        refs = refs[3:]
    if last:
        out, lse = refs[:2]
        held, bias, peak, total, mix = refs[2:]
    else:
        peak, total, mix = refs[:3]
        held, bias = refs[3:]
    rows = pos.shape[-1]
    if first:
        peak[...] = jnp.full(peak.shape, MASKED, F32)
        total[...] = jnp.zeros(total.shape, F32)
        mix[...] = jnp.zeros(mix.shape, F32)
    else:
        peak[...] = peak_in[...]
        total[...] = total_in[...]
        mix[...] = mix_in[...]
    load_blocks(kv, held)

    def work(q, k, block_id):
        place = sc[q] * rows + lax.broadcasted_iota(jnp.int32, (1, rows), 1)
        bias[...] = bias_of(place - pos[q], place, block_id, rows, rows)
        for c in range(KV_HEADS):
            seen = dot(held[k, c], qz[q, c], 1, 0) + jnp.concatenate([bias[...]] * GROUP, axis=1)
            old = peak[q, c]
            new = jnp.maximum(old, jnp.max(seen, axis=0, keepdims=True))
            expo = jnp.exp(seen - new)
            fade = jnp.exp(old - new)
            peak[q, c] = new
            total[q, c] = total[q, c] * fade + jnp.sum(expo, axis=0, keepdims=True)
            values = held[k, c].T[HEAD_DIM:]
            mix[q, c] = mix[q, c] * fade + dot(values, expo.astype(BF16), 1, 0)

    each_pair(sc, stage, work)
    if last:
        lse[...] = peak[...] + jnp.log(total[...])
        for q in range(2):
            for c in range(KV_HEADS):
                out[q, c] = (mix[q, c] / total[q, c]).astype(BF16)


def backward_kernel(stage, first, own_type, *refs):
    refs = list(refs)
    sc, pos, qz, gz, lse, delta = refs[:6]
    kv = refs[6:8]
    refs = refs[8:]
    if not first:
        dq_in = refs[0]
        refs = refs[1:]
    dq, own, other_a, other_b, held, bias, dkv = refs
    rows = pos.shape[-1]
    if first:
        dq[...] = jnp.zeros(dq.shape, F32)
    else:
        dq[...] = dq_in[...]
    load_blocks(kv, held)
    dkv[...] = jnp.zeros(dkv.shape, F32)

    def work(q, k, block_id):
        place = sc[q] * rows + lax.broadcasted_iota(jnp.int32, (1, rows), 1)
        bias[...] = bias_of(place - pos[q], place, block_id, rows, rows)
        scores = [dot(held[k, c], qz[q, c], 1, 0) for c in range(KV_HEADS)]
        for c in range(KV_HEADS):
            seen = scores[c] + jnp.concatenate([bias[...]] * GROUP, axis=1)
            probs = jnp.exp(seen - lse[q, c])
            d_scores = (probs * (dot(held[k, c], gz[q, c], 1, 0) - delta[q, c])).astype(BF16)
            dkv[k, c] += dot(d_scores, qz[q, c], 1, 1) + dot(probs.astype(BF16), gz[q, c], 1, 1)
            dq[q, c] += dot(held[k, c].T[:HEAD_DIM], d_scores, 1, 0)

    each_pair(sc, stage, work)
    own[...] = dkv[:2].astype(own_type)
    other_a[...] = dkv[2].astype(BF16)
    other_b[...] = dkv[3].astype(BF16)


SM = pl.BlockSpec(memory_space=pltpu.SMEM)
HB = pl.BlockSpec(memory_space=pl.ANY)


def whole(a):
    return pl.BlockSpec(
        a.shape, lambda i: (0,) * len(a.shape), pipeline_mode=pl.Buffered(buffer_count=1)
    )


def wholes(*arrays):
    return [whole(a) for a in arrays]


def takes(us):
    return pl.CostEstimate(flops=int(us * 1.15e9), bytes_accessed=0, transcendentals=0)


LIMIT = pltpu.CompilerParams(vmem_limit_bytes=(64 << 20) - (256 << 10))


def attend_forward(stage, sc, pos, qz, pieces, carried, last):
    rows = pos.shape[-1]
    blocks = 4
    first = carried is None
    stat = jax.ShapeDtypeStruct((2, KV_HEADS, 1, GROUP * rows), F32)
    mix = jax.ShapeDtypeStruct((2, KV_HEADS, HEAD_DIM, GROUP * rows), F32)
    scratch = [
        pltpu.VMEM((blocks, KV_HEADS, rows, 2 * HEAD_DIM), BF16),
        pltpu.VMEM((rows, rows), F32),
    ]
    if last:
        out_shape = (jax.ShapeDtypeStruct(mix.shape, BF16), stat)
        scratch += [pltpu.VMEM(s.shape, F32) for s in (stat, stat, mix)]
        aliases = {}
    else:
        out_shape = (stat, stat, mix)
        aliases = {} if first else {3 + len(pieces) + i: i for i in range(3)}
    given = (sc, pos, qz, *pieces) + (() if first else tuple(carried))
    pairs = blocks * HEADS * rows * rows
    return pl.pallas_call(
        functools.partial(forward_kernel, stage, last),
        out_shape=out_shape,
        grid=(1,),
        in_specs=[SM] + wholes(*given[1:]),
        out_specs=wholes(*out_shape),
        scratch_shapes=scratch,
        input_output_aliases=aliases,
        compiler_params=LIMIT,
        cost_estimate=takes(0),
    )(*given)


def attend_backward(stage, sc, pos, qz, gz, lse, delta, pieces, dq, own_type):
    rows = pos.shape[-1]
    blocks = 4
    first = dq is None
    wide = (KV_HEADS, rows, 2 * HEAD_DIM)
    given = (sc, pos, qz, gz, lse, delta, *pieces) + (() if first else (dq,))
    pairs = blocks * HEADS * rows * rows
    out_shape = (
        jax.ShapeDtypeStruct((2, KV_HEADS, HEAD_DIM, GROUP * rows), F32),
        jax.ShapeDtypeStruct((blocks // 2,) + wide, own_type),
        jax.ShapeDtypeStruct(wide, BF16),
        jax.ShapeDtypeStruct(wide, BF16),
    )
    return pl.pallas_call(
        functools.partial(backward_kernel, stage, first, own_type),
        out_shape=out_shape,
        grid=(1,),
        in_specs=[SM] + wholes(*given[1:]),
        out_specs=wholes(*out_shape),
        scratch_shapes=[
            pltpu.VMEM((blocks,) + wide, BF16),
            pltpu.VMEM((rows, rows), F32),
            pltpu.VMEM((blocks,) + wide, F32),
        ],
        input_output_aliases={} if first else {len(given) - 1: 0},
        compiler_params=LIMIT,
        cost_estimate=takes((12, 14)[stage] if stage < 2 else 4),
    )(*given)


def load_parts(sc, at, pieces, full, sems, dim):
    size = pieces[0].shape[dim]
    copies = []
    for i, piece in enumerate(pieces):
        if len(pieces) == 1:
            to = full
        elif dim == 0:
            to = full.at[pl.ds(pl.multiple_of(sc[at + i] * size, 16), size)]
        else:
            to = full.at[:, pl.ds(pl.multiple_of(sc[at + i] * size, 128), size)]
        copies.append(pltpu.make_async_copy(piece, to, sems.at[i]))
    for copy in copies:
        copy.start()
    return copies


def norm_scale(v):
    return lax.rsqrt(jnp.mean(v * v, axis=0, keepdims=True) + EPSILON)


def prepare_kernel(sc, tokens, positions, first, second):
    width, count = tokens.shape
    rows = count // 2
    p = positions[:, pl.ds(pl.multiple_of(sc[0], 128), count)]
    row = lax.broadcasted_iota(jnp.int32, (16, count), 0)
    p = jnp.where(row == 0, p >> 6, jnp.where(row == 1, p & 63, 0)).astype(F32).astype(BF16)
    for parity in range(2):

        @pl.when(sc[1] == parity)
        def _(parity=parity):
            for half, out in enumerate((first, second)):
                half = half ^ parity
                out[:width] = tokens[:, half * rows : (half + 1) * rows]
                out[width:] = p[:, half * rows : (half + 1) * rows]


def prepare(at, h, tokens, positions):
    width, count = tokens.shape
    out = jax.ShapeDtypeStruct((width + 16, count // 2), BF16)
    sc = jnp.stack([at, lax.rem(h, 2)]).astype(jnp.int32)
    return pl.pallas_call(
        prepare_kernel,
        out_shape=(out, out),
        grid=(1,),
        in_specs=[SM] + wholes(tokens, positions),
        out_specs=wholes(out, out),
        compiler_params=LIMIT,
        cost_estimate=takes(2),
    )(sc, tokens, positions)


def project_kernel(pieces, *refs):
    sc, xa, xb, cos, sin = refs[:5]
    parts = refs[5 : 5 + pieces]
    qz, kv, normed_t, gains, pos, ids, full, sems = refs[5 + pieces :]
    copies = load_parts(sc, 3, parts, full, sems, 0)
    rows = xa.shape[-1]
    width = full.shape[0]
    for q, x in enumerate((xa, xb)):
        p = x[width : width + 16].astype(F32)
        p = p[0:1] * 64.0 + p[1:2]
        pos[q] = p.astype(jnp.int32)
        block = sc[2] + (sc[0] if q == 0 else 3 - sc[0])
        lane = lax.broadcasted_iota(jnp.int32, (1, rows), 1).astype(F32)
        begin = block * rows + jnp.min(lane - p).astype(jnp.int32)
        ids[q] = block
        ids[2 + q] = lax.div(begin, rows)
    ids[4] = sc[2]
    ids[5] = sc[0]
    flat = [x[:width].astype(F32) for x in (xa, xb)]
    scaled = [v * norm_scale(v) for v in flat]
    for copy in copies:
        copy.wait()
    gains[...] = full[:, width + 320 : width + 448]
    gain = full[:, width + 384 : width + 385].astype(F32)
    half = HEAD_DIM // 2
    for q in range(2):
        normed = (scaled[q] * gain).astype(BF16)
        at = slice(q * rows, (q + 1) * rows)
        normed_t[:, at] = normed
        made = jnp.dot(normed.T, full[:, : width + 384], preferred_element_type=F32).T
        c, s = cos[:, at], sin[:, at]
        for h in range(HEADS):
            a = made[64 * h : 64 * h + half]
            b = made[64 * h + half : 64 * h + 64]
            ra = (a * c - b * s).astype(BF16) * jnp.asarray(HEAD_DIM**-0.5, BF16)
            rb = (b * c + a * s).astype(BF16) * jnp.asarray(HEAD_DIM**-0.5, BF16)
            group, lanes = h // GROUP, slice(h % GROUP * rows, (h % GROUP + 1) * rows)
            qz[q, group, :half, lanes] = ra
            qz[q, group, half : 2 * half, lanes] = rb
            qz[q, group, 2 * half :, lanes] = jnp.zeros((2 * half, rows), BF16)
        for k in range(KV_HEADS):
            row = width + 64 * k
            a = made[row : row + half]
            b = made[row + half : row + 64]
            ra = (a * c - b * s).astype(BF16)
            rb = (b * c + a * s).astype(BF16)
            v = made[row + 192 : row + 256].astype(BF16)
            kv[q, k] = jnp.concatenate([ra, rb, v], axis=0).T


def project(sc, xs, cos, sin, parts):
    rows = xs[0].shape[1]
    count = 2 * rows
    width = HEADS * HEAD_DIM
    out_shape = (
        jax.ShapeDtypeStruct((2, KV_HEADS, 2 * HEAD_DIM, GROUP * rows), BF16),
        jax.ShapeDtypeStruct((2, KV_HEADS, rows, 2 * HEAD_DIM), BF16),
        jax.ShapeDtypeStruct((width, count), BF16),
        jax.ShapeDtypeStruct((width, 128), BF16),
        jax.ShapeDtypeStruct((2, 1, rows), jnp.int32),
        jax.ShapeDtypeStruct((8,), jnp.int32),
    )
    return pl.pallas_call(
        functools.partial(project_kernel, len(parts)),
        out_shape=out_shape,
        grid=(1,),
        in_specs=[SM] + wholes(*xs, cos, sin) + [HB] * len(parts),
        out_specs=wholes(*out_shape[:-1]) + [SM],
        scratch_shapes=[
            pltpu.VMEM((width, parts[0].shape[1]), BF16),
            pltpu.SemaphoreType.DMA((len(parts),)),
        ],
        compiler_params=LIMIT,
        cost_estimate=takes(0),
    )(sc, *xs, cos, sin, *parts)


def wide(value):
    over = -value.shape[1] % 128
    if not over:
        return value
    return jnp.concatenate([value, jnp.zeros((value.shape[0], over), value.dtype)], axis=1)


def slot_of(sc, fsdp, f):
    ys = fsdp // 2
    return lax.rem(f + sc[0], 2), lax.rem(lax.div(f, 2) - sc[1] + ys, ys)


def put_slabs(packed, sc, fsdp, at, value):
    value = wide(value).astype(BF16)
    r = value.shape[0] // fsdp
    for f in range(fsdp):
        k, y = slot_of(sc, fsdp, f)
        for s in range(value.shape[1] // 128):
            packed[k, y, pl.ds(at + s * r, r)] = value[
                f * r : (f + 1) * r, s * 128 : (s + 1) * 128
            ]


def norm_back(v, gain, grad):
    r = norm_scale(v)
    scaled = grad * gain
    d_v = r * scaled - v * (r * r * r * jnp.mean(scaled * v, axis=0, keepdims=True))
    return d_v, jnp.sum(grad * (v * r), axis=1, keepdims=True)


def feed_kernel(fsdp, pieces, chunk, *refs):
    sc, xa, xb, ca, cb, mix, gains = refs[:7]
    parts = refs[7 : 7 + pieces]
    downs = refs[7 + pieces : 7 + 2 * pieces]
    refs = refs[7 + 2 * pieces :]
    res_a, res_b, d_middle, gz, delta, mine, give, second = refs[:8]
    full, out_w, down, packed, att_t, mid, n2, n2_t, res, d_second, cot_t, cot = refs[8:20]
    sems, out_sems, down_sems, grad_sems = refs[20:]
    ff = down.shape[1]
    out_copies = load_parts(sc, 3, [p.at[:, 2 * ff :] for p in parts], out_w, out_sems, 0)
    copies = load_parts(sc, 3, [p.at[:, : 2 * ff] for p in parts], full, sems, 0)
    down_copies = load_parts(sc, 3, downs, down, down_sems, 1)
    rows = xa.shape[-1]
    width, ff = down.shape
    shard = width // fsdp
    down_shard = ff // fsdp
    for q, c in enumerate((ca, cb)):
        cot_t[:, q * rows : (q + 1) * rows] = c[...]
        for h in range(HEADS):
            att_t[64 * h : 64 * h + 64, q * rows : (q + 1) * rows] = mix[
                q, h // GROUP, :, h % GROUP * rows : (h % GROUP + 1) * rows
            ]
    cot[...] = cot_t[...].T
    gain = gains[:, 65:66].astype(F32)
    for copy in out_copies:
        copy.wait()
    branch_t = jnp.dot(out_w[...].T, att_t[...], preferred_element_type=F32)
    for q, x in enumerate((xa, xb)):
        at = slice(q * rows, (q + 1) * rows)
        mid[:, at] = x[:width].astype(F32) + branch_t[:, at]
    n2_t[...] = (mid[...] * norm_scale(mid[...]) * gain).astype(BF16)
    n2[...] = n2_t[...].T
    res[...] = mid[...]
    d_second[...] = jnp.zeros(d_second.shape, F32)
    for copy in copies + down_copies:
        copy.wait()
    up_at = ff // 128 * shard
    out_at = 2 * up_at
    down_at = out_at + -(-width // 128) * shard
    used = down_at + -(-down_shard // 128) * width
    rows_all = packed.shape[2]
    if rows_all > used:
        packed[:, :, used:] = jnp.zeros((2, fsdp // 2, rows_all - used, 128), BF16)

    sends = []

    def send(at, n):
        for k, to in enumerate((mine, give)):
            span = pl.ds(at, n)
            copy = pltpu.make_async_copy(
                packed.at[k, :, span], to.at[:, span], grad_sems.at[len(sends)]
            )
            copy.start()
            sends.append(copy)

    for j in range(ff // chunk):
        cols = slice(j * chunk, (j + 1) * chunk)
        up_cols = slice(ff + j * chunk, ff + (j + 1) * chunk)
        gate_w, up_w, down_w = full[:, cols], full[:, up_cols], down[:, cols]
        gate = jnp.dot(n2[...], gate_w, preferred_element_type=F32)
        up = jnp.dot(n2[...], up_w, preferred_element_type=F32)
        sig = 1.0 / (1.0 + jnp.exp(-gate))
        silu = gate * sig
        hidden = (silu * up).astype(BF16)
        res[...] += dot(down_w, hidden, 1, 1)
        d_hidden = jnp.dot(cot[...], down_w, preferred_element_type=F32)
        d_gate = (d_hidden * up * (sig * (1.0 + gate * (1.0 - sig)))).astype(BF16)
        d_up = (d_hidden * silu).astype(BF16)
        d_second[...] += dot(gate_w, d_gate, 1, 1) + dot(up_w, d_up, 1, 1)
        slab = j * (chunk // 128) * shard
        put_slabs(packed, sc, fsdp, slab, jnp.dot(n2_t[...], d_gate, preferred_element_type=F32))
        put_slabs(
            packed, sc, fsdp, up_at + slab, jnp.dot(n2_t[...], d_up, preferred_element_type=F32)
        )
        down_g = jnp.dot(cot_t[...], hidden, preferred_element_type=F32).astype(BF16)
        if down_shard % 128:
            for n in range(chunk // down_shard):
                slot_k, slot_y = slot_of(sc, fsdp, j * (chunk // down_shard) + n)
                part = wide(down_g[:, n * down_shard : (n + 1) * down_shard])
                for s in range(part.shape[1] // 128):
                    packed[slot_k, slot_y, down_at + s * width : down_at + (s + 1) * width] = part[
                        :, s * 128 : (s + 1) * 128
                    ]
        else:
            for n in range(chunk // 128):
                slab = j * (chunk // 128) + n
                slot_k, slot_y = slot_of(sc, fsdp, slab // (down_shard // 128))
                at = down_at + slab % (down_shard // 128) * width
                packed[slot_k, slot_y, at : at + width] = down_g[:, n * 128 : (n + 1) * 128]
        send(j * (chunk // 128) * shard, chunk // 128 * shard)
        send(up_at + j * (chunk // 128) * shard, chunk // 128 * shard)

    send(down_at, rows_all - down_at)
    res_a[...] = res[:, :rows].astype(BF16)
    res_b[...] = res[:, rows:].astype(BF16)
    d_v, gain_grad = norm_back(mid[...], gain, d_second[...])
    second[...] = jnp.broadcast_to(gain_grad, second.shape)
    d_mid = cot_t[...].astype(F32) + d_v
    d_middle[...] = d_mid
    branch = d_mid.astype(BF16)
    put_slabs(packed, sc, fsdp, out_at, dot(att_t[...], branch, 1, 1))
    send(out_at, down_at - out_at)
    d_mix = jnp.dot(out_w[...], branch, preferred_element_type=F32).astype(BF16)
    for q in range(2):
        for h in range(HEADS):
            at = slice(q * rows, (q + 1) * rows)
            part = d_mix[64 * h : 64 * h + 64, at]
            group, lanes = h // GROUP, slice(h % GROUP * rows, (h % GROUP + 1) * rows)
            gz[q, group, :64, lanes] = jnp.zeros((64, rows), BF16)
            gz[q, group, 64:, lanes] = part
            delta[q, group, :, lanes] = jnp.sum(
                part.astype(F32) * att_t[64 * h : 64 * h + 64, at].astype(F32),
                axis=0,
                keepdims=True,
            )
    for copy in sends:
        copy.wait()


def feed_rows(fsdp, ctx, width, ff):
    used = (2 * (ff // 128) + -(-width // 128)) * (width // fsdp) + -(-(ff // fsdp) // 128) * width
    return -(-used // (16 * ctx)) * 16 * ctx


def feed(fsdp, ctx, sc, xs, cots, mix, gains, parts, downs):
    rows = cots[0].shape[1]
    width = cots[0].shape[0]
    count = 2 * rows
    ff = downs[0].shape[1] * len(downs)
    packed = (fsdp // 2, feed_rows(fsdp, ctx, width, ff), 128)
    out_shape = (
        jax.ShapeDtypeStruct((width, rows), BF16),
        jax.ShapeDtypeStruct((width, rows), BF16),
        jax.ShapeDtypeStruct((width, count), F32),
        jax.ShapeDtypeStruct((2, KV_HEADS, 2 * HEAD_DIM, GROUP * rows), BF16),
        jax.ShapeDtypeStruct((2, KV_HEADS, 1, GROUP * rows), F32),
        jax.ShapeDtypeStruct(packed, BF16),
        jax.ShapeDtypeStruct(packed, BF16),
        jax.ShapeDtypeStruct((width, 128), F32),
    )
    return pl.pallas_call(
        functools.partial(feed_kernel, fsdp, len(parts), ff // 4 if ff // fsdp % 128 else ff // 3),
        out_shape=out_shape,
        grid=(1,),
        in_specs=[SM] + wholes(*xs, *cots, mix, gains) + [HB] * (2 * len(parts)),
        out_specs=wholes(*out_shape[:5]) + [HB, HB] + wholes(out_shape[7]),
        scratch_shapes=[
            pltpu.VMEM((width, 2 * ff), BF16),
            pltpu.VMEM((width, width), BF16),
            pltpu.VMEM((width, ff), BF16),
            pltpu.VMEM((2,) + packed, BF16),
            pltpu.VMEM((width, count), BF16),
            pltpu.VMEM((width, count), F32),
            pltpu.VMEM((count, width), BF16),
            pltpu.VMEM((width, count), BF16),
            pltpu.VMEM((width, count), F32),
            pltpu.VMEM((width, count), F32),
            pltpu.VMEM((width, count), BF16),
            pltpu.VMEM((count, width), BF16),
            pltpu.SemaphoreType.DMA((len(parts),)),
            pltpu.SemaphoreType.DMA((len(parts),)),
            pltpu.SemaphoreType.DMA((len(parts),)),
            pltpu.SemaphoreType.DMA((24,)),
        ],
        compiler_params=LIMIT,
        cost_estimate=takes(19),
    )(sc, *xs, *cots, mix, gains, *parts, *downs)


def last_kernel(fsdp, pieces, chain, *refs):
    sc, xa, xb, cos, sin, normed_t, gains, second, d_middle, dq, own, *twin = refs[:13]
    refs = refs[13:]
    if chain:
        came = refs[0]
        refs = refs[1:]
    parts = refs[:pieces]
    grad_a, grad_b, mine, give, full, packed, made, sems = refs[pieces:]
    copies = load_parts(sc, 3, parts, full, sems, 0)
    rows = xa.shape[-1]
    width = full.shape[0]
    half = HEAD_DIM // 2
    for q in range(2):
        at = slice(q * rows, (q + 1) * rows)
        c, s = cos[:, at], sin[:, at]
        for h in range(HEADS):
            group, lanes = h // GROUP, slice(h % GROUP * rows, (h % GROUP + 1) * rows)
            a = dq[q, group, :half, lanes] * HEAD_DIM**-0.5
            b = dq[q, group, half:, lanes] * HEAD_DIM**-0.5
            made[64 * h : 64 * h + half, at] = (a * c + b * s).astype(BF16)
            made[64 * h + half : 64 * h + 64, at] = (b * c - a * s).astype(BF16)
        for k in range(KV_HEADS):
            both = own[q, k] + twin[q][k].astype(F32)
            if chain:
                both = both + came[q, k].astype(F32)
            both = both.T
            a, b = both[:half], both[half : 2 * half]
            row = width + 64 * k
            made[row : row + half, at] = (a * c + b * s).astype(BF16)
            made[row + half : row + 64, at] = (b * c - a * s).astype(BF16)
            made[row + 192 : row + 256, at] = both[2 * half :].astype(BF16)
    for copy in copies:
        copy.wait()
    gain = gains[:, 64:65].astype(F32)
    d_first = jnp.dot(full[:, : width + 384], made[...], preferred_element_type=F32)
    v = jnp.concatenate([xa[:width], xb[:width]], axis=1).astype(F32)
    d_v, first = norm_back(v, gain, d_first)
    d_x = (d_middle[...] + d_v).astype(BF16)
    grad_a[...] = d_x[:, :rows]
    grad_b[...] = d_x[:, rows:]
    front = dot(normed_t[...], made[...], 1, 1)
    lane = lax.broadcasted_iota(jnp.int32, (width, 64), 1)
    ends = jnp.where(lane == 0, first, second[:, :64])
    put_slabs(packed, sc, fsdp, 0, jnp.concatenate([front, ends], axis=1))
    used = (width + 448) // 128 * (width // fsdp)
    total = packed.shape[2]
    if total > used:
        packed[:, :, used:] = jnp.zeros((2, fsdp // 2, total - used, 128), BF16)
    mine[...] = packed[0]
    give[...] = packed[1]


def last(fsdp, ctx, sc, xs, cos, sin, normed_t, gains, second, d_middle, dq, dkv, parts):
    width, count = normed_t.shape
    rows = count // 2
    used = (width + 448) // 128 * (width // fsdp)
    packed = (fsdp // 2, -(-used // (16 * ctx)) * 16 * ctx, 128)
    given = (*xs, cos, sin, normed_t, gains, second, d_middle, dq, *dkv)
    out_shape = (
        jax.ShapeDtypeStruct((width, rows), BF16),
        jax.ShapeDtypeStruct((width, rows), BF16),
        jax.ShapeDtypeStruct(packed, BF16),
        jax.ShapeDtypeStruct(packed, BF16),
    )
    return pl.pallas_call(
        functools.partial(last_kernel, fsdp, len(parts), len(dkv) == 4),
        out_shape=out_shape,
        grid=(1,),
        in_specs=[SM] + wholes(*given) + [HB] * len(parts),
        out_specs=wholes(*out_shape),
        scratch_shapes=[
            pltpu.VMEM((width, parts[0].shape[1]), BF16),
            pltpu.VMEM((2,) + packed, BF16),
            pltpu.VMEM((width + 384, count), BF16),
            pltpu.SemaphoreType.DMA((len(parts),)),
        ],
        compiler_params=LIMIT,
        cost_estimate=takes(7),
    )(sc, *given, *parts)


def unpack_kernel(places, flat, *outs):
    for out, (at, rows, skip) in zip(outs, places, strict=True):
        columns = out.shape[1]
        done = 0
        while done < columns:
            slab, lane = divmod(skip + done, 128)
            n = min(128 - lane, columns - done)
            out[:, done : done + n] = flat[
                at + slab * rows : at + (slab + 1) * rows, lane : lane + n
            ].astype(F32)
            done += n


def join_unpack_kernel(places, parts, sc, *refs):
    pieces, outs, flat = refs[: 2 * parts], refs[2 * parts : -1], refs[-1]
    n = pieces[0].shape[0]
    half = parts // 2
    for i, piece in enumerate(pieces):
        x = lax.rem(sc[0] + i // parts, 2)
        p = lax.rem(sc[1] + parts - i % parts, parts)
        at = lax.div(p, half) * (parts * n) + x * (half * n) + lax.rem(p, half) * n
        flat[pl.ds(pl.multiple_of(at, 16), n)] = piece[...]
    unpack_kernel(places, flat, *outs)


def unpack(flat, places):
    out_shape = tuple(jax.ShapeDtypeStruct((p[1], p[3]), F32) for p in places)
    return pl.pallas_call(
        functools.partial(unpack_kernel, [p[:3] for p in places]),
        out_shape=out_shape,
        grid=(1,),
        in_specs=wholes(flat),
        out_specs=wholes(*out_shape),
        compiler_params=LIMIT,
        cost_estimate=takes(2),
    )(flat)


def join_unpack(place, near, far, places):
    pieces = (*near, *far)
    out_shape = tuple(jax.ShapeDtypeStruct((p[1], p[3]), F32) for p in places)
    return pl.pallas_call(
        functools.partial(join_unpack_kernel, [p[:3] for p in places], len(near)),
        out_shape=out_shape,
        grid=(1,),
        in_specs=[SM] + wholes(*pieces),
        out_specs=wholes(*out_shape),
        scratch_shapes=[pltpu.VMEM((len(pieces) * near[0].shape[0], 128), BF16)],
        compiler_params=LIMIT,
        cost_estimate=takes(3),
    )(place, *pieces)


def chip_sum(mine, got, i):
    return mine[i].astype(F32) + got[i].astype(F32)


def sum_y(mine, got, send):
    total = chip_sum(mine, got, 0)
    for s in range(1, mine.shape[0]):
        total = total + send["shift"][s](chip_sum(mine, got, s).astype(BF16)).astype(F32)
    return total.astype(BF16)


def spread_kernel(got, out):
    total = got[0].astype(F32)
    for i in range(1, got.shape[0]):
        total = total + got[i].astype(F32)
    total = total.astype(BF16)
    for i in range(got.shape[0]):
        out[i] = total


def sum_kernel(got, out):
    total = got[0].astype(F32)
    for i in range(1, got.shape[0]):
        total = total + got[i].astype(F32)
    out[...] = total.astype(BF16)


def simple_call(kernel, out_shape, *given):
    return pl.pallas_call(
        kernel,
        out_shape=out_shape,
        grid=(1,),
        in_specs=wholes(*given),
        out_specs=whole(out_shape),
        compiler_params=LIMIT,
        cost_estimate=takes(0),
    )(*given)


def exchange(total, axes, size):
    parts = total.reshape(size, total.shape[0] // size, 128)
    return lax.all_to_all(parts, axes, 0, 0, tiled=True)


def spread(got):
    return simple_call(spread_kernel, jax.ShapeDtypeStruct(got.shape, BF16), got)


def gather_over(spread, axes):
    return lax.all_to_all(spread, axes, 0, 0, tiled=True).reshape(-1, 128)


def came_kernel(own, twin_a, twin_b, *refs):
    *came, out = refs
    for i, twin in enumerate((twin_a, twin_b)):
        total = own[i].astype(F32) + twin[...].astype(F32)
        for c in came:
            total = total + c[i].astype(F32)
        out[i] = total.astype(BF16)


def halves_kernel(one, one_came, two, two_came, out):
    n = one.shape[0]
    out[:n] = (one[...].astype(F32) + one_came[...].astype(F32)).astype(BF16)
    out[n:] = (two[...].astype(F32) + two_came[...].astype(F32)).astype(BF16)


def first_kernel(x, *refs):
    mine, got, (to_y, to_x) = refs[:4], refs[4:8], refs[8:]
    for i in range(4):
        out = to_y if i < 2 else to_x
        out[i % 2] = (mine[i][0].astype(F32) + got[i][0].astype(F32)).astype(BF16)


def first_sums(x, mine, got):
    n = mine.shape[1] // 4
    block = (1, n, 128)
    places = [
        lambda i, x: (1, 0, 0),
        lambda i, x: (1, 1, 0),
        lambda i, x: (0, 3 - x[0], 0),
        lambda i, x: (1, 3 - x[0], 0),
    ]
    out = pl.BlockSpec((2, n, 128), lambda i, x: (0, 0, 0))
    return pl.pallas_call(
        first_kernel,
        out_shape=(jax.ShapeDtypeStruct((2, n, 128), BF16),) * 2,
        grid_spec=pltpu.PrefetchScalarGridSpec(
            num_scalar_prefetch=1,
            grid=(1,),
            in_specs=[pl.BlockSpec(block, at) for at in places] * 2,
            out_specs=[out, out],
        ),
        compiler_params=LIMIT,
        cost_estimate=takes(0),
    )(x, *[mine] * 4, *[got] * 4)


def second_kernel(x, *refs):
    mine, got, came, outs = refs[:4], refs[4:8], refs[8:12], refs[12:]
    for i in range(4):
        total = mine[i][0].astype(F32) + got[i][0].astype(F32) + came[i][0].astype(F32)
        outs[i][...] = total.astype(BF16)


def second_sums(x, mine, got, came_y, came_x):
    n = mine.shape[1] // 4
    block = (1, n, 128)
    own = [
        lambda i, x: (0, 1 - x[0], 0),
        lambda i, x: (0, x[0], 0),
        lambda i, x: (1, 2 + x[0], 0),
        lambda i, x: (0, 2 + x[0], 0),
    ]
    came = [
        lambda i, x: (1 - x[0], 0, 0),
        lambda i, x: (x[0], 0, 0),
        lambda i, x: (1, 0, 0),
        lambda i, x: (0, 0, 0),
    ]
    return pl.pallas_call(
        second_kernel,
        out_shape=(jax.ShapeDtypeStruct((n, 128), BF16),) * 4,
        grid_spec=pltpu.PrefetchScalarGridSpec(
            num_scalar_prefetch=1,
            grid=(1,),
            in_specs=[pl.BlockSpec(block, at) for at in own + own + came],
            out_specs=[pl.BlockSpec((n, 128), lambda i, x: (0, 0))] * 4,
        ),
        compiler_params=LIMIT,
        cost_estimate=takes(0),
    )(x, *[mine] * 4, *[got] * 4, came_y, came_y, came_x, came_x)


def gather_y(own, send, fsdp):
    return [own] + [send["shift"][s](own) for s in range(1, fsdp // 2)]


def gather_pieces(got, send, fsdp, core, y, join, dim):
    pieces = got + [send["core"](g) for g in got]
    own = got[0]
    if not join:
        return pieces
    buffer = jnp.zeros((fsdp,) + own.shape, own.dtype)
    for piece, f in zip(pieces, piece_order(fsdp, core, y), strict=True):
        buffer = lax.dynamic_update_index_in_dim(buffer, piece, f, 0)
    if dim:
        buffer = buffer.swapaxes(0, 1)
        return [buffer.reshape(own.shape[0], fsdp * own.shape[1])]
    return [buffer.reshape(fsdp * own.shape[0], own.shape[1])]


def piece_order(fsdp, core, y):
    ys = fsdp // 2
    source = [lax.rem(y - s + ys, ys) * 2 for s in range(ys)]
    return [f + core for f in source] + [f + 1 - core for f in source]


def body(
    fsdp,
    ctx,
    tokens,
    segment_ids,
    positions,
    cotangent,
    norm_first,
    query_weight,
    key_weight,
    value_weight,
    output_weight,
    norm_second,
    gate_weight,
    up_weight,
    down_weight,
):
    send = make_send(fsdp, ctx)
    ys, hs = fsdp // 2, ctx // 2
    _, count, width = tokens.shape
    rows = count // 2
    kv_width = KV_HEADS * HEAD_DIM
    y, core = lax.axis_index("y"), lax.axis_index("core")
    h, x = lax.axis_index("h"), lax.axis_index("x")
    ci = 2 * h + x
    reach = min(hs - 1, -(-(-(-(DOC_MOST - 1) // rows)) // 4))
    order = jnp.stack([core, y, 4 * h] + piece_order(fsdp, core, y)).astype(jnp.int32)
    shard = gate_weight.shape[0]
    join = shard % 16 != 0
    x_pair = prepare(2 * count * h + count * x, h, tokens.reshape(count, width).T, positions)
    *pair, query_weight, norm_first, norm_second = tie(
        *x_pair, query_weight, norm_first, norm_second
    )
    xs = send_home(send, pair)
    packed = jnp.concatenate(
        [
            query_weight,
            key_weight,
            value_weight,
            norm_first[:, None],
            norm_second[:, None],
            jnp.zeros((shard, 62), BF16),
        ],
        axis=1,
    )
    first_parts = gather_y(packed, send, fsdp)
    first_parts = gather_pieces(first_parts, send, fsdp, core, y, join, 0)
    cot_t, _ = tie(cotangent.reshape(count, width).T, first_parts[-1])
    cots = send_home(send, pick_home(cot_t, h))
    pos_f = jnp.concatenate([a[width : width + 2] for a in xs], axis=1).astype(F32)
    pos_f = pos_f[0:1] * 64.0 + pos_f[1:2]
    frequency = jnp.exp(
        jnp.arange(HEAD_DIM // 2, dtype=F32) * (-math.log(10000.0) * 2.0 / HEAD_DIM)
    )
    angle = frequency[:, None] * pos_f
    cos, sin = jnp.cos(angle), jnp.sin(angle)
    feed_own = jnp.concatenate([gate_weight, up_weight, output_weight], axis=1)
    feed_own, down_own, _ = tie(feed_own, down_weight.T, first_parts[-1])
    feed_got = gather_y(feed_own, send, fsdp)
    down_got = gather_y(down_own, send, fsdp)
    feed_got[0], *xs = tie(feed_got[0], *xs)
    qz, kv, normed_t, gains, pos, ids = project(order, xs, cos, sin, first_parts)

    stages = []
    carried = None
    for s in range(reach + 1):
        stages.append((kv, send["core"](kv)))
        if s < reach:
            kv = send["up"](kv)
        carried = attend_forward(s, ids, pos, qz, stages[s], carried, s == reach)
        if s < reach:
            kv, *carried = tie(kv, *carried)
    mixed, lse = carried
    feed_parts = gather_pieces(feed_got, send, fsdp, core, y, join, 0)
    down_parts = gather_pieces(down_got, send, fsdp, core, y, join, 1)
    res_a, res_b, d_middle, gz, delta, mine, give, second = feed(
        fsdp, ctx, order, xs, cots, mixed, gains, feed_parts, down_parts
    )

    got = send["core"](give)
    crossed = ys == 2
    x_ref = x.astype(jnp.int32).reshape(1)
    dq = None
    came = None
    for s in range(reach, -1, -1):
        sc = ids
        if s == reach - 1 and crossed:
            first_y, first_x = first_sums(x_ref, mine, got)
            sc, first_y, first_x = tie(sc, first_y, first_x)
            came_y, came_x = send["shift"][1](first_y), send["across"](first_x)
        if s == 0 and crossed:
            came_y, came_x, dq = tie(came_y, came_x, dq)
            give_one, keep_one, give_two, keep_two = second_sums(x_ref, mine, got, came_y, came_x)
            sc, give_one, give_two = tie(sc, give_one, give_two)
            came_one, came_two = send["across"](give_one), send["shift"][1](give_two)
        if came is not None:
            sc, came = tie(sc, came)
            came = send["down"](came)
        dq, own, *other = attend_backward(
            s, sc, pos, qz, gz, lse, delta, stages[s], dq, F32 if s == 0 else BF16
        )
        twin = tuple(send["core"](o) for o in other)
        if s > 0:
            if s == reach - 1:
                *twin, came, dq, res_a, res_b = tie(*twin, came, dq, *result)
            elif s < reach:
                *twin, came, dq = tie(*twin, came, dq)
            given = (own, *twin) if came is None else (own, *twin, came)
            came = simple_call(came_kernel, jax.ShapeDtypeStruct(own.shape, BF16), *given)
            if s == reach:
                came, res_a, res_b = tie(came, res_a, res_b)
                result = send_back(send, res_a, res_b)
    dkv = (own, *twin) if came is None else (own, *twin, came)
    if crossed:
        late = simple_call(
            halves_kernel,
            jax.ShapeDtypeStruct((mine.shape[1] // 2, 128), BF16),
            keep_one,
            came_one,
            keep_two,
            came_two,
        )
        late, dq = tie(late, dq)
        late = exchange(late, ("h",), hs)
    else:
        late = exchange(sum_y(mine, got, send), CTX, ctx)
    tok_a, tok_b, mine_front, give_front = last(
        fsdp, ctx, order, xs, cos, sin, normed_t, gains, second, d_middle, dq, dkv, first_parts
    )
    got_front = send["core"](give_front)
    late, got_front = tie(late, got_front)
    front = sum_y(mine_front, got_front, send)
    if crossed:
        piece = simple_call(sum_kernel, jax.ShapeDtypeStruct(late.shape[1:], BF16), late)
        near = [piece] + [send["around"][s](piece) for s in range(1, hs)]
        far = [send["across"](p) for p in near]
        *near, tok_a, tok_b = tie(*near, tok_a, tok_b)
    else:
        late = gather_over(spread(late), CTX)
    front = spread(exchange(front, CTX, ctx))
    front = gather_over(front, CTX)
    tokens_grad = send_back(send, tok_a, tok_b)

    ff = gate_weight.shape[1]
    down_shard = down_weight.shape[0]
    gate_rows, out_rows = ff // 128 * shard, -(-width // 128) * shard
    places = [
        (0, shard, 0, ff),
        (gate_rows, shard, 0, ff),
        (2 * gate_rows, shard, 0, width),
        (2 * gate_rows + out_rows, width, 0, down_shard),
    ]
    if crossed:
        late_grads = join_unpack(jnp.stack([x, h]).astype(jnp.int32), near, far, places)
    else:
        late_grads = unpack(late, places)
    gate_grad, up_grad, output_grad, down_grad = late_grads
    query_grad, key_grad, value_grad, ends = unpack(
        front,
        [
            (0, shard, 0, width),
            (0, shard, width, kv_width),
            (0, shard, width + kv_width, kv_width),
            (0, shard, width + 2 * kv_width, 64),
        ],
    )
    return (
        low_high(res_a, res_b, h).T[None],
        low_high(*tokens_grad, h).T[None],
        ends[:, 0],
        query_grad,
        key_grad,
        value_grad,
        output_grad,
        ends[:, 1],
        gate_grad,
        up_grad,
        down_grad.T,
    )


def solution(mesh):
    fsdp, ctx = mesh.shape["fsdp"], mesh.shape["ctx"]
    places = Mesh(mesh.devices.reshape(fsdp // 2, 2, ctx // 2, 2), AXES)
    owner = ("y", "core")
    flat, split = P(owner), P(owner, None)
    whole = P(owner, CTX, None)
    return jax.shard_map(
        functools.partial(body, fsdp, ctx),
        mesh=places,
        in_specs=(whole, split, split, whole, flat, split, split, split, split, flat, split, split, split),
        out_specs=(whole, whole, flat, split, split, split, split, flat, split, split, split),
        check_vma=False,
    )
```

```python
import functools
import math

import jax
import jax.numpy as jnp
from jax import lax
from jax.experimental import pallas as pl
from jax.experimental.pallas import tpu as pltpu
from jax.sharding import Mesh
from jax.sharding import PartitionSpec as P

HEADS = 9
KV_HEADS = 3
GROUP = HEADS // KV_HEADS
HEAD_DIM = 64
EPSILON = 1e-05
MASKED = -1e30
DOC_MOST = 2000
AXES = ("y", "core", "h", "x")
CTX = ("h", "x")
F32 = jnp.float32
BF16 = jnp.bfloat16


def moves(fsdp, ctx, step):
    pairs = []
    for f in range(fsdp):
        for c in range(ctx):
            to = step(f // 2, f % 2, c // 2, c % 2)
            if to is not None:
                y, core, h, x = to
                pairs.append((f * ctx + c, (2 * y + core) * ctx + 2 * h + x))
    return pairs


def make_send(fsdp, ctx):
    ys, hs, blocks = fsdp // 2, ctx // 2, 2 * ctx

    def along(pairs):
        return lambda a: lax.ppermute(a, AXES, pairs)

    def by(step):
        return along(moves(fsdp, ctx, step))

    def home(slot):
        def step(y, core, h, x):
            low = 2 * h + x
            block = low if h % 2 == slot else blocks - 1 - low
            return (y, int(block % 4 in (1, 2)), block // 4, core)

        return moves(fsdp, ctx, step)

    def back(pairs):
        return along([(b, a) for a, b in pairs])

    return dict(
        home=[along(home(0)), along(home(1))],
        back=[back(home(0)), back(home(1))],
        core=by(lambda y, k, h, x: (y, 1 - k, h, x)),
        across=by(lambda y, k, h, x: (y, k, h, 1 - x)),
        up=by(lambda y, k, h, x: (y, k, h + 1, x) if h + 1 < hs else None),
        down=by(lambda y, k, h, x: (y, k, h - 1, x) if h > 0 else None),
        around=[by(lambda y, k, h, x, s=s: (y, k, (h + s) % hs, x)) for s in range(hs)],
        shift=[by(lambda y, k, h, x, s=s: ((y + s) % ys, k, h, x)) for s in range(ys)],
    )


def pick_home(a, h):
    r = a.shape[1] // 2
    low, high = a[:, :r], a[:, r:]
    even = lax.rem(h, 2) == 0
    return jnp.where(even, low, high), jnp.where(even, high, low)


def send_home(send, pair):
    return send["home"][0](pair[0]), send["home"][1](pair[1])


def send_back(send, a, b):
    return send["back"][0](a), send["back"][1](b)


def low_high(a, b, h):
    even = lax.rem(h, 2) == 0
    return jnp.concatenate([jnp.where(even, a, b), jnp.where(even, b, a)], axis=1)


def tie(*values):
    return lax.optimization_barrier(values)


def bias_of(begin, place, block_id, keys, rows):
    key_place = block_id * keys + lax.broadcasted_iota(jnp.int32, (keys, rows), 0)
    seen = (key_place >= begin) & (key_place <= place)
    return jnp.where(seen, 0.0, MASKED)


def dot(left, right, left_dim, right_dim):
    return lax.dot_general(
        left, right, (((left_dim,), (right_dim,)), ((), ())), preferred_element_type=F32
    )


def load_blocks(pieces, held):
    held[:2] = pieces[0][...]
    held[2:] = pieces[1][...]


def each_pair(sc, stage, work):
    base, core = sc[4] - 4 * stage, sc[5]

    def step(i, _):
        q = lax.div(i, 4)
        k = lax.rem(i, 4)
        within = jnp.where(k < 2, core, 1 - core)
        block_id = base + jnp.where(lax.rem(k, 2) == 0, within, 3 - within)

        @pl.when((block_id >= sc[2 + q]) & (block_id <= sc[q]))
        def _():
            work(q, k, block_id)

        return 0

    lax.fori_loop(0, 8, step, 0)


def forward_kernel(stage, last, *refs):
    first = stage == 0
    refs = list(refs)
    sc, pos, qz = refs[:3]
    kv = refs[3:5]
    refs = refs[5:]
    if not first:
        peak_in, total_in, mix_in = refs[:3]
        refs = refs[3:]
    if last:
        out, lse = refs[:2]
        held, bias, peak, total, mix = refs[2:]
    else:
        peak, total, mix = refs[:3]
        held, bias = refs[3:]
    rows = pos.shape[-1]
    if first:
        peak[...] = jnp.full(peak.shape, MASKED, F32)
        total[...] = jnp.zeros(total.shape, F32)
        mix[...] = jnp.zeros(mix.shape, F32)
    else:
        peak[...] = peak_in[...]
        total[...] = total_in[...]
        mix[...] = mix_in[...]
    load_blocks(kv, held)

    def work(q, k, block_id):
        place = sc[q] * rows + lax.broadcasted_iota(jnp.int32, (1, rows), 1)
        bias[...] = bias_of(place - pos[q], place, block_id, rows, rows)
        for c in range(KV_HEADS):
            seen = dot(held[k, c, :, :HEAD_DIM], qz[q, c], 1, 0) + jnp.concatenate([bias[...]] * GROUP, axis=1)
            old = peak[q, c]
            new = jnp.maximum(old, jnp.max(seen, axis=0, keepdims=True))
            expo = jnp.exp(seen - new)
            fade = jnp.exp(old - new)
            peak[q, c] = new
            total[q, c] = total[q, c] * fade + jnp.sum(expo, axis=0, keepdims=True)
            values = held[k, c].T[HEAD_DIM:]
            mix[q, c] = mix[q, c] * fade + dot(values, expo.astype(BF16), 1, 0)

    each_pair(sc, stage, work)
    if last:
        lse[...] = peak[...] + jnp.log(total[...])
        for q in range(2):
            for c in range(KV_HEADS):
                out[q, c] = (mix[q, c] / total[q, c]).astype(BF16)


def backward_kernel(stage, first, own_type, *refs):
    refs = list(refs)
    sc, pos, qz, gz, lse, delta = refs[:6]
    kv = refs[6:8]
    refs = refs[8:]
    if not first:
        dq_in = refs[0]
        refs = refs[1:]
    dq, own, other_a, other_b, held, bias, dkv = refs
    rows = pos.shape[-1]
    if first:
        dq[...] = jnp.zeros(dq.shape, F32)
    else:
        dq[...] = dq_in[...]
    load_blocks(kv, held)
    dkv[...] = jnp.zeros(dkv.shape, F32)

    def work(q, k, block_id):
        place = sc[q] * rows + lax.broadcasted_iota(jnp.int32, (1, rows), 1)
        bias[...] = bias_of(place - pos[q], place, block_id, rows, rows)
        for c in range(KV_HEADS):
            block = held[k, c]
            keys, values = block[:, :HEAD_DIM], block[:, HEAD_DIM:]
            seen = dot(keys, qz[q, c], 1, 0) + jnp.concatenate([bias[...]] * GROUP, axis=1)
            probs = jnp.exp(seen - lse[q, c])
            d_scores = (probs * (dot(values, gz[q, c], 1, 0) - delta[q, c])).astype(BF16)
            d_both = [dot(d_scores, qz[q, c], 1, 1), dot(probs.astype(BF16), gz[q, c], 1, 1)]
            dkv[k, c] += jnp.concatenate(d_both, axis=1)
            dq[q, c] += dot(block.T[:HEAD_DIM], d_scores, 1, 0)

    each_pair(sc, stage, work)
    own[...] = dkv[:2].astype(own_type)
    other_a[...] = dkv[2].astype(BF16)
    other_b[...] = dkv[3].astype(BF16)


SM = pl.BlockSpec(memory_space=pltpu.SMEM)
HB = pl.BlockSpec(memory_space=pl.ANY)


def whole(a):
    return pl.BlockSpec(
        a.shape, lambda i: (0,) * len(a.shape), pipeline_mode=pl.Buffered(buffer_count=1)
    )


def wholes(*arrays):
    return [whole(a) for a in arrays]


def takes(us):
    return pl.CostEstimate(flops=int(us * 1.15e9), bytes_accessed=0, transcendentals=0)


LIMIT = pltpu.CompilerParams(vmem_limit_bytes=64 << 20)


def attend_forward(stage, sc, pos, qz, pieces, carried, last):
    rows = pos.shape[-1]
    blocks = 4
    first = carried is None
    stat = jax.ShapeDtypeStruct((2, KV_HEADS, 1, GROUP * rows), F32)
    mix = jax.ShapeDtypeStruct((2, KV_HEADS, HEAD_DIM, GROUP * rows), F32)
    scratch = [
        pltpu.VMEM((blocks, KV_HEADS, rows, 2 * HEAD_DIM), BF16),
        pltpu.VMEM((rows, rows), F32),
    ]
    if last:
        out_shape = (jax.ShapeDtypeStruct(mix.shape, BF16), stat)
        scratch += [pltpu.VMEM(s.shape, F32) for s in (stat, stat, mix)]
        aliases = {}
    else:
        out_shape = (stat, stat, mix)
        aliases = {} if first else {3 + len(pieces) + i: i for i in range(3)}
    given = (sc, pos, qz, *pieces) + (() if first else tuple(carried))
    pairs = blocks * HEADS * rows * rows
    return pl.pallas_call(
        functools.partial(forward_kernel, stage, last),
        out_shape=out_shape,
        grid=(1,),
        in_specs=[SM] + wholes(*given[1:]),
        out_specs=wholes(*out_shape),
        scratch_shapes=scratch,
        input_output_aliases=aliases,
        compiler_params=LIMIT,
        cost_estimate=takes(0),
    )(*given)


def attend_backward(stage, sc, pos, qz, gz, lse, delta, pieces, dq, own_type):
    rows = pos.shape[-1]
    blocks = 4
    first = dq is None
    wide = (KV_HEADS, rows, 2 * HEAD_DIM)
    given = (sc, pos, qz, gz, lse, delta, *pieces) + (() if first else (dq,))
    pairs = blocks * HEADS * rows * rows
    out_shape = (
        jax.ShapeDtypeStruct((2, KV_HEADS, HEAD_DIM, GROUP * rows), F32),
        jax.ShapeDtypeStruct((blocks // 2,) + wide, own_type),
        jax.ShapeDtypeStruct(wide, BF16),
        jax.ShapeDtypeStruct(wide, BF16),
    )
    return pl.pallas_call(
        functools.partial(backward_kernel, stage, first, own_type),
        out_shape=out_shape,
        grid=(1,),
        in_specs=[SM] + wholes(*given[1:]),
        out_specs=wholes(*out_shape),
        scratch_shapes=[
            pltpu.VMEM((blocks,) + wide, BF16),
            pltpu.VMEM((rows, rows), F32),
            pltpu.VMEM((blocks,) + wide, F32),
        ],
        input_output_aliases={} if first else {len(given) - 1: 0},
        compiler_params=LIMIT,
        cost_estimate=takes((12, 14)[stage] if stage < 2 else 4),
    )(*given)


def load_parts(sc, at, pieces, full, sems, dim):
    size = pieces[0].shape[dim]
    copies = []
    for i, piece in enumerate(pieces):
        if len(pieces) == 1:
            to = full
        elif dim == 0:
            to = full.at[pl.ds(pl.multiple_of(sc[at + i] * size, 16), size)]
        else:
            to = full.at[:, pl.ds(pl.multiple_of(sc[at + i] * size, 128), size)]
        copies.append(pltpu.make_async_copy(piece, to, sems.at[i]))
    for copy in copies:
        copy.start()
    return copies


def norm_scale(v):
    return lax.rsqrt(jnp.mean(v * v, axis=0, keepdims=True) + EPSILON)


def prepare_kernel(sc, tokens, positions, first, second):
    width, count = tokens.shape
    rows = count // 2
    p = positions[:, pl.ds(pl.multiple_of(sc[0], 128), count)]
    row = lax.broadcasted_iota(jnp.int32, (16, count), 0)
    p = jnp.where(row == 0, p >> 6, jnp.where(row == 1, p & 63, 0)).astype(F32).astype(BF16)
    for parity in range(2):

        @pl.when(sc[1] == parity)
        def _(parity=parity):
            for half, out in enumerate((first, second)):
                half = half ^ parity
                out[:width] = tokens[:, half * rows : (half + 1) * rows]
                out[width:] = p[:, half * rows : (half + 1) * rows]


def prepare(at, h, tokens, positions):
    width, count = tokens.shape
    out = jax.ShapeDtypeStruct((width + 16, count // 2), BF16)
    sc = jnp.stack([at, lax.rem(h, 2)]).astype(jnp.int32)
    return pl.pallas_call(
        prepare_kernel,
        out_shape=(out, out),
        grid=(1,),
        in_specs=[SM] + wholes(tokens, positions),
        out_specs=wholes(out, out),
        compiler_params=LIMIT,
        cost_estimate=takes(2),
    )(sc, tokens, positions)


def project_kernel(pieces, *refs):
    sc, xa, xb, cos, sin = refs[:5]
    parts = refs[5 : 5 + pieces]
    qz, kv, normed_t, gains, pos, ids, full, sems = refs[5 + pieces :]
    copies = load_parts(sc, 3, parts, full, sems, 0)
    rows = xa.shape[-1]
    width = full.shape[0]
    for q, x in enumerate((xa, xb)):
        p = x[width : width + 16].astype(F32)
        p = p[0:1] * 64.0 + p[1:2]
        pos[q] = p.astype(jnp.int32)
        block = sc[2] + (sc[0] if q == 0 else 3 - sc[0])
        lane = lax.broadcasted_iota(jnp.int32, (1, rows), 1).astype(F32)
        begin = block * rows + jnp.min(lane - p).astype(jnp.int32)
        ids[q] = block
        ids[2 + q] = lax.div(begin, rows)
    ids[4] = sc[2]
    ids[5] = sc[0]
    flat = [x[:width].astype(F32) for x in (xa, xb)]
    scaled = [v * norm_scale(v) for v in flat]
    for copy in copies:
        copy.wait()
    gains[...] = full[:, width + 320 : width + 448]
    gain = full[:, width + 384 : width + 385].astype(F32)
    half = HEAD_DIM // 2
    for q in range(2):
        normed = (scaled[q] * gain).astype(BF16)
        at = slice(q * rows, (q + 1) * rows)
        normed_t[:, at] = normed
        made = jnp.dot(normed.T, full[:, : width + 384], preferred_element_type=F32).T
        c, s = cos[:, at], sin[:, at]
        for h in range(HEADS):
            a = made[64 * h : 64 * h + half]
            b = made[64 * h + half : 64 * h + 64]
            ra = (a * c - b * s).astype(BF16) * jnp.asarray(HEAD_DIM**-0.5, BF16)
            rb = (b * c + a * s).astype(BF16) * jnp.asarray(HEAD_DIM**-0.5, BF16)
            group, lanes = h // GROUP, slice(h % GROUP * rows, (h % GROUP + 1) * rows)
            qz[q, group, :half, lanes] = ra
            qz[q, group, half:, lanes] = rb
        for k in range(KV_HEADS):
            row = width + 64 * k
            a = made[row : row + half]
            b = made[row + half : row + 64]
            ra = (a * c - b * s).astype(BF16)
            rb = (b * c + a * s).astype(BF16)
            v = made[row + 192 : row + 256].astype(BF16)
            kv[q, k] = jnp.concatenate([ra, rb, v], axis=0).T


def project(sc, xs, cos, sin, parts):
    rows = xs[0].shape[1]
    count = 2 * rows
    width = HEADS * HEAD_DIM
    out_shape = (
        jax.ShapeDtypeStruct((2, KV_HEADS, HEAD_DIM, GROUP * rows), BF16),
        jax.ShapeDtypeStruct((2, KV_HEADS, rows, 2 * HEAD_DIM), BF16),
        jax.ShapeDtypeStruct((width, count), BF16),
        jax.ShapeDtypeStruct((width, 128), BF16),
        jax.ShapeDtypeStruct((2, 1, rows), jnp.int32),
        jax.ShapeDtypeStruct((8,), jnp.int32),
    )
    return pl.pallas_call(
        functools.partial(project_kernel, len(parts)),
        out_shape=out_shape,
        grid=(1,),
        in_specs=[SM] + wholes(*xs, cos, sin) + [HB] * len(parts),
        out_specs=wholes(*out_shape[:-1]) + [SM],
        scratch_shapes=[
            pltpu.VMEM((width, parts[0].shape[1]), BF16),
            pltpu.SemaphoreType.DMA((len(parts),)),
        ],
        compiler_params=LIMIT,
        cost_estimate=takes(0),
    )(sc, *xs, cos, sin, *parts)


def wide(value):
    over = -value.shape[1] % 128
    if not over:
        return value
    return jnp.concatenate([value, jnp.zeros((value.shape[0], over), value.dtype)], axis=1)


def slot_of(sc, fsdp, f):
    ys = fsdp // 2
    return lax.rem(f + sc[0], 2), lax.rem(lax.div(f, 2) - sc[1] + ys, ys)


def put_slabs(packed, sc, fsdp, at, value):
    value = wide(value).astype(BF16)
    r = value.shape[0] // fsdp
    for f in range(fsdp):
        k, y = slot_of(sc, fsdp, f)
        for s in range(value.shape[1] // 128):
            packed[k, y, pl.ds(at + s * r, r)] = value[
                f * r : (f + 1) * r, s * 128 : (s + 1) * 128
            ]


def norm_back(v, gain, grad):
    r = norm_scale(v)
    scaled = grad * gain
    d_v = r * scaled - v * (r * r * r * jnp.mean(scaled * v, axis=0, keepdims=True))
    return d_v, jnp.sum(grad * (v * r), axis=1, keepdims=True)


def feed_kernel(fsdp, pieces, chunk, *refs):
    sc, xa, xb, ca, cb, mix, gains = refs[:7]
    parts = refs[7 : 7 + pieces]
    downs = refs[7 + pieces : 7 + 2 * pieces]
    refs = refs[7 + 2 * pieces :]
    res_a, res_b, d_middle, gz, delta, mine, give, second = refs[:8]
    full, out_w, down, packed, att_t, mid, n2, n2_t, res, d_second, cot_t, cot = refs[8:20]
    sems, out_sems, down_sems, grad_sems = refs[20:]
    ff = down.shape[1]
    out_copies = load_parts(sc, 3, [p.at[:, 2 * ff :] for p in parts], out_w, out_sems, 0)
    copies = load_parts(sc, 3, [p.at[:, : 2 * ff] for p in parts], full, sems, 0)
    down_copies = load_parts(sc, 3, downs, down, down_sems, 1)
    rows = xa.shape[-1]
    width, ff = down.shape
    shard = width // fsdp
    down_shard = ff // fsdp
    for q, c in enumerate((ca, cb)):
        cot_t[:, q * rows : (q + 1) * rows] = c[...]
        for h in range(HEADS):
            att_t[64 * h : 64 * h + 64, q * rows : (q + 1) * rows] = mix[
                q, h // GROUP, :, h % GROUP * rows : (h % GROUP + 1) * rows
            ]
    cot[...] = cot_t[...].T
    gain = gains[:, 65:66].astype(F32)
    for copy in out_copies:
        copy.wait()
    branch_t = jnp.dot(out_w[...].T, att_t[...], preferred_element_type=F32)
    for q, x in enumerate((xa, xb)):
        at = slice(q * rows, (q + 1) * rows)
        mid[:, at] = x[:width].astype(F32) + branch_t[:, at]
    n2_t[...] = (mid[...] * norm_scale(mid[...]) * gain).astype(BF16)
    n2[...] = n2_t[...].T
    res[...] = mid[...]
    d_second[...] = jnp.zeros(d_second.shape, F32)
    for copy in copies + down_copies:
        copy.wait()
    up_at = ff // 128 * shard
    out_at = 2 * up_at
    down_at = out_at + -(-width // 128) * shard
    used = down_at + -(-down_shard // 128) * width
    rows_all = packed.shape[2]
    if rows_all > used:
        packed[:, :, used:] = jnp.zeros((2, fsdp // 2, rows_all - used, 128), BF16)

    sends = []

    def send(at, n):
        for k, to in enumerate((mine, give)):
            span = pl.ds(at, n)
            copy = pltpu.make_async_copy(
                packed.at[k, :, span], to.at[:, span], grad_sems.at[len(sends)]
            )
            copy.start()
            sends.append(copy)

    for j in range(ff // chunk):
        cols = slice(j * chunk, (j + 1) * chunk)
        up_cols = slice(ff + j * chunk, ff + (j + 1) * chunk)
        gate_w, up_w, down_w = full[:, cols], full[:, up_cols], down[:, cols]
        gate = jnp.dot(n2[...], gate_w, preferred_element_type=F32)
        up = jnp.dot(n2[...], up_w, preferred_element_type=F32)
        sig = 1.0 / (1.0 + jnp.exp(-gate))
        silu = gate * sig
        hidden = (silu * up).astype(BF16)
        res[...] += dot(down_w, hidden, 1, 1)
        d_hidden = jnp.dot(cot[...], down_w, preferred_element_type=F32)
        d_gate = (d_hidden * up * (sig * (1.0 + gate * (1.0 - sig)))).astype(BF16)
        d_up = (d_hidden * silu).astype(BF16)
        d_second[...] += dot(gate_w, d_gate, 1, 1) + dot(up_w, d_up, 1, 1)
        slab = j * (chunk // 128) * shard
        put_slabs(packed, sc, fsdp, slab, jnp.dot(n2_t[...], d_gate, preferred_element_type=F32))
        put_slabs(
            packed, sc, fsdp, up_at + slab, jnp.dot(n2_t[...], d_up, preferred_element_type=F32)
        )
        down_g = jnp.dot(cot_t[...], hidden, preferred_element_type=F32).astype(BF16)
        if down_shard % 128:
            for n in range(chunk // down_shard):
                slot_k, slot_y = slot_of(sc, fsdp, j * (chunk // down_shard) + n)
                part = wide(down_g[:, n * down_shard : (n + 1) * down_shard])
                for s in range(part.shape[1] // 128):
                    packed[slot_k, slot_y, down_at + s * width : down_at + (s + 1) * width] = part[
                        :, s * 128 : (s + 1) * 128
                    ]
        else:
            for n in range(chunk // 128):
                slab = j * (chunk // 128) + n
                slot_k, slot_y = slot_of(sc, fsdp, slab // (down_shard // 128))
                at = down_at + slab % (down_shard // 128) * width
                packed[slot_k, slot_y, at : at + width] = down_g[:, n * 128 : (n + 1) * 128]
        send(j * (chunk // 128) * shard, chunk // 128 * shard)
        send(up_at + j * (chunk // 128) * shard, chunk // 128 * shard)

    send(down_at, rows_all - down_at)
    res_a[...] = res[:, :rows].astype(BF16)
    res_b[...] = res[:, rows:].astype(BF16)
    d_v, gain_grad = norm_back(mid[...], gain, d_second[...])
    second[...] = jnp.broadcast_to(gain_grad, second.shape)
    d_mid = cot_t[...].astype(F32) + d_v
    d_middle[...] = d_mid
    branch = d_mid.astype(BF16)
    put_slabs(packed, sc, fsdp, out_at, dot(att_t[...], branch, 1, 1))
    send(out_at, down_at - out_at)
    d_mix = jnp.dot(out_w[...], branch, preferred_element_type=F32).astype(BF16)
    for q in range(2):
        for h in range(HEADS):
            at = slice(q * rows, (q + 1) * rows)
            part = d_mix[64 * h : 64 * h + 64, at]
            group, lanes = h // GROUP, slice(h % GROUP * rows, (h % GROUP + 1) * rows)
            gz[q, group, :, lanes] = part
            delta[q, group, :, lanes] = jnp.sum(
                part.astype(F32) * att_t[64 * h : 64 * h + 64, at].astype(F32),
                axis=0,
                keepdims=True,
            )
    for copy in sends:
        copy.wait()


def feed_rows(fsdp, ctx, width, ff):
    used = (2 * (ff // 128) + -(-width // 128)) * (width // fsdp) + -(-(ff // fsdp) // 128) * width
    return -(-used // (16 * ctx)) * 16 * ctx


def feed(fsdp, ctx, sc, xs, cots, mix, gains, parts, downs):
    rows = cots[0].shape[1]
    width = cots[0].shape[0]
    count = 2 * rows
    ff = downs[0].shape[1] * len(downs)
    packed = (fsdp // 2, feed_rows(fsdp, ctx, width, ff), 128)
    out_shape = (
        jax.ShapeDtypeStruct((width, rows), BF16),
        jax.ShapeDtypeStruct((width, rows), BF16),
        jax.ShapeDtypeStruct((width, count), F32),
        jax.ShapeDtypeStruct((2, KV_HEADS, HEAD_DIM, GROUP * rows), BF16),
        jax.ShapeDtypeStruct((2, KV_HEADS, 1, GROUP * rows), F32),
        jax.ShapeDtypeStruct(packed, BF16),
        jax.ShapeDtypeStruct(packed, BF16),
        jax.ShapeDtypeStruct((width, 128), F32),
    )
    return pl.pallas_call(
        functools.partial(feed_kernel, fsdp, len(parts), ff // 4 if ff // fsdp % 128 else ff // 3),
        out_shape=out_shape,
        grid=(1,),
        in_specs=[SM] + wholes(*xs, *cots, mix, gains) + [HB] * (2 * len(parts)),
        out_specs=wholes(*out_shape[:5]) + [HB, HB] + wholes(out_shape[7]),
        scratch_shapes=[
            pltpu.VMEM((width, 2 * ff), BF16),
            pltpu.VMEM((width, width), BF16),
            pltpu.VMEM((width, ff), BF16),
            pltpu.VMEM((2,) + packed, BF16),
            pltpu.VMEM((width, count), BF16),
            pltpu.VMEM((width, count), F32),
            pltpu.VMEM((count, width), BF16),
            pltpu.VMEM((width, count), BF16),
            pltpu.VMEM((width, count), F32),
            pltpu.VMEM((width, count), F32),
            pltpu.VMEM((width, count), BF16),
            pltpu.VMEM((count, width), BF16),
            pltpu.SemaphoreType.DMA((len(parts),)),
            pltpu.SemaphoreType.DMA((len(parts),)),
            pltpu.SemaphoreType.DMA((len(parts),)),
            pltpu.SemaphoreType.DMA((24,)),
        ],
        compiler_params=LIMIT,
        cost_estimate=takes(19),
    )(sc, *xs, *cots, mix, gains, *parts, *downs)


def last_kernel(fsdp, pieces, chain, *refs):
    sc, xa, xb, cos, sin, normed_t, gains, second, d_middle, dq, own, *twin = refs[:13]
    refs = refs[13:]
    if chain:
        came = refs[0]
        refs = refs[1:]
    parts = refs[:pieces]
    grad_a, grad_b, mine, give, full, packed, made, sems = refs[pieces:]
    copies = load_parts(sc, 3, parts, full, sems, 0)
    rows = xa.shape[-1]
    width = full.shape[0]
    half = HEAD_DIM // 2
    for q in range(2):
        at = slice(q * rows, (q + 1) * rows)
        c, s = cos[:, at], sin[:, at]
        for h in range(HEADS):
            group, lanes = h // GROUP, slice(h % GROUP * rows, (h % GROUP + 1) * rows)
            a = dq[q, group, :half, lanes] * HEAD_DIM**-0.5
            b = dq[q, group, half:, lanes] * HEAD_DIM**-0.5
            made[64 * h : 64 * h + half, at] = (a * c + b * s).astype(BF16)
            made[64 * h + half : 64 * h + 64, at] = (b * c - a * s).astype(BF16)
        for k in range(KV_HEADS):
            both = own[q, k] + twin[q][k].astype(F32)
            if chain:
                both = both + came[q, k].astype(F32)
            both = both.T
            a, b = both[:half], both[half : 2 * half]
            row = width + 64 * k
            made[row : row + half, at] = (a * c + b * s).astype(BF16)
            made[row + half : row + 64, at] = (b * c - a * s).astype(BF16)
            made[row + 192 : row + 256, at] = both[2 * half :].astype(BF16)
    for copy in copies:
        copy.wait()
    gain = gains[:, 64:65].astype(F32)
    d_first = jnp.dot(full[:, : width + 384], made[...], preferred_element_type=F32)
    v = jnp.concatenate([xa[:width], xb[:width]], axis=1).astype(F32)
    d_v, first = norm_back(v, gain, d_first)
    d_x = (d_middle[...] + d_v).astype(BF16)
    grad_a[...] = d_x[:, :rows]
    grad_b[...] = d_x[:, rows:]
    front = dot(normed_t[...], made[...], 1, 1)
    lane = lax.broadcasted_iota(jnp.int32, (width, 64), 1)
    ends = jnp.where(lane == 0, first, second[:, :64])
    put_slabs(packed, sc, fsdp, 0, jnp.concatenate([front, ends], axis=1))
    used = (width + 448) // 128 * (width // fsdp)
    total = packed.shape[2]
    if total > used:
        packed[:, :, used:] = jnp.zeros((2, fsdp // 2, total - used, 128), BF16)
    mine[...] = packed[0]
    give[...] = packed[1]


def last(fsdp, ctx, sc, xs, cos, sin, normed_t, gains, second, d_middle, dq, dkv, parts):
    width, count = normed_t.shape
    rows = count // 2
    used = (width + 448) // 128 * (width // fsdp)
    packed = (fsdp // 2, -(-used // (16 * ctx)) * 16 * ctx, 128)
    given = (*xs, cos, sin, normed_t, gains, second, d_middle, dq, *dkv)
    out_shape = (
        jax.ShapeDtypeStruct((width, rows), BF16),
        jax.ShapeDtypeStruct((width, rows), BF16),
        jax.ShapeDtypeStruct(packed, BF16),
        jax.ShapeDtypeStruct(packed, BF16),
    )
    return pl.pallas_call(
        functools.partial(last_kernel, fsdp, len(parts), len(dkv) == 4),
        out_shape=out_shape,
        grid=(1,),
        in_specs=[SM] + wholes(*given) + [HB] * len(parts),
        out_specs=wholes(*out_shape),
        scratch_shapes=[
            pltpu.VMEM((width, parts[0].shape[1]), BF16),
            pltpu.VMEM((2,) + packed, BF16),
            pltpu.VMEM((width + 384, count), BF16),
            pltpu.SemaphoreType.DMA((len(parts),)),
        ],
        compiler_params=LIMIT,
        cost_estimate=takes(7),
    )(sc, *given, *parts)


def unpack_kernel(places, flat, *outs):
    for out, (at, rows, skip) in zip(outs, places, strict=True):
        columns = out.shape[1]
        done = 0
        while done < columns:
            slab, lane = divmod(skip + done, 128)
            n = min(128 - lane, columns - done)
            out[:, done : done + n] = flat[
                at + slab * rows : at + (slab + 1) * rows, lane : lane + n
            ].astype(F32)
            done += n


def front_unpack_kernel(places, flat, *outs):
    *outs, first, second = outs
    unpack_kernel(places, flat, *outs)
    rows = first.shape[1]
    ends = flat[7 * rows : 8 * rows].astype(F32).T
    first[...] = ends[64:65]
    second[...] = ends[65:66]


def front_unpack(flat, shard, widths):
    places = [(0, shard, sum(widths[:i])) for i in range(len(widths))]
    out_shape = tuple(jax.ShapeDtypeStruct((shard, n), F32) for n in widths)
    out_shape += (jax.ShapeDtypeStruct((1, shard), F32),) * 2
    return pl.pallas_call(
        functools.partial(front_unpack_kernel, places),
        out_shape=out_shape,
        grid=(1,),
        in_specs=wholes(flat),
        out_specs=wholes(*out_shape),
        compiler_params=LIMIT,
        cost_estimate=takes(2),
    )(flat)


def join_unpack_kernel(places, parts, sc, *refs):
    pieces, outs, flat = refs[: 2 * parts], refs[2 * parts : -1], refs[-1]
    n = pieces[0].shape[0]
    half = parts // 2
    for i, piece in enumerate(pieces):
        x = lax.rem(sc[0] + i // parts, 2)
        p = lax.rem(sc[1] + parts - i % parts, parts)
        at = lax.div(p, half) * (parts * n) + x * (half * n) + lax.rem(p, half) * n
        flat[pl.ds(pl.multiple_of(at, 16), n)] = piece[...]
    unpack_kernel(places, flat, *outs)


def unpack(flat, places):
    out_shape = tuple(jax.ShapeDtypeStruct((p[1], p[3]), F32) for p in places)
    return pl.pallas_call(
        functools.partial(unpack_kernel, [p[:3] for p in places]),
        out_shape=out_shape,
        grid=(1,),
        in_specs=wholes(flat),
        out_specs=wholes(*out_shape),
        compiler_params=LIMIT,
        cost_estimate=takes(2),
    )(flat)


def join_unpack(place, near, far, places):
    pieces = (*near, *far)
    out_shape = tuple(jax.ShapeDtypeStruct((p[1], p[3]), F32) for p in places)
    return pl.pallas_call(
        functools.partial(join_unpack_kernel, [p[:3] for p in places], len(near)),
        out_shape=out_shape,
        grid=(1,),
        in_specs=[SM] + wholes(*pieces),
        out_specs=wholes(*out_shape),
        scratch_shapes=[pltpu.VMEM((len(pieces) * near[0].shape[0], 128), BF16)],
        compiler_params=LIMIT,
        cost_estimate=takes(3),
    )(place, *pieces)


def chip_sum(mine, got, i):
    return mine[i].astype(F32) + got[i].astype(F32)


def sum_y(mine, got, send):
    total = chip_sum(mine, got, 0)
    for s in range(1, mine.shape[0]):
        total = total + send["shift"][s](chip_sum(mine, got, s).astype(BF16)).astype(F32)
    return total.astype(BF16)


def spread_kernel(got, out):
    total = got[0].astype(F32)
    for i in range(1, got.shape[0]):
        total = total + got[i].astype(F32)
    total = total.astype(BF16)
    for i in range(got.shape[0]):
        out[i] = total


def sum_kernel(got, out):
    total = got[0].astype(F32)
    for i in range(1, got.shape[0]):
        total = total + got[i].astype(F32)
    out[...] = total.astype(BF16)


def simple_call(kernel, out_shape, *given):
    return pl.pallas_call(
        kernel,
        out_shape=out_shape,
        grid=(1,),
        in_specs=wholes(*given),
        out_specs=whole(out_shape),
        compiler_params=LIMIT,
        cost_estimate=takes(0),
    )(*given)


def exchange(total, axes, size):
    parts = total.reshape(size, total.shape[0] // size, 128)
    return lax.all_to_all(parts, axes, 0, 0, tiled=True)


def spread(got):
    return simple_call(spread_kernel, jax.ShapeDtypeStruct(got.shape, BF16), got)


def gather_over(spread, axes):
    return lax.all_to_all(spread, axes, 0, 0, tiled=True).reshape(-1, 128)


def came_kernel(own, twin_a, twin_b, *refs):
    *came, out = refs
    for i, twin in enumerate((twin_a, twin_b)):
        total = own[i].astype(F32) + twin[...].astype(F32)
        for c in came:
            total = total + c[i].astype(F32)
        out[i] = total.astype(BF16)


def halves_kernel(one, one_came, two, two_came, out):
    n = one.shape[0]
    out[:n] = (one[...].astype(F32) + one_came[...].astype(F32)).astype(BF16)
    out[n:] = (two[...].astype(F32) + two_came[...].astype(F32)).astype(BF16)


def first_kernel(x, *refs):
    mine, got, (to_y, to_x) = refs[:4], refs[4:8], refs[8:]
    for i in range(4):
        out = to_y if i < 2 else to_x
        out[i % 2] = (mine[i][0].astype(F32) + got[i][0].astype(F32)).astype(BF16)


def first_sums(x, mine, got):
    n = mine.shape[1] // 4
    block = (1, n, 128)
    places = [
        lambda i, x: (1, 0, 0),
        lambda i, x: (1, 1, 0),
        lambda i, x: (0, 3 - x[0], 0),
        lambda i, x: (1, 3 - x[0], 0),
    ]
    out = pl.BlockSpec((2, n, 128), lambda i, x: (0, 0, 0))
    return pl.pallas_call(
        first_kernel,
        out_shape=(jax.ShapeDtypeStruct((2, n, 128), BF16),) * 2,
        grid_spec=pltpu.PrefetchScalarGridSpec(
            num_scalar_prefetch=1,
            grid=(1,),
            in_specs=[pl.BlockSpec(block, at) for at in places] * 2,
            out_specs=[out, out],
        ),
        compiler_params=LIMIT,
        cost_estimate=takes(0),
    )(x, *[mine] * 4, *[got] * 4)


def second_kernel(x, *refs):
    mine, got, came, outs = refs[:4], refs[4:8], refs[8:12], refs[12:]
    for i in range(4):
        total = mine[i][0].astype(F32) + got[i][0].astype(F32) + came[i][0].astype(F32)
        outs[i][...] = total.astype(BF16)


def second_sums(x, mine, got, came_y, came_x):
    n = mine.shape[1] // 4
    block = (1, n, 128)
    own = [
        lambda i, x: (0, 1 - x[0], 0),
        lambda i, x: (0, x[0], 0),
        lambda i, x: (1, 2 + x[0], 0),
        lambda i, x: (0, 2 + x[0], 0),
    ]
    came = [
        lambda i, x: (1 - x[0], 0, 0),
        lambda i, x: (x[0], 0, 0),
        lambda i, x: (1, 0, 0),
        lambda i, x: (0, 0, 0),
    ]
    return pl.pallas_call(
        second_kernel,
        out_shape=(jax.ShapeDtypeStruct((n, 128), BF16),) * 4,
        grid_spec=pltpu.PrefetchScalarGridSpec(
            num_scalar_prefetch=1,
            grid=(1,),
            in_specs=[pl.BlockSpec(block, at) for at in own + own + came],
            out_specs=[pl.BlockSpec((n, 128), lambda i, x: (0, 0))] * 4,
        ),
        compiler_params=LIMIT,
        cost_estimate=takes(0),
    )(x, *[mine] * 4, *[got] * 4, came_y, came_y, came_x, came_x)


def gather_y(own, send, fsdp):
    return [own] + [send["shift"][s](own) for s in range(1, fsdp // 2)]


def gather_pieces(got, send, fsdp, core, y, join, dim):
    pieces = got + [send["core"](g) for g in got]
    own = got[0]
    if not join:
        return pieces
    buffer = jnp.zeros((fsdp,) + own.shape, own.dtype)
    for piece, f in zip(pieces, piece_order(fsdp, core, y), strict=True):
        buffer = lax.dynamic_update_index_in_dim(buffer, piece, f, 0)
    if dim:
        buffer = buffer.swapaxes(0, 1)
        return [buffer.reshape(own.shape[0], fsdp * own.shape[1])]
    return [buffer.reshape(fsdp * own.shape[0], own.shape[1])]


def piece_order(fsdp, core, y):
    ys = fsdp // 2
    source = [lax.rem(y - s + ys, ys) * 2 for s in range(ys)]
    return [f + core for f in source] + [f + 1 - core for f in source]


def body(
    fsdp,
    ctx,
    tokens,
    segment_ids,
    positions,
    cotangent,
    norm_first,
    query_weight,
    key_weight,
    value_weight,
    output_weight,
    norm_second,
    gate_weight,
    up_weight,
    down_weight,
):
    send = make_send(fsdp, ctx)
    ys, hs = fsdp // 2, ctx // 2
    _, count, width = tokens.shape
    rows = count // 2
    kv_width = KV_HEADS * HEAD_DIM
    y, core = lax.axis_index("y"), lax.axis_index("core")
    h, x = lax.axis_index("h"), lax.axis_index("x")
    ci = 2 * h + x
    reach = min(hs - 1, -(-(-(-(DOC_MOST - 1) // rows)) // 4))
    order = jnp.stack([core, y, 4 * h] + piece_order(fsdp, core, y)).astype(jnp.int32)
    shard = gate_weight.shape[0]
    join = shard % 16 != 0
    x_pair = prepare(2 * count * h + count * x, h, tokens.reshape(count, width).T, positions)
    *pair, query_weight, norm_first, norm_second = tie(
        *x_pair, query_weight, norm_first, norm_second
    )
    xs = send_home(send, pair)
    packed = jnp.concatenate(
        [
            query_weight,
            key_weight,
            value_weight,
            norm_first[:, None],
            norm_second[:, None],
            jnp.zeros((shard, 62), BF16),
        ],
        axis=1,
    )
    first_parts = gather_y(packed, send, fsdp)
    first_parts = gather_pieces(first_parts, send, fsdp, core, y, join, 0)
    cot_t, _ = tie(cotangent.reshape(count, width).T, first_parts[-1])
    cots = send_home(send, pick_home(cot_t, h))
    pos_f = jnp.concatenate([a[width : width + 2] for a in xs], axis=1).astype(F32)
    pos_f = pos_f[0:1] * 64.0 + pos_f[1:2]
    frequency = jnp.exp(
        jnp.arange(HEAD_DIM // 2, dtype=F32) * (-math.log(10000.0) * 2.0 / HEAD_DIM)
    )
    angle = frequency[:, None] * pos_f
    cos, sin = jnp.cos(angle), jnp.sin(angle)
    feed_own = jnp.concatenate([gate_weight, up_weight, output_weight], axis=1)
    feed_own, down_own, _ = tie(feed_own, down_weight.T, first_parts[-1])
    feed_got = gather_y(feed_own, send, fsdp)
    down_got = gather_y(down_own, send, fsdp)
    feed_got[0], *xs = tie(feed_got[0], *xs)
    qz, kv, normed_t, gains, pos, ids = project(order, xs, cos, sin, first_parts)

    stages = []
    carried = None
    for s in range(reach + 1):
        stages.append((kv, send["core"](kv)))
        if s < reach:
            kv = send["up"](kv)
        carried = attend_forward(s, ids, pos, qz, stages[s], carried, s == reach)
        if s < reach:
            kv, *carried = tie(kv, *carried)
    mixed, lse = carried
    feed_parts = gather_pieces(feed_got, send, fsdp, core, y, join, 0)
    down_parts = gather_pieces(down_got, send, fsdp, core, y, join, 1)
    res_a, res_b, d_middle, gz, delta, mine, give, second = feed(
        fsdp, ctx, order, xs, cots, mixed, gains, feed_parts, down_parts
    )

    got = send["core"](give)
    crossed = ys == 2
    x_ref = x.astype(jnp.int32).reshape(1)
    dq = None
    came = None
    for s in range(reach, -1, -1):
        sc = ids
        if s == reach - 1 and crossed:
            first_y, first_x = first_sums(x_ref, mine, got)
            sc, first_y, first_x = tie(sc, first_y, first_x)
            came_y, came_x = send["shift"][1](first_y), send["across"](first_x)
        if s == 0 and crossed:
            came_y, came_x, dq = tie(came_y, came_x, dq)
            give_one, keep_one, give_two, keep_two = second_sums(x_ref, mine, got, came_y, came_x)
            sc, give_one, give_two = tie(sc, give_one, give_two)
            came_one, came_two = send["across"](give_one), send["shift"][1](give_two)
        if came is not None:
            sc, came = tie(sc, came)
            came = send["down"](came)
        dq, own, *other = attend_backward(
            s, sc, pos, qz, gz, lse, delta, stages[s], dq, F32 if s == 0 else BF16
        )
        twin = tuple(send["core"](o) for o in other)
        if s > 0:
            if s == reach - 1:
                *twin, came, dq, res_a, res_b = tie(*twin, came, dq, *result)
            elif s < reach:
                *twin, came, dq = tie(*twin, came, dq)
            given = (own, *twin) if came is None else (own, *twin, came)
            came = simple_call(came_kernel, jax.ShapeDtypeStruct(own.shape, BF16), *given)
            if s == reach:
                came, res_a, res_b = tie(came, res_a, res_b)
                result = send_back(send, res_a, res_b)
    dkv = (own, *twin) if came is None else (own, *twin, came)
    if crossed:
        late = simple_call(
            halves_kernel,
            jax.ShapeDtypeStruct((mine.shape[1] // 2, 128), BF16),
            keep_one,
            came_one,
            keep_two,
            came_two,
        )
        late, dq = tie(late, dq)
        late = exchange(late, ("h",), hs)
    else:
        late = exchange(sum_y(mine, got, send), CTX, ctx)
    tok_a, tok_b, mine_front, give_front = last(
        fsdp, ctx, order, xs, cos, sin, normed_t, gains, second, d_middle, dq, dkv, first_parts
    )
    got_front = send["core"](give_front)
    late, got_front = tie(late, got_front)
    front = sum_y(mine_front, got_front, send)
    if crossed:
        piece = simple_call(sum_kernel, jax.ShapeDtypeStruct(late.shape[1:], BF16), late)
        near = [piece] + [send["around"][s](piece) for s in range(1, hs)]
        far = [send["across"](p) for p in near]
        *near, tok_a, tok_b = tie(*near, tok_a, tok_b)
    else:
        late = gather_over(spread(late), CTX)
    front = spread(exchange(front, CTX, ctx))
    front = gather_over(front, CTX)
    tokens_grad = send_back(send, tok_a, tok_b)

    ff = gate_weight.shape[1]
    down_shard = down_weight.shape[0]
    gate_rows, out_rows = ff // 128 * shard, -(-width // 128) * shard
    places = [
        (0, shard, 0, ff),
        (gate_rows, shard, 0, ff),
        (2 * gate_rows, shard, 0, width),
        (2 * gate_rows + out_rows, width, 0, down_shard),
    ]
    if crossed:
        late_grads = join_unpack(jnp.stack([x, h]).astype(jnp.int32), near, far, places)
    else:
        late_grads = unpack(late, places)
    gate_grad, up_grad, output_grad, down_grad = late_grads
    query_grad, key_grad, value_grad, first_grad, second_grad = front_unpack(
        front, shard, (width, kv_width, kv_width)
    )
    return (
        low_high(res_a, res_b, h).T[None],
        low_high(*tokens_grad, h).T[None],
        first_grad[0],
        query_grad,
        key_grad,
        value_grad,
        output_grad,
        second_grad[0],
        gate_grad,
        up_grad,
        down_grad.T,
    )


def solution(mesh):
    fsdp, ctx = mesh.shape["fsdp"], mesh.shape["ctx"]
    places = Mesh(mesh.devices.reshape(fsdp // 2, 2, ctx // 2, 2), AXES)
    owner = ("y", "core")
    flat, split = P(owner), P(owner, None)
    whole = P(owner, CTX, None)
    return jax.shard_map(
        functools.partial(body, fsdp, ctx),
        mesh=places,
        in_specs=(whole, split, split, whole, flat, split, split, split, split, flat, split, split, split),
        out_specs=(whole, whole, flat, split, split, split, split, flat, split, split, split),
        check_vma=False,
    )
```

```python
import functools
import math

import jax
import jax.numpy as jnp
from jax import lax
from jax.experimental import pallas as pl
from jax.experimental.pallas import tpu as pltpu
from jax.sharding import Mesh
from jax.sharding import PartitionSpec as P

HEADS = 9
KV_HEADS = 3
GROUP = HEADS // KV_HEADS
HEAD_DIM = 64
EPSILON = 1e-05
MASKED = -1e30
DOC_MOST = 2000
AXES = ("y", "core", "h", "x")
CTX = ("h", "x")
F32 = jnp.float32
BF16 = jnp.bfloat16


def moves(fsdp, ctx, step):
    pairs = []
    for f in range(fsdp):
        for c in range(ctx):
            to = step(f // 2, f % 2, c // 2, c % 2)
            if to is not None:
                y, core, h, x = to
                pairs.append((f * ctx + c, (2 * y + core) * ctx + 2 * h + x))
    return pairs


def make_send(fsdp, ctx):
    ys, hs, blocks = fsdp // 2, ctx // 2, 2 * ctx

    def along(pairs):
        return lambda a: lax.ppermute(a, AXES, pairs)

    def by(step):
        return along(moves(fsdp, ctx, step))

    def home(slot):
        def step(y, core, h, x):
            low = 2 * h + x
            block = low if h % 2 == slot else blocks - 1 - low
            return (y, int(block % 4 in (1, 2)), block // 4, core)

        return moves(fsdp, ctx, step)

    def back(pairs):
        return along([(b, a) for a, b in pairs])

    return dict(
        home=[along(home(0)), along(home(1))],
        back=[back(home(0)), back(home(1))],
        core=by(lambda y, k, h, x: (y, 1 - k, h, x)),
        across=by(lambda y, k, h, x: (y, k, h, 1 - x)),
        up=by(lambda y, k, h, x: (y, k, h + 1, x) if h + 1 < hs else None),
        down=by(lambda y, k, h, x: (y, k, h - 1, x) if h > 0 else None),
        around=[by(lambda y, k, h, x, s=s: (y, k, (h + s) % hs, x)) for s in range(hs)],
        shift=[by(lambda y, k, h, x, s=s: ((y + s) % ys, k, h, x)) for s in range(ys)],
    )


def pick_home(a, h):
    r = a.shape[1] // 2
    low, high = a[:, :r], a[:, r:]
    even = lax.rem(h, 2) == 0
    return jnp.where(even, low, high), jnp.where(even, high, low)


def send_home(send, pair):
    return send["home"][0](pair[0]), send["home"][1](pair[1])


def send_back(send, a, b):
    return send["back"][0](a), send["back"][1](b)


def low_high(a, b, h):
    even = lax.rem(h, 2) == 0
    return jnp.concatenate([jnp.where(even, a, b), jnp.where(even, b, a)], axis=1)


def tie(*values):
    return lax.optimization_barrier(values)


def bias_of(begin, place, block_id, keys, rows):
    key_place = block_id * keys + lax.broadcasted_iota(jnp.int32, (keys, rows), 0)
    seen = (key_place >= begin) & (key_place <= place)
    return jnp.where(seen, 0.0, MASKED)


def dot(left, right, left_dim, right_dim):
    return lax.dot_general(
        left, right, (((left_dim,), (right_dim,)), ((), ())), preferred_element_type=F32
    )


def load_blocks(pieces, held):
    held[:2] = pieces[0][...]
    held[2:] = pieces[1][...]


def each_pair(sc, stage, work):
    base, core = sc[4] - 4 * stage, sc[5]

    def step(i, _):
        q = lax.div(i, 4)
        k = lax.rem(i, 4)
        within = jnp.where(k < 2, core, 1 - core)
        block_id = base + jnp.where(lax.rem(k, 2) == 0, within, 3 - within)

        @pl.when((block_id >= sc[2 + q]) & (block_id <= sc[q]))
        def _():
            work(q, k, block_id)

        return 0

    lax.fori_loop(0, 8, step, 0)


def forward_kernel(stage, last, *refs):
    first = stage == 0
    refs = list(refs)
    sc, pos, qz = refs[:3]
    kv = refs[3:5]
    refs = refs[5:]
    if not first:
        peak_in, total_in, mix_in = refs[:3]
        refs = refs[3:]
    if last:
        out, lse = refs[:2]
        held, bias, peak, total, mix = refs[2:]
    else:
        peak, total, mix = refs[:3]
        held, bias = refs[3:]
    rows = pos.shape[-1]
    if first:
        peak[...] = jnp.full(peak.shape, MASKED, F32)
        total[...] = jnp.zeros(total.shape, F32)
        mix[...] = jnp.zeros(mix.shape, F32)
    else:
        peak[...] = peak_in[...]
        total[...] = total_in[...]
        mix[...] = mix_in[...]
    load_blocks(kv, held)

    def work(q, k, block_id):
        place = sc[q] * rows + lax.broadcasted_iota(jnp.int32, (1, rows), 1)
        bias[...] = bias_of(place - pos[q], place, block_id, rows, rows)
        for c in range(KV_HEADS):
            seen = dot(held[k, c, :, :HEAD_DIM], qz[q, c], 1, 0) + jnp.concatenate([bias[...]] * GROUP, axis=1)
            old = peak[q, c]
            new = jnp.maximum(old, jnp.max(seen, axis=0, keepdims=True))
            expo = jnp.exp(seen - new)
            fade = jnp.exp(old - new)
            peak[q, c] = new
            total[q, c] = total[q, c] * fade + jnp.sum(expo, axis=0, keepdims=True)
            values = held[k, c].T[HEAD_DIM:]
            mix[q, c] = mix[q, c] * fade + dot(values, expo.astype(BF16), 1, 0)

    each_pair(sc, stage, work)
    if last:
        lse[...] = peak[...] + jnp.log(total[...])
        for q in range(2):
            for c in range(KV_HEADS):
                out[q, c] = (mix[q, c] / total[q, c]).astype(BF16)


def backward_kernel(stage, first, own_type, *refs):
    refs = list(refs)
    sc, pos, qz, gz, lse, delta = refs[:6]
    kv = refs[6:8]
    refs = refs[8:]
    if not first:
        dq_in = refs[0]
        refs = refs[1:]
    dq, own, other_a, other_b, held, bias, dkv = refs
    rows = pos.shape[-1]
    if first:
        dq[...] = jnp.zeros(dq.shape, F32)
    else:
        dq[...] = dq_in[...]
    load_blocks(kv, held)
    dkv[...] = jnp.zeros(dkv.shape, F32)

    def work(q, k, block_id):
        place = sc[q] * rows + lax.broadcasted_iota(jnp.int32, (1, rows), 1)
        bias[...] = bias_of(place - pos[q], place, block_id, rows, rows)
        for c in range(KV_HEADS):
            block = held[k, c]
            keys, values = block[:, :HEAD_DIM], block[:, HEAD_DIM:]
            seen = dot(keys, qz[q, c], 1, 0) + jnp.concatenate([bias[...]] * GROUP, axis=1)
            probs = jnp.exp(seen - lse[q, c])
            d_scores = (probs * (dot(values, gz[q, c], 1, 0) - delta[q, c])).astype(BF16)
            d_both = [dot(d_scores, qz[q, c], 1, 1), dot(probs.astype(BF16), gz[q, c], 1, 1)]
            dkv[k, c] += jnp.concatenate(d_both, axis=1)
            dq[q, c] += dot(block.T[:HEAD_DIM], d_scores, 1, 0)

    each_pair(sc, stage, work)
    own[...] = dkv[:2].astype(own_type)
    other_a[...] = dkv[2].astype(BF16)
    other_b[...] = dkv[3].astype(BF16)


SM = pl.BlockSpec(memory_space=pltpu.SMEM)
HB = pl.BlockSpec(memory_space=pl.ANY)


def whole(a):
    return pl.BlockSpec(
        a.shape, lambda i: (0,) * len(a.shape), pipeline_mode=pl.Buffered(buffer_count=1)
    )


def wholes(*arrays):
    return [whole(a) for a in arrays]


def takes(us):
    return pl.CostEstimate(flops=int(us * 1.15e9), bytes_accessed=0, transcendentals=0)


LIMIT = pltpu.CompilerParams(vmem_limit_bytes=64 << 20)


def attend_forward(stage, sc, pos, qz, pieces, carried, last):
    rows = pos.shape[-1]
    blocks = 4
    first = carried is None
    stat = jax.ShapeDtypeStruct((2, KV_HEADS, 1, GROUP * rows), F32)
    mix = jax.ShapeDtypeStruct((2, KV_HEADS, HEAD_DIM, GROUP * rows), F32)
    scratch = [
        pltpu.VMEM((blocks, KV_HEADS, rows, 2 * HEAD_DIM), BF16),
        pltpu.VMEM((rows, rows), F32),
    ]
    if last:
        out_shape = (jax.ShapeDtypeStruct(mix.shape, BF16), stat)
        scratch += [pltpu.VMEM(s.shape, F32) for s in (stat, stat, mix)]
        aliases = {}
    else:
        out_shape = (stat, stat, mix)
        aliases = {} if first else {3 + len(pieces) + i: i for i in range(3)}
    given = (sc, pos, qz, *pieces) + (() if first else tuple(carried))
    pairs = blocks * HEADS * rows * rows
    return pl.pallas_call(
        functools.partial(forward_kernel, stage, last),
        out_shape=out_shape,
        grid=(1,),
        in_specs=[SM] + wholes(*given[1:]),
        out_specs=wholes(*out_shape),
        scratch_shapes=scratch,
        input_output_aliases=aliases,
        compiler_params=LIMIT,
        cost_estimate=takes(0),
    )(*given)


def attend_backward(stage, sc, pos, qz, gz, lse, delta, pieces, dq, own_type):
    rows = pos.shape[-1]
    blocks = 4
    first = dq is None
    wide = (KV_HEADS, rows, 2 * HEAD_DIM)
    given = (sc, pos, qz, gz, lse, delta, *pieces) + (() if first else (dq,))
    pairs = blocks * HEADS * rows * rows
    out_shape = (
        jax.ShapeDtypeStruct((2, KV_HEADS, HEAD_DIM, GROUP * rows), F32),
        jax.ShapeDtypeStruct((blocks // 2,) + wide, own_type),
        jax.ShapeDtypeStruct(wide, BF16),
        jax.ShapeDtypeStruct(wide, BF16),
    )
    return pl.pallas_call(
        functools.partial(backward_kernel, stage, first, own_type),
        out_shape=out_shape,
        grid=(1,),
        in_specs=[SM] + wholes(*given[1:]),
        out_specs=wholes(*out_shape),
        scratch_shapes=[
            pltpu.VMEM((blocks,) + wide, BF16),
            pltpu.VMEM((rows, rows), F32),
            pltpu.VMEM((blocks,) + wide, F32),
        ],
        input_output_aliases={} if first else {len(given) - 1: 0},
        compiler_params=LIMIT,
        cost_estimate=takes((12, 14)[stage] if stage < 2 else 4),
    )(*given)


def load_parts(sc, at, pieces, full, sems, dim):
    size = pieces[0].shape[dim]
    copies = []
    for i, piece in enumerate(pieces):
        if len(pieces) == 1:
            to = full
        elif dim == 0:
            to = full.at[pl.ds(pl.multiple_of(sc[at + i] * size, 16), size)]
        else:
            to = full.at[:, pl.ds(pl.multiple_of(sc[at + i] * size, 128), size)]
        copies.append(pltpu.make_async_copy(piece, to, sems.at[i]))
    for copy in copies:
        copy.start()
    return copies


def norm_scale(v):
    return lax.rsqrt(jnp.mean(v * v, axis=0, keepdims=True) + EPSILON)


def prepare_kernel(sc, tokens, positions, query, key, value, gains, first, second, packed):
    ends = jnp.concatenate([gains[...], jnp.zeros((56, gains.shape[1]), F32)], axis=0).T
    packed[...] = jnp.concatenate([query[...], key[...], value[...], ends.astype(BF16)], axis=1)
    width, count = tokens.shape
    rows = count // 2
    p = positions[:, pl.ds(pl.multiple_of(sc[0], 128), count)]
    row = lax.broadcasted_iota(jnp.int32, (16, count), 0)
    p = jnp.where(row == 0, p >> 6, jnp.where(row == 1, p & 63, 0)).astype(F32).astype(BF16)
    for parity in range(2):

        @pl.when(sc[1] == parity)
        def _(parity=parity):
            for half, out in enumerate((first, second)):
                half = half ^ parity
                out[:width] = tokens[:, half * rows : (half + 1) * rows]
                out[width:] = p[:, half * rows : (half + 1) * rows]


def prepare(at, h, tokens, positions, query, key, value, gains):
    width, count = tokens.shape
    out = jax.ShapeDtypeStruct((width + 16, count // 2), BF16)
    given = (tokens, positions, query, key, value, gains)
    columns = sum(w.shape[1] for w in (query, key, value)) + 64
    packed = jax.ShapeDtypeStruct((query.shape[0], columns), BF16)
    sc = jnp.stack([at, lax.rem(h, 2)]).astype(jnp.int32)
    return pl.pallas_call(
        prepare_kernel,
        out_shape=(out, out, packed),
        grid=(1,),
        in_specs=[SM] + wholes(*given),
        out_specs=wholes(out, out, packed),
        compiler_params=LIMIT,
        cost_estimate=takes(2),
    )(sc, *given)


def project_kernel(pieces, *refs):
    sc, xa, xb, cos, sin = refs[:5]
    parts = refs[5 : 5 + pieces]
    qz, kv, normed_t, gains, pos, ids, full, sems = refs[5 + pieces :]
    copies = load_parts(sc, 3, parts, full, sems, 0)
    rows = xa.shape[-1]
    width = full.shape[0]
    for q, x in enumerate((xa, xb)):
        p = x[width : width + 16].astype(F32)
        p = p[0:1] * 64.0 + p[1:2]
        pos[q] = p.astype(jnp.int32)
        block = sc[2] + (sc[0] if q == 0 else 3 - sc[0])
        lane = lax.broadcasted_iota(jnp.int32, (1, rows), 1).astype(F32)
        begin = block * rows + jnp.min(lane - p).astype(jnp.int32)
        ids[q] = block
        ids[2 + q] = lax.div(begin, rows)
    ids[4] = sc[2]
    ids[5] = sc[0]
    flat = [x[:width].astype(F32) for x in (xa, xb)]
    scaled = [v * norm_scale(v) for v in flat]
    for copy in copies:
        copy.wait()
    gains[...] = full[:, width + 320 : width + 448]
    gain = full[:, width + 384 : width + 385].astype(F32)
    half = HEAD_DIM // 2
    for q in range(2):
        normed = (scaled[q] * gain).astype(BF16)
        at = slice(q * rows, (q + 1) * rows)
        normed_t[:, at] = normed
        made = jnp.dot(normed.T, full[:, : width + 384], preferred_element_type=F32).T
        c, s = cos[:, at], sin[:, at]
        for h in range(HEADS):
            a = made[64 * h : 64 * h + half]
            b = made[64 * h + half : 64 * h + 64]
            ra = (a * c - b * s).astype(BF16) * jnp.asarray(HEAD_DIM**-0.5, BF16)
            rb = (b * c + a * s).astype(BF16) * jnp.asarray(HEAD_DIM**-0.5, BF16)
            group, lanes = h // GROUP, slice(h % GROUP * rows, (h % GROUP + 1) * rows)
            qz[q, group, :half, lanes] = ra
            qz[q, group, half:, lanes] = rb
        for k in range(KV_HEADS):
            row = width + 64 * k
            a = made[row : row + half]
            b = made[row + half : row + 64]
            ra = (a * c - b * s).astype(BF16)
            rb = (b * c + a * s).astype(BF16)
            v = made[row + 192 : row + 256].astype(BF16)
            kv[q, k] = jnp.concatenate([ra, rb, v], axis=0).T


def project(sc, xs, cos, sin, parts):
    rows = xs[0].shape[1]
    count = 2 * rows
    width = HEADS * HEAD_DIM
    out_shape = (
        jax.ShapeDtypeStruct((2, KV_HEADS, HEAD_DIM, GROUP * rows), BF16),
        jax.ShapeDtypeStruct((2, KV_HEADS, rows, 2 * HEAD_DIM), BF16),
        jax.ShapeDtypeStruct((width, count), BF16),
        jax.ShapeDtypeStruct((width, 128), BF16),
        jax.ShapeDtypeStruct((2, 1, rows), jnp.int32),
        jax.ShapeDtypeStruct((8,), jnp.int32),
    )
    return pl.pallas_call(
        functools.partial(project_kernel, len(parts)),
        out_shape=out_shape,
        grid=(1,),
        in_specs=[SM] + wholes(*xs, cos, sin) + [HB] * len(parts),
        out_specs=wholes(*out_shape[:-1]) + [SM],
        scratch_shapes=[
            pltpu.VMEM((width, parts[0].shape[1]), BF16),
            pltpu.SemaphoreType.DMA((len(parts),)),
        ],
        compiler_params=LIMIT,
        cost_estimate=takes(0),
    )(sc, *xs, cos, sin, *parts)


def wide(value):
    over = -value.shape[1] % 128
    if not over:
        return value
    return jnp.concatenate([value, jnp.zeros((value.shape[0], over), value.dtype)], axis=1)


def slot_of(sc, fsdp, f):
    ys = fsdp // 2
    return lax.rem(f + sc[0], 2), lax.rem(lax.div(f, 2) - sc[1] + ys, ys)


def put_slabs(packed, sc, fsdp, at, value):
    value = wide(value).astype(BF16)
    r = value.shape[0] // fsdp
    for f in range(fsdp):
        k, y = slot_of(sc, fsdp, f)
        for s in range(value.shape[1] // 128):
            packed[k, y, pl.ds(at + s * r, r)] = value[
                f * r : (f + 1) * r, s * 128 : (s + 1) * 128
            ]


def norm_back(v, gain, grad):
    r = norm_scale(v)
    scaled = grad * gain
    d_v = r * scaled - v * (r * r * r * jnp.mean(scaled * v, axis=0, keepdims=True))
    return d_v, jnp.sum(grad * (v * r), axis=1, keepdims=True)


def feed_kernel(fsdp, pieces, chunk, *refs):
    sc, xa, xb, ca, cb, mix, gains = refs[:7]
    parts = refs[7 : 7 + pieces]
    downs = refs[7 + pieces : 7 + 2 * pieces]
    refs = refs[7 + 2 * pieces :]
    res_a, res_b, d_middle, gz, delta, mine, give, second = refs[:8]
    full, out_w, down, packed, att_t, mid, n2, n2_t, res, d_second, cot_t, cot = refs[8:20]
    sems, out_sems, down_sems, grad_sems = refs[20:]
    ff = down.shape[1]
    out_copies = load_parts(sc, 3, [p.at[:, 2 * ff :] for p in parts], out_w, out_sems, 0)
    copies = load_parts(sc, 3, [p.at[:, : 2 * ff] for p in parts], full, sems, 0)
    down_copies = load_parts(sc, 3, downs, down, down_sems, 1)
    rows = xa.shape[-1]
    width, ff = down.shape
    shard = width // fsdp
    down_shard = ff // fsdp
    for q, c in enumerate((ca, cb)):
        cot_t[:, q * rows : (q + 1) * rows] = c[...]
        for h in range(HEADS):
            att_t[64 * h : 64 * h + 64, q * rows : (q + 1) * rows] = mix[
                q, h // GROUP, :, h % GROUP * rows : (h % GROUP + 1) * rows
            ]
    cot[...] = cot_t[...].T
    gain = gains[:, 65:66].astype(F32)
    for copy in out_copies:
        copy.wait()
    branch_t = jnp.dot(out_w[...].T, att_t[...], preferred_element_type=F32)
    for q, x in enumerate((xa, xb)):
        at = slice(q * rows, (q + 1) * rows)
        mid[:, at] = x[:width].astype(F32) + branch_t[:, at]
    n2_t[...] = (mid[...] * norm_scale(mid[...]) * gain).astype(BF16)
    n2[...] = n2_t[...].T
    res[...] = mid[...]
    d_second[...] = jnp.zeros(d_second.shape, F32)
    for copy in copies + down_copies:
        copy.wait()
    up_at = ff // 128 * shard
    out_at = 2 * up_at
    down_at = out_at + -(-width // 128) * shard
    used = down_at + -(-down_shard // 128) * width
    rows_all = packed.shape[2]
    if rows_all > used:
        packed[:, :, used:] = jnp.zeros((2, fsdp // 2, rows_all - used, 128), BF16)

    sends = []

    def send(at, n):
        for k, to in enumerate((mine, give)):
            span = pl.ds(at, n)
            copy = pltpu.make_async_copy(
                packed.at[k, :, span], to.at[:, span], grad_sems.at[len(sends)]
            )
            copy.start()
            sends.append(copy)

    for j in range(ff // chunk):
        cols = slice(j * chunk, (j + 1) * chunk)
        up_cols = slice(ff + j * chunk, ff + (j + 1) * chunk)
        gate_w, up_w, down_w = full[:, cols], full[:, up_cols], down[:, cols]
        gate = jnp.dot(n2[...], gate_w, preferred_element_type=F32)
        up = jnp.dot(n2[...], up_w, preferred_element_type=F32)
        sig = 1.0 / (1.0 + jnp.exp(-gate))
        silu = gate * sig
        hidden = (silu * up).astype(BF16)
        res[...] += dot(down_w, hidden, 1, 1)
        d_hidden = jnp.dot(cot[...], down_w, preferred_element_type=F32)
        d_gate = (d_hidden * up * (sig * (1.0 + gate * (1.0 - sig)))).astype(BF16)
        d_up = (d_hidden * silu).astype(BF16)
        d_second[...] += dot(gate_w, d_gate, 1, 1) + dot(up_w, d_up, 1, 1)
        slab = j * (chunk // 128) * shard
        put_slabs(packed, sc, fsdp, slab, jnp.dot(n2_t[...], d_gate, preferred_element_type=F32))
        put_slabs(
            packed, sc, fsdp, up_at + slab, jnp.dot(n2_t[...], d_up, preferred_element_type=F32)
        )
        down_g = jnp.dot(cot_t[...], hidden, preferred_element_type=F32).astype(BF16)
        if down_shard % 128:
            for n in range(chunk // down_shard):
                slot_k, slot_y = slot_of(sc, fsdp, j * (chunk // down_shard) + n)
                part = wide(down_g[:, n * down_shard : (n + 1) * down_shard])
                for s in range(part.shape[1] // 128):
                    packed[slot_k, slot_y, down_at + s * width : down_at + (s + 1) * width] = part[
                        :, s * 128 : (s + 1) * 128
                    ]
        else:
            for n in range(chunk // 128):
                slab = j * (chunk // 128) + n
                slot_k, slot_y = slot_of(sc, fsdp, slab // (down_shard // 128))
                at = down_at + slab % (down_shard // 128) * width
                packed[slot_k, slot_y, at : at + width] = down_g[:, n * 128 : (n + 1) * 128]
        send(j * (chunk // 128) * shard, chunk // 128 * shard)
        send(up_at + j * (chunk // 128) * shard, chunk // 128 * shard)

    send(down_at, rows_all - down_at)
    res_a[...] = res[:, :rows].astype(BF16)
    res_b[...] = res[:, rows:].astype(BF16)
    d_v, gain_grad = norm_back(mid[...], gain, d_second[...])
    second[...] = jnp.broadcast_to(gain_grad, second.shape)
    d_mid = cot_t[...].astype(F32) + d_v
    d_middle[...] = d_mid
    branch = d_mid.astype(BF16)
    put_slabs(packed, sc, fsdp, out_at, dot(att_t[...], branch, 1, 1))
    send(out_at, down_at - out_at)
    d_mix = jnp.dot(out_w[...], branch, preferred_element_type=F32).astype(BF16)
    for q in range(2):
        for h in range(HEADS):
            at = slice(q * rows, (q + 1) * rows)
            part = d_mix[64 * h : 64 * h + 64, at]
            group, lanes = h // GROUP, slice(h % GROUP * rows, (h % GROUP + 1) * rows)
            gz[q, group, :, lanes] = part
            delta[q, group, :, lanes] = jnp.sum(
                part.astype(F32) * att_t[64 * h : 64 * h + 64, at].astype(F32),
                axis=0,
                keepdims=True,
            )
    for copy in sends:
        copy.wait()


def feed_rows(fsdp, ctx, width, ff):
    used = (2 * (ff // 128) + -(-width // 128)) * (width // fsdp) + -(-(ff // fsdp) // 128) * width
    return -(-used // (16 * ctx)) * 16 * ctx


def feed(fsdp, ctx, sc, xs, cots, mix, gains, parts, downs):
    rows = cots[0].shape[1]
    width = cots[0].shape[0]
    count = 2 * rows
    ff = downs[0].shape[1] * len(downs)
    packed = (fsdp // 2, feed_rows(fsdp, ctx, width, ff), 128)
    out_shape = (
        jax.ShapeDtypeStruct((width, rows), BF16),
        jax.ShapeDtypeStruct((width, rows), BF16),
        jax.ShapeDtypeStruct((width, count), F32),
        jax.ShapeDtypeStruct((2, KV_HEADS, HEAD_DIM, GROUP * rows), BF16),
        jax.ShapeDtypeStruct((2, KV_HEADS, 1, GROUP * rows), F32),
        jax.ShapeDtypeStruct(packed, BF16),
        jax.ShapeDtypeStruct(packed, BF16),
        jax.ShapeDtypeStruct((width, 128), F32),
    )
    return pl.pallas_call(
        functools.partial(feed_kernel, fsdp, len(parts), ff // 4 if ff // fsdp % 128 else ff // 3),
        out_shape=out_shape,
        grid=(1,),
        in_specs=[SM] + wholes(*xs, *cots, mix, gains) + [HB] * (2 * len(parts)),
        out_specs=wholes(*out_shape[:5]) + [HB, HB] + wholes(out_shape[7]),
        scratch_shapes=[
            pltpu.VMEM((width, 2 * ff), BF16),
            pltpu.VMEM((width, width), BF16),
            pltpu.VMEM((width, ff), BF16),
            pltpu.VMEM((2,) + packed, BF16),
            pltpu.VMEM((width, count), BF16),
            pltpu.VMEM((width, count), F32),
            pltpu.VMEM((count, width), BF16),
            pltpu.VMEM((width, count), BF16),
            pltpu.VMEM((width, count), F32),
            pltpu.VMEM((width, count), F32),
            pltpu.VMEM((width, count), BF16),
            pltpu.VMEM((count, width), BF16),
            pltpu.SemaphoreType.DMA((len(parts),)),
            pltpu.SemaphoreType.DMA((len(parts),)),
            pltpu.SemaphoreType.DMA((len(parts),)),
            pltpu.SemaphoreType.DMA((24,)),
        ],
        compiler_params=LIMIT,
        cost_estimate=takes(19),
    )(sc, *xs, *cots, mix, gains, *parts, *downs)


def last_kernel(fsdp, pieces, chain, *refs):
    sc, xa, xb, cos, sin, normed_t, gains, second, d_middle, dq, own, *twin = refs[:13]
    refs = refs[13:]
    if chain:
        came = refs[0]
        refs = refs[1:]
    parts = refs[:pieces]
    grad_a, grad_b, mine, give, full, packed, made, sems = refs[pieces:]
    copies = load_parts(sc, 3, parts, full, sems, 0)
    rows = xa.shape[-1]
    width = full.shape[0]
    half = HEAD_DIM // 2
    for q in range(2):
        at = slice(q * rows, (q + 1) * rows)
        c, s = cos[:, at], sin[:, at]
        for h in range(HEADS):
            group, lanes = h // GROUP, slice(h % GROUP * rows, (h % GROUP + 1) * rows)
            a = dq[q, group, :half, lanes] * HEAD_DIM**-0.5
            b = dq[q, group, half:, lanes] * HEAD_DIM**-0.5
            made[64 * h : 64 * h + half, at] = (a * c + b * s).astype(BF16)
            made[64 * h + half : 64 * h + 64, at] = (b * c - a * s).astype(BF16)
        for k in range(KV_HEADS):
            both = own[q, k] + twin[q][k].astype(F32)
            if chain:
                both = both + came[q, k].astype(F32)
            both = both.T
            a, b = both[:half], both[half : 2 * half]
            row = width + 64 * k
            made[row : row + half, at] = (a * c + b * s).astype(BF16)
            made[row + half : row + 64, at] = (b * c - a * s).astype(BF16)
            made[row + 192 : row + 256, at] = both[2 * half :].astype(BF16)
    for copy in copies:
        copy.wait()
    gain = gains[:, 64:65].astype(F32)
    d_first = jnp.dot(full[:, : width + 384], made[...], preferred_element_type=F32)
    v = jnp.concatenate([xa[:width], xb[:width]], axis=1).astype(F32)
    d_v, first = norm_back(v, gain, d_first)
    d_x = (d_middle[...] + d_v).astype(BF16)
    grad_a[...] = d_x[:, :rows]
    grad_b[...] = d_x[:, rows:]
    front = dot(normed_t[...], made[...], 1, 1)
    lane = lax.broadcasted_iota(jnp.int32, (width, 64), 1)
    ends = jnp.where(lane == 0, first, second[:, :64])
    put_slabs(packed, sc, fsdp, 0, jnp.concatenate([front, ends], axis=1))
    used = (width + 448) // 128 * (width // fsdp)
    total = packed.shape[2]
    if total > used:
        packed[:, :, used:] = jnp.zeros((2, fsdp // 2, total - used, 128), BF16)
    mine[...] = packed[0]
    give[...] = packed[1]


def last(fsdp, ctx, sc, xs, cos, sin, normed_t, gains, second, d_middle, dq, dkv, parts):
    width, count = normed_t.shape
    rows = count // 2
    used = (width + 448) // 128 * (width // fsdp)
    packed = (fsdp // 2, -(-used // (16 * ctx)) * 16 * ctx, 128)
    given = (*xs, cos, sin, normed_t, gains, second, d_middle, dq, *dkv)
    out_shape = (
        jax.ShapeDtypeStruct((width, rows), BF16),
        jax.ShapeDtypeStruct((width, rows), BF16),
        jax.ShapeDtypeStruct(packed, BF16),
        jax.ShapeDtypeStruct(packed, BF16),
    )
    return pl.pallas_call(
        functools.partial(last_kernel, fsdp, len(parts), len(dkv) == 4),
        out_shape=out_shape,
        grid=(1,),
        in_specs=[SM] + wholes(*given) + [HB] * len(parts),
        out_specs=wholes(*out_shape),
        scratch_shapes=[
            pltpu.VMEM((width, parts[0].shape[1]), BF16),
            pltpu.VMEM((2,) + packed, BF16),
            pltpu.VMEM((width + 384, count), BF16),
            pltpu.SemaphoreType.DMA((len(parts),)),
        ],
        compiler_params=LIMIT,
        cost_estimate=takes(7),
    )(sc, *given, *parts)


def unpack_kernel(places, flat, *outs):
    for out, (at, rows, skip) in zip(outs, places, strict=True):
        columns = out.shape[1]
        done = 0
        while done < columns:
            slab, lane = divmod(skip + done, 128)
            n = min(128 - lane, columns - done)
            out[:, done : done + n] = flat[
                at + slab * rows : at + (slab + 1) * rows, lane : lane + n
            ].astype(F32)
            done += n


def front_unpack_kernel(places, flat, *outs):
    *outs, first, second = outs
    unpack_kernel(places, flat, *outs)
    rows = first.shape[1]
    ends = flat[7 * rows : 8 * rows].astype(F32).T
    first[...] = ends[64:65]
    second[...] = ends[65:66]


def front_unpack(flat, shard, widths):
    places = [(0, shard, sum(widths[:i])) for i in range(len(widths))]
    out_shape = tuple(jax.ShapeDtypeStruct((shard, n), F32) for n in widths)
    out_shape += (jax.ShapeDtypeStruct((1, shard), F32),) * 2
    return pl.pallas_call(
        functools.partial(front_unpack_kernel, places),
        out_shape=out_shape,
        grid=(1,),
        in_specs=wholes(flat),
        out_specs=wholes(*out_shape),
        compiler_params=LIMIT,
        cost_estimate=takes(2),
    )(flat)


def join_unpack_kernel(places, parts, sc, *refs):
    pieces, outs, flat = refs[: 2 * parts], refs[2 * parts : -1], refs[-1]
    n = pieces[0].shape[0]
    half = parts // 2
    for i, piece in enumerate(pieces):
        x = lax.rem(sc[0] + i // parts, 2)
        p = lax.rem(sc[1] + parts - i % parts, parts)
        at = lax.div(p, half) * (parts * n) + x * (half * n) + lax.rem(p, half) * n
        flat[pl.ds(pl.multiple_of(at, 16), n)] = piece[...]
    unpack_kernel(places, flat, *outs)


def unpack(flat, places):
    out_shape = tuple(jax.ShapeDtypeStruct((p[1], p[3]), F32) for p in places)
    return pl.pallas_call(
        functools.partial(unpack_kernel, [p[:3] for p in places]),
        out_shape=out_shape,
        grid=(1,),
        in_specs=wholes(flat),
        out_specs=wholes(*out_shape),
        compiler_params=LIMIT,
        cost_estimate=takes(2),
    )(flat)


def join_unpack(place, near, far, places):
    pieces = (*near, *far)
    out_shape = tuple(jax.ShapeDtypeStruct((p[1], p[3]), F32) for p in places)
    return pl.pallas_call(
        functools.partial(join_unpack_kernel, [p[:3] for p in places], len(near)),
        out_shape=out_shape,
        grid=(1,),
        in_specs=[SM] + wholes(*pieces),
        out_specs=wholes(*out_shape),
        scratch_shapes=[pltpu.VMEM((len(pieces) * near[0].shape[0], 128), BF16)],
        compiler_params=LIMIT,
        cost_estimate=takes(3),
    )(place, *pieces)


def chip_kernel(mine, got, *refs):
    *came, out = refs
    total = mine[0].astype(F32) + got[0].astype(F32)
    for c in came:
        total = total + c[...].astype(F32)
    out[...] = total.astype(BF16)


def chip_sum(mine, got, i, *came):
    out = jax.ShapeDtypeStruct(mine.shape[1:], BF16)
    one = pl.BlockSpec((1,) + mine.shape[1:], lambda n: (i, 0, 0))
    return pl.pallas_call(
        chip_kernel,
        out_shape=out,
        grid=(1,),
        in_specs=[one, one] + wholes(*came),
        out_specs=whole(out),
        compiler_params=LIMIT,
        cost_estimate=takes(0),
    )(mine, got, *came)


def sum_y(mine, got, send):
    came = [send["shift"][s](chip_sum(mine, got, s)) for s in range(1, mine.shape[0])]
    return chip_sum(mine, got, 0, *came)


def spread_kernel(got, out):
    total = got[0].astype(F32)
    for i in range(1, got.shape[0]):
        total = total + got[i].astype(F32)
    total = total.astype(BF16)
    for i in range(got.shape[0]):
        out[i] = total


def sum_kernel(got, out):
    total = got[0].astype(F32)
    for i in range(1, got.shape[0]):
        total = total + got[i].astype(F32)
    out[...] = total.astype(BF16)


def simple_call(kernel, out_shape, *given):
    return pl.pallas_call(
        kernel,
        out_shape=out_shape,
        grid=(1,),
        in_specs=wholes(*given),
        out_specs=whole(out_shape),
        compiler_params=LIMIT,
        cost_estimate=takes(0),
    )(*given)


def exchange(total, axes, size):
    parts = total.reshape(size, total.shape[0] // size, 128)
    return lax.all_to_all(parts, axes, 0, 0, tiled=True)


def spread(got):
    return simple_call(spread_kernel, jax.ShapeDtypeStruct(got.shape, BF16), got)


def gather_over(spread, axes):
    return lax.all_to_all(spread, axes, 0, 0, tiled=True).reshape(-1, 128)


def came_kernel(own, twin_a, twin_b, *refs):
    *came, out = refs
    for i, twin in enumerate((twin_a, twin_b)):
        total = own[i].astype(F32) + twin[...].astype(F32)
        for c in came:
            total = total + c[i].astype(F32)
        out[i] = total.astype(BF16)


def halves_kernel(one, one_came, two, two_came, out):
    n = one.shape[0]
    out[:n] = (one[...].astype(F32) + one_came[...].astype(F32)).astype(BF16)
    out[n:] = (two[...].astype(F32) + two_came[...].astype(F32)).astype(BF16)


def first_kernel(x, *refs):
    mine, got, (to_y, to_x) = refs[:4], refs[4:8], refs[8:]
    for i in range(4):
        out = to_y if i < 2 else to_x
        out[i % 2] = (mine[i][0].astype(F32) + got[i][0].astype(F32)).astype(BF16)


def first_sums(x, mine, got):
    n = mine.shape[1] // 4
    block = (1, n, 128)
    places = [
        lambda i, x: (1, 0, 0),
        lambda i, x: (1, 1, 0),
        lambda i, x: (0, 3 - x[0], 0),
        lambda i, x: (1, 3 - x[0], 0),
    ]
    out = pl.BlockSpec((2, n, 128), lambda i, x: (0, 0, 0))
    return pl.pallas_call(
        first_kernel,
        out_shape=(jax.ShapeDtypeStruct((2, n, 128), BF16),) * 2,
        grid_spec=pltpu.PrefetchScalarGridSpec(
            num_scalar_prefetch=1,
            grid=(1,),
            in_specs=[pl.BlockSpec(block, at) for at in places] * 2,
            out_specs=[out, out],
        ),
        compiler_params=LIMIT,
        cost_estimate=takes(0),
    )(x, *[mine] * 4, *[got] * 4)


def second_kernel(x, *refs):
    mine, got, came, outs = refs[:4], refs[4:8], refs[8:12], refs[12:]
    for i in range(4):
        total = mine[i][0].astype(F32) + got[i][0].astype(F32) + came[i][0].astype(F32)
        outs[i][...] = total.astype(BF16)


def second_sums(x, mine, got, came_y, came_x):
    n = mine.shape[1] // 4
    block = (1, n, 128)
    own = [
        lambda i, x: (0, 1 - x[0], 0),
        lambda i, x: (0, x[0], 0),
        lambda i, x: (1, 2 + x[0], 0),
        lambda i, x: (0, 2 + x[0], 0),
    ]
    came = [
        lambda i, x: (1 - x[0], 0, 0),
        lambda i, x: (x[0], 0, 0),
        lambda i, x: (1, 0, 0),
        lambda i, x: (0, 0, 0),
    ]
    return pl.pallas_call(
        second_kernel,
        out_shape=(jax.ShapeDtypeStruct((n, 128), BF16),) * 4,
        grid_spec=pltpu.PrefetchScalarGridSpec(
            num_scalar_prefetch=1,
            grid=(1,),
            in_specs=[pl.BlockSpec(block, at) for at in own + own + came],
            out_specs=[pl.BlockSpec((n, 128), lambda i, x: (0, 0))] * 4,
        ),
        compiler_params=LIMIT,
        cost_estimate=takes(0),
    )(x, *[mine] * 4, *[got] * 4, came_y, came_y, came_x, came_x)


def gather_y(own, send, fsdp):
    return [own] + [send["shift"][s](own) for s in range(1, fsdp // 2)]


def gather_pieces(got, send, fsdp, core, y, join, dim):
    pieces = got + [send["core"](g) for g in got]
    own = got[0]
    if not join:
        return pieces
    buffer = jnp.zeros((fsdp,) + own.shape, own.dtype)
    for piece, f in zip(pieces, piece_order(fsdp, core, y), strict=True):
        buffer = lax.dynamic_update_index_in_dim(buffer, piece, f, 0)
    if dim:
        buffer = buffer.swapaxes(0, 1)
        return [buffer.reshape(own.shape[0], fsdp * own.shape[1])]
    return [buffer.reshape(fsdp * own.shape[0], own.shape[1])]


def piece_order(fsdp, core, y):
    ys = fsdp // 2
    source = [lax.rem(y - s + ys, ys) * 2 for s in range(ys)]
    return [f + core for f in source] + [f + 1 - core for f in source]


def body(
    fsdp,
    ctx,
    tokens,
    segment_ids,
    positions,
    cotangent,
    norm_first,
    query_weight,
    key_weight,
    value_weight,
    output_weight,
    norm_second,
    gate_weight,
    up_weight,
    down_weight,
):
    send = make_send(fsdp, ctx)
    ys, hs = fsdp // 2, ctx // 2
    _, count, width = tokens.shape
    rows = count // 2
    kv_width = KV_HEADS * HEAD_DIM
    y, core = lax.axis_index("y"), lax.axis_index("core")
    h, x = lax.axis_index("h"), lax.axis_index("x")
    ci = 2 * h + x
    reach = min(hs - 1, -(-(-(-(DOC_MOST - 1) // rows)) // 4))
    order = jnp.stack([core, y, 4 * h] + piece_order(fsdp, core, y)).astype(jnp.int32)
    shard = gate_weight.shape[0]
    join = shard % 16 != 0
    row = lax.broadcasted_iota(jnp.int32, (8, shard), 0)
    gain_rows = jnp.where(row == 0, norm_first.astype(F32), norm_second.astype(F32))
    gain_rows = jnp.where(row < 2, gain_rows, 0.0)
    *pair, packed = prepare(
        2 * count * h + count * x,
        h,
        tokens.reshape(count, width).T,
        positions,
        query_weight,
        key_weight,
        value_weight,
        gain_rows,
    )
    xs = send_home(send, pair)
    first_parts = gather_y(packed, send, fsdp)
    first_parts = gather_pieces(first_parts, send, fsdp, core, y, join, 0)
    cot_t, _ = tie(cotangent.reshape(count, width).T, first_parts[-1])
    cots = send_home(send, pick_home(cot_t, h))
    pos_f = jnp.concatenate([a[width : width + 2] for a in xs], axis=1).astype(F32)
    pos_f = pos_f[0:1] * 64.0 + pos_f[1:2]
    frequency = jnp.exp(
        jnp.arange(HEAD_DIM // 2, dtype=F32) * (-math.log(10000.0) * 2.0 / HEAD_DIM)
    )
    angle = frequency[:, None] * pos_f
    cos, sin = jnp.cos(angle), jnp.sin(angle)
    feed_own = jnp.concatenate([gate_weight, up_weight, output_weight], axis=1)
    feed_own, down_own, _ = tie(feed_own, down_weight.T, first_parts[-1])
    feed_got = gather_y(feed_own, send, fsdp)
    down_got = gather_y(down_own, send, fsdp)
    feed_got[0], *xs = tie(feed_got[0], *xs)
    qz, kv, normed_t, gains, pos, ids = project(order, xs, cos, sin, first_parts)

    stages = []
    carried = None
    for s in range(reach + 1):
        stages.append((kv, send["core"](kv)))
        if s < reach:
            kv = send["up"](kv)
        carried = attend_forward(s, ids, pos, qz, stages[s], carried, s == reach)
        if s < reach:
            kv, *carried = tie(kv, *carried)
    mixed, lse = carried
    feed_parts = gather_pieces(feed_got, send, fsdp, core, y, join, 0)
    down_parts = gather_pieces(down_got, send, fsdp, core, y, join, 1)
    res_a, res_b, d_middle, gz, delta, mine, give, second = feed(
        fsdp, ctx, order, xs, cots, mixed, gains, feed_parts, down_parts
    )

    got = send["core"](give)
    crossed = ys == 2
    x_ref = x.astype(jnp.int32).reshape(1)
    dq = None
    came = None
    for s in range(reach, -1, -1):
        sc = ids
        if s == reach - 1 and crossed:
            first_y, first_x = first_sums(x_ref, mine, got)
            sc, first_y, first_x = tie(sc, first_y, first_x)
            came_y, came_x = send["shift"][1](first_y), send["across"](first_x)
        if s == 0 and crossed:
            came_y, came_x, dq = tie(came_y, came_x, dq)
            give_one, keep_one, give_two, keep_two = second_sums(x_ref, mine, got, came_y, came_x)
            sc, give_one, give_two = tie(sc, give_one, give_two)
            came_one, came_two = send["across"](give_one), send["shift"][1](give_two)
        if came is not None:
            sc, came = tie(sc, came)
            came = send["down"](came)
        dq, own, *other = attend_backward(
            s, sc, pos, qz, gz, lse, delta, stages[s], dq, F32 if s == 0 else BF16
        )
        twin = tuple(send["core"](o) for o in other)
        if s > 0:
            if s == reach - 1:
                *twin, came, dq, res_a, res_b = tie(*twin, came, dq, *result)
            elif s < reach:
                *twin, came, dq = tie(*twin, came, dq)
            given = (own, *twin) if came is None else (own, *twin, came)
            came = simple_call(came_kernel, jax.ShapeDtypeStruct(own.shape, BF16), *given)
            if s == reach:
                came, res_a, res_b = tie(came, res_a, res_b)
                result = send_back(send, res_a, res_b)
    dkv = (own, *twin) if came is None else (own, *twin, came)
    if crossed:
        late = simple_call(
            halves_kernel,
            jax.ShapeDtypeStruct((mine.shape[1] // 2, 128), BF16),
            keep_one,
            came_one,
            keep_two,
            came_two,
        )
        late, dq = tie(late, dq)
        late = exchange(late, ("h",), hs)
    else:
        late = exchange(sum_y(mine, got, send), CTX, ctx)
    tok_a, tok_b, mine_front, give_front = last(
        fsdp, ctx, order, xs, cos, sin, normed_t, gains, second, d_middle, dq, dkv, first_parts
    )
    got_front = send["core"](give_front)
    late, got_front = tie(late, got_front)
    front = sum_y(mine_front, got_front, send)
    if crossed:
        piece = simple_call(sum_kernel, jax.ShapeDtypeStruct(late.shape[1:], BF16), late)
        near = [piece] + [send["around"][s](piece) for s in range(1, hs)]
        far = [send["across"](p) for p in near]
        *near, tok_a, tok_b = tie(*near, tok_a, tok_b)
    else:
        late = gather_over(spread(late), CTX)
    front = spread(exchange(front, CTX, ctx))
    front = gather_over(front, CTX)
    tokens_grad = send_back(send, tok_a, tok_b)

    ff = gate_weight.shape[1]
    down_shard = down_weight.shape[0]
    gate_rows, out_rows = ff // 128 * shard, -(-width // 128) * shard
    places = [
        (0, shard, 0, ff),
        (gate_rows, shard, 0, ff),
        (2 * gate_rows, shard, 0, width),
        (2 * gate_rows + out_rows, width, 0, down_shard),
    ]
    if crossed:
        late_grads = join_unpack(jnp.stack([x, h]).astype(jnp.int32), near, far, places)
    else:
        late_grads = unpack(late, places)
    gate_grad, up_grad, output_grad, down_grad = late_grads
    query_grad, key_grad, value_grad, first_grad, second_grad = front_unpack(
        front, shard, (width, kv_width, kv_width)
    )
    return (
        low_high(res_a, res_b, h).T[None],
        low_high(*tokens_grad, h).T[None],
        first_grad[0],
        query_grad,
        key_grad,
        value_grad,
        output_grad,
        second_grad[0],
        gate_grad,
        up_grad,
        down_grad.T,
    )


def solution(mesh):
    fsdp, ctx = mesh.shape["fsdp"], mesh.shape["ctx"]
    places = Mesh(mesh.devices.reshape(fsdp // 2, 2, ctx // 2, 2), AXES)
    owner = ("y", "core")
    flat, split = P(owner), P(owner, None)
    whole = P(owner, CTX, None)
    return jax.shard_map(
        functools.partial(body, fsdp, ctx),
        mesh=places,
        in_specs=(whole, split, split, whole, flat, split, split, split, split, flat, split, split, split),
        out_specs=(whole, whole, flat, split, split, split, split, flat, split, split, split),
        check_vma=False,
    )
```
